256 devices in a mesh: strike: 16 (over z, y_hi), dip: 4 (over x), depth: 4 (over y_lo, core).
Axes of the slice: x: 4, y: 4 (y_hi: 2, y_lo: 2; y = y_hi * 2 + y_lo), z: 8, core: 2. Of those that a mesh axis runs over, the one named last changes fastest.
Arguments:
- velocity: float32 [3, 256, 128, 512], P(None, 'strike', 'dip', 'depth'), may hold values from -6 to 6
- stress: float32 [6, 256, 128, 512], P(None, 'strike', 'dip', 'depth'), may hold values from -6 to 6
- memory: float32 [6, 256, 128, 512], P(None, 'strike', 'dip', 'depth'), may hold values from -4 to 4
- lame_lambda: float32 [256, 128, 512], P('strike', 'dip', 'depth'), may hold values from 0.5 to 2
- shear_modulus: float32 [256, 128, 512], P('strike', 'dip', 'depth'), may hold values from 0.5 to 2
- buoyancy: float32 [256, 128, 512], P('strike', 'dip', 'depth'), may hold values from 0.5 to 2
- relax: float32 [256, 128, 512], P('strike', 'dip', 'depth'), may hold values from 0.2 to 0.95
- anelastic: float32 [256, 128, 512], P('strike', 'dip', 'depth'), may hold values from 0.1 to 1
- moment_rate: float32 [16, 32, 6, 2048], P('strike'), may hold values from -6 to 6
- subfault_cell: int32 [16, 2048], replicated, may hold values from 0 to 131071, as said below
- active_segment: int32 [2], replicated, may hold values from 0 to 15
- stf_offset: int32 [2], replicated, may hold values from 0 to 24
Outputs:
- velocity_out: float32 [3, 256, 128, 512], P(None, 'strike', 'dip', 'depth')
- stress_out: float32 [6, 256, 128, 512], P(None, 'strike', 'dip', 'depth')
- memory_out: float32 [6, 256, 128, 512], P(None, 'strike', 'dip', 'depth')
The draws below stay inside these ranges and needn't reach their ends.
Inputs may be any that keep to these rules, and one draw needn't show every extreme that they name: subfault_cell[s, j] = x * 512 + z names strike cell x and depth cell z of subfault j of segment s; the subfaults of every segment lie along the whole strike extent, every block of 16 strike cells holding some of them; several subfaults may share a cell.
All inputs are finite; a program needn't handle non-finite values.
Results may differ from the reference program's by a relative error of at most 0.0003.
Values sent between devices are 32-bit elements; how exact they have to be, the bound alone decides.
A program may use at most 64 MiB of HBM per device.

```python
import math
from functools import partial
import jax
import jax.numpy as jnp
from jax import lax

CX = 16
CY = 32
SUBF = 2048
STF_LEN = 32
TB = 8
STEPS = 2
SEGMENTS = 16
NX = 256
NY = 128
NZ = 512
N_DIP = 4


def draw_subfault_cell(key, part):
    key = jax.random.fold_in(key, 5)
    strike_key = jax.random.fold_in(key, 11)
    depth_key = jax.random.fold_in(key, 12)
    order_key = jax.random.fold_in(key, 13)
    within = jax.random.randint(strike_key, (SEGMENTS, SUBF), 0, CX)
    depth_cell = jax.random.randint(depth_key, (SEGMENTS, SUBF), 0, NZ)
    order = jax.vmap(lambda single: jax.random.permutation(single, SUBF))(jax.random.split(order_key, SEGMENTS)).astype(jnp.int32)
    strike_block = order % SEGMENTS
    segment_ids = jnp.arange(SEGMENTS, dtype=jnp.int32)[:, None]
    first_pick = (segment_ids == 0) & (order == 0)
    last_pick = (segment_ids == SEGMENTS - 1) & (order == SEGMENTS - 1)
    within = jnp.where(first_pick, 0, jnp.where(last_pick, CX - 1, within))
    depth_cell = jnp.where(first_pick, 0, jnp.where(last_pick, NZ - 1, depth_cell))
    strike_cell = strike_block * CX + within
    cells = strike_cell * NZ + depth_cell
    return cells.astype(jnp.int32)


def level_of(own_key, dims, cuts, least, high):
    level = 1.0
    for axis_at, shards_of in cuts:
        draws = jax.random.uniform(jax.random.fold_in(jax.random.fold_in(own_key, 6), axis_at), (shards_of,), jnp.float32, least / len(cuts), high / len(cuts))
        level = level * jnp.repeat(jnp.exp(draws), dims[axis_at] // shards_of).reshape((-1,) + (1,) * (len(dims) - 1 - axis_at))
    return level


def scatter_about(key, dims, deviation, reach, cuts=(), kind=jnp.bfloat16):
    array = jax.random.normal(key, dims, jnp.float32) * deviation
    if len(cuts) > 0:
        array = level_of(key, dims, cuts, -0.22, 0.18) * array
    return jnp.clip(array, min=-reach, max=reach).astype(kind)


def setup_inputs(seed: int = 0) -> dict:
    arg_keys = jax.random.split(jax.random.key(seed), 13)
    return {
        "velocity": scatter_about(arg_keys[0], (3, NX, NY, NZ), 1.0, 6.0, ((1, 16), (2, 4), (3, 4)), jnp.float32),
        "stress": scatter_about(arg_keys[1], (6, NX, NY, NZ), 1.0, 6.0, ((1, 16), (2, 4), (3, 4)), jnp.float32),
        "memory": scatter_about(arg_keys[2], (6, NX, NY, NZ), 0.5, 4.0, ((1, 16), (2, 4), (3, 4)), jnp.float32),
        "lame_lambda": jnp.clip(jnp.exp(math.log(2.0) - 1.3862944 * jax.random.uniform(arg_keys[3], (NX, NY, NZ), jnp.float32) ** level_of(arg_keys[3], (NX, NY, NZ), ((0, 16), (1, 4), (2, 4)), -0.2, 0.2)), 0.5, 2.0),
        "shear_modulus": jnp.clip(jnp.exp(math.log(2.0) - 1.3862944 * jax.random.uniform(arg_keys[4], (NX, NY, NZ), jnp.float32) ** level_of(arg_keys[4], (NX, NY, NZ), ((0, 16), (1, 4), (2, 4)), -0.2, 0.2)), 0.5, 2.0),
        "buoyancy": jnp.clip(jnp.exp(math.log(2.0) - 1.3862944 * jax.random.uniform(arg_keys[5], (NX, NY, NZ), jnp.float32) ** level_of(arg_keys[5], (NX, NY, NZ), ((0, 16), (1, 4), (2, 4)), -0.2, 0.2)), 0.5, 2.0),
        "relax": jnp.clip(jnp.exp(math.log(0.95) - 1.5581446 * jax.random.uniform(arg_keys[6], (NX, NY, NZ), jnp.float32) ** level_of(arg_keys[6], (NX, NY, NZ), ((0, 16), (1, 4), (2, 4)), -0.2, 0.2)), 0.2, 0.95),
        "anelastic": jnp.clip(jnp.exp(math.log(1.0) - 2.3025851 * jax.random.uniform(arg_keys[7], (NX, NY, NZ), jnp.float32) ** level_of(arg_keys[7], (NX, NY, NZ), ((0, 16), (1, 4), (2, 4)), -0.2, 0.2)), 0.1, 1.0),
        "moment_rate": scatter_about(arg_keys[8], (SEGMENTS, STF_LEN, 6, SUBF), 1.0, 6.0, ((0, 16),), jnp.float32),
        "subfault_cell": draw_subfault_cell(jax.random.fold_in(arg_keys[12], 71), 0),
        "active_segment": jax.random.randint(arg_keys[10], (STEPS,), 0, SEGMENTS).astype(jnp.int32),
        "stf_offset": jax.random.randint(arg_keys[11], (STEPS,), 0, STF_LEN - TB + 1).astype(jnp.int32),
    }


COEF_NEAR = 9.0 / 8.0
COEF_FAR = -1.0 / 24.0
STEP_RATIO = 0.12


def forward_diff(padded, axis):
    length = padded.shape[axis] - 4
    near_term = lax.slice_in_dim(padded, 3, length + 3, axis=axis) - lax.slice_in_dim(padded, 2, length + 2, axis=axis)
    far_term = lax.slice_in_dim(padded, 4, length + 4, axis=axis) - lax.slice_in_dim(padded, 1, length + 1, axis=axis)
    return COEF_NEAR * near_term + COEF_FAR * far_term


def backward_diff(padded, axis):
    length = padded.shape[axis] - 4
    near_term = lax.slice_in_dim(padded, 2, length + 2, axis=axis) - lax.slice_in_dim(padded, 1, length + 1, axis=axis)
    far_term = lax.slice_in_dim(padded, 3, length + 3, axis=axis) - lax.slice_in_dim(padded, 0, length, axis=axis)
    return COEF_NEAR * near_term + COEF_FAR * far_term


def velocity_update(velocity, along, buoyancy):
    gain = STEP_RATIO * buoyancy
    first = forward_diff(along(0, 0), 0) + backward_diff(along(3, 1), 1) + backward_diff(along(4, 2), 2)
    second = backward_diff(along(3, 0), 0) + forward_diff(along(1, 1), 1) + backward_diff(along(5, 2), 2)
    third = backward_diff(along(4, 0), 0) + backward_diff(along(5, 1), 1) + forward_diff(along(2, 2), 2)
    return jnp.stack([velocity[0] + gain * first, velocity[1] + gain * second, velocity[2] + gain * third])


def stress_update(stress, memory, along, lame_lambda, shear_modulus, relax, anelastic):
    strain_xx = backward_diff(along(0, 0), 0)
    strain_yy = backward_diff(along(1, 1), 1)
    strain_zz = backward_diff(along(2, 2), 2)
    volume = strain_xx + strain_yy + strain_zz
    normal_part = STEP_RATIO * lame_lambda * volume
    twice_shear = 2.0 * STEP_RATIO * shear_modulus
    shear_rate = STEP_RATIO * shear_modulus
    elastic = [normal_part + twice_shear * strain_xx,
               normal_part + twice_shear * strain_yy,
               normal_part + twice_shear * strain_zz,
               shear_rate * (forward_diff(along(0, 1), 1) + forward_diff(along(1, 0), 0)),
               shear_rate * (forward_diff(along(0, 2), 2) + forward_diff(along(2, 0), 0)),
               shear_rate * (forward_diff(along(1, 2), 2) + forward_diff(along(2, 1), 1))]
    new_stress = []
    new_memory = []
    for comp in range(6):
        updated = relax * memory[comp] + (1.0 - relax) * anelastic * elastic[comp]
        new_stress.append(stress[comp] + elastic[comp] - 0.5 * (memory[comp] + updated))
        new_memory.append(updated)
    return jnp.stack(new_stress), jnp.stack(new_memory)


def sample_weights():
    samples = jnp.arange(TB)
    ends = (samples == 0) | (samples == TB - 1)
    return jnp.where(ends, 0.5, 1.0).astype(jnp.float32) / jnp.float32(TB - 1)


def pad_component(fields, comp, axis):
    widths = [(2, 2) if dim == axis else (0, 0) for dim in range(3)]
    return jnp.pad(fields[comp], widths)


def reference(velocity, stress, memory, lame_lambda, shear_modulus, buoyancy, relax, anelastic, moment_rate, subfault_cell, active_segment, stf_offset):
    fault_row = (N_DIP // 2) * CY
    weights = sample_weights()
    for step_index in range(STEPS):
        velocity = velocity_update(velocity, partial(pad_component, stress), buoyancy)
        stress, memory = stress_update(stress, memory, partial(pad_component, velocity), lame_lambda, shear_modulus, relax, anelastic)
        segment = active_segment[step_index].astype(jnp.int32)
        offset = stf_offset[step_index].astype(jnp.int32)
        block = lax.dynamic_slice_in_dim(moment_rate[segment], offset, TB, 0)
        moment = jnp.sum(weights[:, None, None] * block, axis=0)
        cells = subfault_cell[segment]
        plane = jnp.zeros((6, NX * NZ), jnp.float32).at[:, cells].add(moment)
        stress = stress.at[:, :, fault_row, :].add(-plane.reshape(6, NX, NZ))
    return velocity, stress, memory
```

```python
import functools

import jax
import jax.numpy as jnp
from jax import lax
from jax.experimental import pallas as pl
from jax.experimental.pallas import tpu as pltpu
from jax.sharding import PartitionSpec as P

MESH = pl.DeviceIdType.MESH
TB = 8
STEPS = 2
R24 = 0.12 / 24.0
XP = 2
YP = 8
NA = 2

X_GROUPS = {"s": ((0, 1, 1, 2), (3, 2, 2, 1)), "v": ((0, 1, 2, 1), (1, 2, 1, 2))}
Y_FIELDS = {"s": ((3, True), (5, True), (1, False)), "v": ((1, True), (0, False), (2, False))}
Z_FIELDS = {"s": (4, 5, 2), "v": (0, 1, 2)}
Z_BACK = {"s": (True, True, False), "v": (False, False, True)}


def stress_tiles(x, m, sizes, Sf, Vf, M, deep, material, put):
    CY, ROW = sizes
    for j in range(0, CY, 8):
        at = (x + XP) * ROW + YP + j
        rows = pl.ds(j, 8)

        def get(c, n, at=at):
            return Vf[c, pl.ds(at + n, 8), :]

        vx = [get(0, n * ROW) for n in range(-2, 3)]
        vy = [get(1, n * ROW) for n in range(-1, 4)]
        vz = [get(2, n * ROW) for n in range(-1, 4)]
        for p in range(2):
            o = p * ROW
            lam, mu, relax, ane = material(m + p, rows)
            shear = R24 * mu
            twice = 2.0 * shear
            part = (1.0 - relax) * ane
            vx_at, vy_at, vz_at = vx[2 + p], vy[1 + p], vz[1 + p]
            xx = 27.0 * (vx_at - vx[1 + p]) - (vx[3 + p] - vx[p])
            yy = 27.0 * (vy_at - get(1, o - 1)) - (get(1, o + 1) - get(1, o - 2))
            zz = deep[2, x + p, rows, :]
            normal = R24 * lam * (xx + yy + zz)
            xy = 27.0 * ((get(0, o + 1) - vx_at) + (vy[2 + p] - vy_at)) - (
                (get(0, o + 2) - get(0, o - 1)) + (vy[3 + p] - vy[p]))
            xz = 27.0 * (vz[2 + p] - vz_at) - (vz[3 + p] - vz[p]) + deep[0, x + p, rows, :]
            yz = 27.0 * (get(2, o + 1) - vz_at) - (get(2, o + 2) - get(2, o - 1)) + deep[1, x + p, rows, :]
            grown = (
                normal + twice * xx, normal + twice * yy, normal + twice * zz,
                shear * xy, shear * xz, shear * yz,
            )
            for c in range(6):
                old = M[c, x + p, rows, :]
                new = relax * old + part * grown[c]
                stress = Sf[c, pl.ds(pl.multiple_of(at + o, 8), 8), :] + grown[c] - 0.5 * (old + new)
                put(c, x + p, at + o, rows, stress, new)


def finish(dims, S, V, M, deep, edge, plane, vel_out, str_out, mem_out, stress, memory, sem):
    CX, CY = dims
    ROW = CY + 2 * YP
    own = pl.ds(YP, CY)
    middle = pl.ds(2, CX - 4)
    copies = [
        pltpu.make_async_copy(V.at[:, pl.ds(XP, CX), own], vel_out, sem.at[0]),
        pltpu.make_async_copy(S.at[:, pl.ds(XP + 2, CX - 4), own], str_out.at[:, middle], sem.at[1]),
        pltpu.make_async_copy(M.at[:, middle], mem_out.at[:, middle], sem.at[2]),
    ]
    for copy in copies:
        copy.start()
    Sf = S.reshape(6, (CX + 2 * XP) * ROW, 128)
    Vf = V.reshape(3, (CX + 2 * XP) * ROW, 128)

    @pl.loop(0, 2)
    def _(i):
        x = i * (CX - 2)

        def material(m, rows):
            return tuple(edge[n, m, rows, :] for n in range(4))

        def put(c, at_x, at, rows, s, m):
            place = at_x - i * (CX - 4)
            stress[c, place, rows, :] = s
            memory[c, place, rows, :] = m

        stress_tiles(x, 2 * i, (CY, ROW), Sf, Vf, M, deep, material, put)

    for c in range(6):
        for n, x in enumerate((0, 1, CX - 2, CX - 1)):
            stress[c, n, 0:1, :] = stress[c, n, 0:1, :] - plane[c * CX + x:c * CX + x + 1, :]
    for n in range(2):
        here, there = pl.ds(2 * n, 2), pl.ds(n * (CX - 2), 2)
        copies.append(pltpu.make_async_copy(stress.at[:, here], str_out.at[:, there], sem.at[3 + 2 * n]))
        copies.append(pltpu.make_async_copy(memory.at[:, here], mem_out.at[:, there], sem.at[4 + 2 * n]))
    for copy in copies[3:]:
        copy.start()
    for copy in copies:
        copy.wait()


def kernel(
    dims,
    vel_hbm, str_hbm, mem_hbm, lam_hbm, mu_hbm, buo_hbm, rel_hbm, ane_hbm, rate_hbm, cell_hbm,
    active_hbm, offset_hbm,
    S, V, M, deep, edge, last_plane,
    lam, mu, buo, rel, ane, rate, cells, active, offset,
    ysend_up, ysend_dn, yrecv_up, yrecv_dn, zsend, zrecv_up, zrecv_dn, band,
    cand, pair, chosen, gathered, acc, plane,
    ld_sem, xs_sem, xr_sem, ys_sem, yr_sem, zs_sem, zr_sem,
    c_send, c_recv, p_send, p_recv, g_send, g_recv,
):
    NS, ND, NH, CX, CY, SUBF = dims
    ROW = CY + 2 * YP
    NB = NS // NA
    s = lax.axis_index("strike")
    k = lax.axis_index("dip")
    d = lax.axis_index("depth")
    fault = ND // 2
    on_fault = k == fault
    group, parity = lax.div(s, NA), lax.rem(s, NA)
    chunk = k * NH + d

    def near(axis, pos, size, step):
        return {axis: jnp.clip(pos + step, 0, size - 1)}

    s_up, s_dn = near("strike", s, NS, 1), near("strike", s, NS, -1)
    k_up, k_dn = near("dip", k, ND, 1), near("dip", k, ND, -1)
    d_up, d_dn = near("depth", d, NH, 1), near("depth", d, NH, -1)
    has = {
        "s_up": s < NS - 1, "s_dn": s > 0,
        "k_up": k < ND - 1, "k_dn": k > 0,
        "d_up": d < NH - 1, "d_dn": d > 0,
    }

    inner = (slice(None), pl.ds(XP, CX), pl.ds(YP, CY))
    loads = [
        pltpu.make_async_copy(str_hbm, S.at[inner], ld_sem.at[0]),
        pltpu.make_async_copy(
            rate_hbm.at[0, :, :, pl.ds(pl.multiple_of(chunk * 128, 128), 128)], rate, ld_sem.at[1]
        ),
        pltpu.make_async_copy(vel_hbm, V.at[inner], ld_sem.at[2]),
        pltpu.make_async_copy(buo_hbm, buo, ld_sem.at[3]),
        pltpu.make_async_copy(mem_hbm, M, ld_sem.at[4]),
        pltpu.make_async_copy(lam_hbm, lam, ld_sem.at[5]),
        pltpu.make_async_copy(mu_hbm, mu, ld_sem.at[6]),
        pltpu.make_async_copy(rel_hbm, rel, ld_sem.at[7]),
        pltpu.make_async_copy(ane_hbm, ane, ld_sem.at[8]),
        pltpu.make_async_copy(cell_hbm, cells, ld_sem.at[9]),
    ]
    for n, ref in enumerate((lam_hbm, mu_hbm, rel_hbm, ane_hbm)):
        for m in range(2):
            loads.append(pltpu.make_async_copy(
                ref.at[pl.ds(m * (CX - 2), 2)], edge.at[n, pl.ds(2 * m, 2)], ld_sem.at[10 + 2 * n + m]))
    order = (
        pltpu.make_async_copy(active_hbm, active, ld_sem.at[18]),
        pltpu.make_async_copy(offset_hbm, offset, ld_sem.at[19]),
    )
    for copy in (loads[0], *order, *loads[1:]):
        copy.start()

    barrier = pltpu.get_barrier_semaphore()
    count = jnp.int32(0)
    for name, to in (("s_up", s_up), ("s_dn", s_dn), ("k_up", k_up), ("k_dn", k_dn), ("d_up", d_up), ("d_dn", d_dn)):
        there = has[name]
        count = count + there.astype(jnp.int32)

        @pl.when(there)
        def _(to=to):
            pl.semaphore_signal(barrier, inc=1, device_id=to, device_id_type=MESH)

    other = {"strike": group * NA + lax.rem(parity + 1, NA)}
    pl.semaphore_signal(barrier, inc=1, device_id=other, device_id_type=MESH)
    count = count + 1

    @pl.loop(0, NB)
    def _(g):
        @pl.when(g != group)
        def _():
            pl.semaphore_signal(
                barrier, inc=1, device_id={"strike": g * NA + parity}, device_id_type=MESH
            )

    count = count + (NB - 1)

    @pl.loop(0, NH)
    def _(h):
        @pl.when(jnp.logical_not(on_fault & (h == d)))
        def _():
            pl.semaphore_signal(
                barrier, inc=1, device_id={"dip": fault, "depth": h}, device_id_type=MESH
            )

    count = count + NH - on_fault.astype(jnp.int32)

    @pl.when(on_fault)
    def _():
        @pl.loop(0, ND * NH)
        def _(j):
            @pl.when(j != chunk)
            def _():
                pl.semaphore_signal(
                    barrier, inc=1,
                    device_id={"dip": lax.div(j, NH), "depth": lax.rem(j, NH)},
                    device_id_type=MESH,
                )

    count = count + jnp.where(on_fault, ND * NH - 1, 0)
    pl.semaphore_wait(barrier, count)

    def x_copies(h):
        kind = "sv"[h % 2]
        ref = S if kind == "s" else V
        up, dn = [], []
        for n, (c0, nc, lu, ld) in enumerate(X_GROUPS[kind]):
            comps = pl.ds(c0, nc)
            rows = pl.ds(YP, CY)
            if h == 0:
                src_up = str_hbm.at[comps, pl.ds(CX - lu, lu)]
                src_dn = str_hbm.at[comps, pl.ds(0, ld)]
            else:
                src_up = ref.at[comps, pl.ds(XP + CX - lu, lu), rows]
                src_dn = ref.at[comps, pl.ds(XP, ld), rows]
            up.append(pltpu.make_async_remote_copy(
                src_up, ref.at[comps, pl.ds(XP - lu, lu), rows],
                xs_sem.at[h, n], xr_sem.at[h, n], device_id=s_up, device_id_type=MESH))
            dn.append(pltpu.make_async_remote_copy(
                src_dn, ref.at[comps, pl.ds(XP + CX, ld), rows],
                xs_sem.at[h, 2 + n], xr_sem.at[h, 2 + n], device_id=s_dn, device_id_type=MESH))
        return up, dn

    def each(there, copies, act):
        @pl.when(there)
        def _():
            for copy in copies:
                act(copy)

    def x_start(h):
        up, dn = x_copies(h)
        each(has["s_up"], up, lambda c: c.start())
        each(has["s_dn"], dn, lambda c: c.start())

    def x_wait_recv(h):
        up, dn = x_copies(h)
        each(has["s_dn"], up, lambda c: c.wait_recv())
        each(has["s_up"], dn, lambda c: c.wait_recv())

    def x_wait_send(h):
        up, dn = x_copies(h)
        each(has["s_up"], up, lambda c: c.wait_send())
        each(has["s_dn"], dn, lambda c: c.wait_send())

    x_start(0)

    Sf = S.reshape(6, (CX + 2 * XP) * ROW, 128)
    Vf = V.reshape(3, (CX + 2 * XP) * ROW, 128)
    flat = {"s": Sf, "v": Vf}

    for F, nc in ((S, 6), (V, 3)):
        zero_x = jnp.zeros((nc, XP, CY, 128), jnp.float32)

        @pl.when(s == 0)
        def _(F=F, zero_x=zero_x):
            F[:, 0:XP, YP:YP + CY, :] = zero_x

        @pl.when(s == NS - 1)
        def _(F=F, zero_x=zero_x):
            F[:, XP + CX:, YP:YP + CY, :] = zero_x

    zero_y = jnp.zeros(yrecv_up.shape, jnp.float32)
    zero_z = jnp.zeros(zrecv_up.shape, jnp.float32)
    for there, ref, zero in (
        (has["k_dn"], yrecv_up, zero_y), (has["k_up"], yrecv_dn, zero_y),
        (has["d_dn"], zrecv_up, zero_z), (has["d_up"], zrecv_dn, zero_z),
    ):
        @pl.when(jnp.logical_not(there))
        def _(ref=ref, zero=zero):
            ref[...] = zero

    def y_layers(kind):
        up, dn = [], []
        for c, back in Y_FIELDS[kind]:
            up += [(c, CY - 2), (c, CY - 1)] if back else [(c, CY - 1)]
            dn += [(c, 0)] if back else [(c, 0), (c, 1)]
        return up, dn

    def y_copies(h):
        up, dn = y_layers("sv"[h % 2])
        nu, nd = len(up), len(dn)
        return (
            pltpu.make_async_remote_copy(
                ysend_up.at[h, pl.ds(0, nu)], yrecv_up.at[h, pl.ds(0, nu)],
                ys_sem.at[h, 0], yr_sem.at[h, 0], device_id=k_up, device_id_type=MESH),
            pltpu.make_async_remote_copy(
                ysend_dn.at[h, pl.ds(0, nd)], yrecv_dn.at[h, pl.ds(0, nd)],
                ys_sem.at[h, 1], yr_sem.at[h, 1], device_id=k_dn, device_id_type=MESH),
        )

    def z_copies(h):
        return (
            pltpu.make_async_remote_copy(
                zsend.at[h], zrecv_up.at[h],
                zs_sem.at[h, 0], zr_sem.at[h, 0], device_id=d_up, device_id_type=MESH),
            pltpu.make_async_remote_copy(
                zsend.at[h], zrecv_dn.at[h],
                zs_sem.at[h, 1], zr_sem.at[h, 1], device_id=d_dn, device_id_type=MESH),
        )

    lane = lax.broadcasted_iota(jnp.int32, (CY, 128), 1)
    slot = lane >> 2
    quarter = lane & 3

    def turn(value, n):
        return pltpu.roll(value, n % 128, 1)

    def yz_send(h):
        kind = "sv"[h % 2]
        F = flat[kind]
        up, dn = y_layers(kind)
        base = XP * ROW + YP
        for n, (c, row) in enumerate(up):
            ysend_up[h, n] = F[c, pl.ds(base + row, CX, stride=ROW), :]
        for n, (c, row) in enumerate(dn):
            ysend_dn[h, n] = F[c, pl.ds(base + row, CX, stride=ROW), :]
        up, dn = y_copies(h)
        each(has["k_up"], [up], lambda c: c.start())
        each(has["k_dn"], [dn], lambda c: c.start())

        first = second = jnp.zeros((CY, 128), jnp.float32)
        for x in range(CX):
            a, b, c = (F[comp, pl.ds((x + XP) * ROW + YP, CY), :] for comp in Z_FIELDS[kind])
            first = jnp.where(slot == x, turn(a, 4 * x + 2), first)
            first = jnp.where(slot == x + CX, turn(b, 4 * x + 66), first)
            second = jnp.where(slot == x, turn(c, 4 * x + 2), second)
        zsend[h, 0] = first
        zsend[h, 1] = second
        up, dn = z_copies(h)
        each(has["d_up"], [up], lambda c: c.start())
        each(has["d_dn"], [dn], lambda c: c.start())

    def yz_recv(h):
        kind = "sv"[h % 2]
        F = flat[kind]
        up, dn = y_copies(h)
        each(has["k_dn"], [up], lambda c: c.wait_recv())
        each(has["k_up"], [dn], lambda c: c.wait_recv())
        up, dn = y_layers(kind)
        base = XP * ROW + YP
        for n, (c, row) in enumerate(up):
            F[c, pl.ds(base + row - CY, CX, stride=ROW), :] = yrecv_up[h, n]
        for n, (c, row) in enumerate(dn):
            F[c, pl.ds(base + row + CY, CX, stride=ROW), :] = yrecv_dn[h, n]
        up, dn = z_copies(h)
        each(has["d_dn"], [up], lambda c: c.wait_recv())
        each(has["d_up"], [dn], lambda c: c.wait_recv())
        fixes = []
        for n in range(2):
            mix = jnp.where(quarter < 2, zrecv_up[h, n], zrecv_dn[h, n])
            below, two_after = turn(mix, 1), turn(mix, -2)
            if Z_BACK[kind][2 * n]:
                fix = jnp.where(quarter == 0, -two_after, jnp.where(quarter == 1, below - 27.0 * mix, below))
            else:
                fix = jnp.where(quarter == 1, 27.0 * turn(mix, -1) - two_after, jnp.where(quarter == 0, -two_after, below))
            fixes.append(jnp.where(quarter == 3, 0.0, fix))
        for place, back in enumerate(Z_BACK[kind]):
            ends = (lane == 127) | (lane < 2) if back else (lane > 125) | (lane == 0)
            for x in range(CX):
                moved = turn(fixes[place // 2], (127 if back else 126) - 4 * x - 64 * (place % 2))
                deep[place, x] = deep[place, x] + jnp.where(ends, moved, 0.0)

    def deep_all(h):
        kind = "sv"[h % 2]
        F = S if kind == "s" else V
        for place, (comp, back) in enumerate(zip(Z_FIELDS[kind], Z_BACK[kind])):
            f = F[comp, XP:XP + CX, YP:YP + CY, :].reshape(CX * CY, 128)
            high = f.astype(jnp.bfloat16)
            low = (f - high.astype(jnp.float32)).astype(jnp.bfloat16)
            out = lax.dot_general(
                jnp.concatenate([high, low], axis=1), band[1 if back else 0],
                (((1,), (0,)), ((), ())), preferred_element_type=jnp.float32)
            deep[place] = out.reshape(CX, CY, 128)

    def velocity_pair(x):
        for j in range(0, CY, 8):
            at = (x + XP) * ROW + YP + j

            def get(c, n, Sf=Sf, at=at):
                return Sf[c, pl.ds(at + n, 8), :]

            xx = [get(0, n * ROW) for n in range(-1, 4)]
            xy = [get(3, n * ROW) for n in range(-2, 3)]
            xz = [get(4, n * ROW) for n in range(-2, 3)]
            for p in range(2):
                o = p * ROW
                gain = R24 * buo[x + p, pl.ds(j, 8), :]
                xy_at, yy, yz = xy[2 + p], [get(1, o + n) for n in range(-1, 3)], [get(5, o + n) for n in range(-2, 2)]
                close = (
                    (xx[2 + p] - xx[1 + p]) + (xy_at - get(3, o - 1)),
                    (xy_at - xy[1 + p]) + (yy[2] - yy[1]),
                    (xz[2 + p] - xz[1 + p]) + (yz[2] - yz[1]),
                )
                far = (
                    (xx[3 + p] - xx[p]) + (get(3, o + 1) - get(3, o - 2)),
                    (xy[3 + p] - xy[p]) + (yy[3] - yy[0]),
                    (xz[3 + p] - xz[p]) + (yz[3] - yz[0]),
                )
                for c in range(3):
                    own = pl.ds(pl.multiple_of(at + o, 8), 8)
                    Vf[c, own, :] = Vf[c, own, :] + gain * (
                        27.0 * close[c] - far[c] + deep[c, x + p, pl.ds(j, 8), :])

    def stress_pair(x):
        def material(x, rows):
            return lam[x, rows, :], mu[x, rows, :], rel[x, rows, :], ane[x, rows, :]

        def put(c, x, at, rows, stress, memory):
            Sf[c, pl.ds(pl.multiple_of(at, 8), 8), :] = stress
            M[c, x, rows, :] = memory

        stress_tiles(x, x, (CY, ROW), Sf, Vf, M, deep, material, put)

    def interior(one):
        @pl.loop(0, (CX - 4) // 2)
        def _(i):
            one(2 * i + 2)

    def boundary(one):
        @pl.loop(0, 2)
        def _(i):
            one(i * (CX - 2))

    def candidates():
        row = lax.broadcasted_iota(jnp.int32, (TB, 128), 0)
        weights = jnp.where((row == 0) | (row == TB - 1), 0.5 / (TB - 1), 1.0 / (TB - 1))
        for t in range(STEPS):
            o = offset[t]
            for c in range(6):
                samples = rate[c, pl.ds(o, TB), :]
                cand[group, t, c:c + 1, :] = jnp.sum(samples * weights, axis=0, keepdims=True)
            cand[group, t, 6:8, :] = jnp.zeros((2, 128), jnp.float32)

    def c_copy(sender, receiver):
        return pltpu.make_async_remote_copy(
            cand.at[sender], cand.at[sender], c_send.at[receiver], c_recv.at[sender],
            device_id={"strike": receiver * NA + parity}, device_id_type=MESH)

    def over_groups(act):
        @pl.loop(0, NB)
        def _(g):
            @pl.when(g != group)
            def _():
                act(g)

    def pair_copy(which):
        return pltpu.make_async_remote_copy(
            pair.at[which], pair.at[which], p_send, p_recv, device_id=other, device_id_type=MESH)

    def g_copy(which, h):
        return pltpu.make_async_remote_copy(
            chosen, gathered.at[which], g_send.at[h], g_recv.at[which],
            device_id={"dip": fault, "depth": h}, device_id_type=MESH)

    def over_fault(act):
        @pl.loop(0, NH)
        def _(h):
            @pl.when(jnp.logical_not(on_fault & (h == d)))
            def _():
                act(h)

    def source_first():
        loads[1].wait()
        for copy in order:
            copy.wait()
        candidates()
        over_groups(lambda g: c_copy(group, g).start())

    def source_second():
        over_groups(lambda g: c_copy(g, group).wait_recv())
        for t in range(STEPS):
            pair[parity, t] = cand[lax.div(active[t], NA), t]
        pair_copy(parity).start()

    def source_third():
        pair_copy(lax.rem(parity + 1, NA)).wait_recv()
        for t in range(STEPS):
            value = pair[lax.rem(active[t], NA), t]
            chosen[t] = value

            @pl.when(on_fault)
            def _(t=t, value=value):
                gathered[chunk, t] = value

        over_fault(lambda h: g_copy(chunk, h).start())

    def source_gather():
        @pl.when(on_fault)
        def _():
            @pl.loop(0, ND * NH)
            def _(j):
                @pl.when(j != chunk)
                def _():
                    g_copy(j, 0).wait_recv()

    def source_plane(t):
        @pl.when(on_fault)
        def _():
            seg = active[t]
            depth_total = 128 * NH
            acc[...] = jnp.zeros_like(acc)
            wide = 8 * 128

            @pl.loop(0, SUBF // wide)
            def _(i):
                cell = cells[pl.ds(seg, 1), pl.ds(pl.multiple_of(i * wide, wide), wide)]
                cell_x = lax.div(cell, depth_total)
                cell_z = cell - cell_x * depth_total - d * 128
                cell_x = cell_x - s * CX
                hot_z = (lax.broadcasted_iota(jnp.int32, (128, wide), 0) == cell_z).astype(jnp.float32).astype(jnp.bfloat16)
                hot_x = lax.broadcasted_iota(jnp.int32, (CX, wide), 0) == cell_x
                value = jnp.concatenate([gathered[8 * i + n, t] for n in range(8)], axis=1)
                parts = []
                for _ in range(3):
                    part = value.astype(jnp.bfloat16).astype(jnp.float32)
                    parts.append(part)
                    value = value - part
                rows = [
                    jnp.where(hot_x, part[c:c + 1, :], 0.0).astype(jnp.bfloat16)
                    for part in parts for c in range(6)
                ]
                acc[...] += lax.dot_general(
                    jnp.concatenate(rows, axis=0), hot_z, (((1,), (1,)), ((), ())),
                    preferred_element_type=jnp.float32)

            n = 6 * CX
            (plane if t == 0 else last_plane)[...] = acc[0:n] + acc[n:2 * n] + acc[2 * n:3 * n]

    def apply_source(ref, spans):
        @pl.when(on_fault)
        def _():
            for c in range(6):
                for x0, n in spans:
                    at = pl.ds((x0 + XP) * ROW + YP, n, stride=ROW)
                    Sf[c, at, :] = Sf[c, at, :] - ref[c * CX + x0:c * CX + x0 + n, :]

    edges = ((0, 2), (CX - 2, 2))
    middle = ((2, CX - 4),)

    i, j = (lax.broadcasted_iota(jnp.int32, (256, 128), n) for n in range(2))
    off = (i & 127) - j
    for n, (a, b) in enumerate(((1, 0), (0, -1))):
        weight = jnp.where(off == a, 27.0, jnp.where(off == b, -27.0, jnp.where(
            off == a + 1, -1.0, jnp.where(off == b - 1, 1.0, 0.0))))
        band[n] = weight.astype(jnp.bfloat16)

    @pl.when(jnp.logical_not(on_fault))
    def _():
        last_plane[...] = jnp.zeros_like(last_plane)

    loads[0].wait()
    yz_send(0)
    source_first()
    deep_all(0)
    loads[2].wait()
    loads[3].wait()
    yz_recv(0)
    interior(velocity_pair)
    source_second()
    x_wait_recv(0)
    boundary(velocity_pair)
    x_start(1)
    yz_send(1)
    source_third()
    deep_all(1)
    for copy in loads[4:]:
        copy.wait()
    yz_recv(1)
    interior(stress_pair)
    source_gather()
    source_plane(0)
    apply_source(plane, middle)
    x_wait_recv(1)
    x_wait_send(0)
    boundary(stress_pair)
    apply_source(plane, edges)
    x_start(2)
    yz_send(2)
    deep_all(2)
    source_plane(1)
    x_wait_send(1)
    yz_recv(2)
    interior(velocity_pair)
    x_wait_recv(2)
    boundary(velocity_pair)
    x_start(3)
    yz_send(3)
    deep_all(3)
    yz_recv(3)
    interior(stress_pair)
    apply_source(last_plane, middle)
    x_wait_recv(3)

    x_wait_send(2)
    x_wait_send(3)
    for h in range(4):
        up, dn = y_copies(h)
        each(has["k_up"], [up], lambda c: c.wait_send())
        each(has["k_dn"], [dn], lambda c: c.wait_send())
        up, dn = z_copies(h)
        each(has["d_up"], [up], lambda c: c.wait_send())
        each(has["d_dn"], [dn], lambda c: c.wait_send())
    over_groups(lambda g: c_copy(group, g).wait_send())
    pair_copy(parity).wait_send()
    over_fault(lambda h: g_copy(chunk, h).wait_send())


def solution(mesh):
    ns, nd, nh = (mesh.shape[a] for a in ("strike", "dip", "depth"))

    def body(velocity, stress, memory, lam, mu, buo, rel, ane, rate, cell, active, offset):
        cx, cy, cz = lam.shape
        subf = cell.shape[1]
        assert cz == 128 and subf == 128 * nd * nh
        planes, rows = cx + 2 * XP, cy + 2 * YP
        f32 = jnp.float32
        block = pltpu.VMEM((cx, cy, cz), f32)
        dma = pltpu.SemaphoreType.DMA
        hbm = pl.BlockSpec(memory_space=pltpu.HBM)
        vmem = pl.BlockSpec(memory_space=pltpu.VMEM)
        between = (
            pltpu.VMEM((6, planes, rows, cz), f32),
            pltpu.VMEM((3, planes, rows, cz), f32),
            pltpu.VMEM((6, cx, cy, cz), f32),
            pltpu.VMEM((3, cx, cy, cz), f32),
            pltpu.VMEM((4, 4, cy, cz), f32),
            pltpu.VMEM((6 * cx, cz), f32),
        )
        held = pl.pallas_call(
            functools.partial(kernel, (ns, nd, nh, cx, cy, subf)),
            out_shape=between,
            in_specs=[hbm] * 12,
            out_specs=(vmem,) * 6,
            scratch_shapes=[
                block, block, block, block, block,
                pltpu.VMEM((6, rate.shape[1], 128), f32),
                pltpu.VMEM(cell.shape, jnp.int32),
                pltpu.SMEM(active.shape, jnp.int32),
                pltpu.SMEM(offset.shape, jnp.int32),
                pltpu.VMEM((4, 5, cx, cz), f32),
                pltpu.VMEM((4, 5, cx, cz), f32),
                pltpu.VMEM((4, 5, cx, cz), f32),
                pltpu.VMEM((4, 5, cx, cz), f32),
                pltpu.VMEM((4, 2, cy, cz), f32),
                pltpu.VMEM((4, 2, cy, cz), f32),
                pltpu.VMEM((4, 2, cy, cz), f32),
                pltpu.VMEM((2, 2 * cz, cz), jnp.bfloat16),
                pltpu.VMEM((ns // NA, STEPS, 8, 128), f32),
                pltpu.VMEM((NA, STEPS, 8, 128), f32),
                pltpu.VMEM((STEPS, 8, 128), f32),
                pltpu.VMEM((nd * nh, STEPS, 8, 128), f32),
                pltpu.VMEM((3 * 6 * cx, cz), f32),
                pltpu.VMEM((6 * cx, cz), f32),
                dma((20,)), dma((4, 4)), dma((4, 4)), dma((4, 2)), dma((4, 2)), dma((4, 2)), dma((4, 2)),
                dma((ns // NA,)), dma((ns // NA,)), dma, dma, dma((nh,)), dma((nd * nh,)),
            ],
            compiler_params=pltpu.CompilerParams(
                collective_id=0, has_side_effects=True, vmem_limit_bytes=40 * 1024 * 1024
            ),
            cost_estimate=pl.CostEstimate(flops=30_000_000, bytes_accessed=6_000_000, transcendentals=0),
        )(*(
            pltpu.with_memory_space_constraint(a, pltpu.HBM)
            for a in (velocity, stress, memory, lam, mu, buo, rel, ane, jnp.transpose(rate, (0, 2, 1, 3)), cell, active, offset)
        ))
        return pl.pallas_call(
            functools.partial(finish, (cx, cy)),
            out_shape=tuple(jax.ShapeDtypeStruct(a.shape, f32) for a in (velocity, stress, memory)),
            in_specs=[vmem] * 6,
            out_specs=(hbm,) * 3,
            scratch_shapes=[
                pltpu.VMEM((6, 4, cy, cz), f32),
                pltpu.VMEM((6, 4, cy, cz), f32),
                dma((7,)),
            ],
            compiler_params=pltpu.CompilerParams(vmem_limit_bytes=40 * 1024 * 1024),
            cost_estimate=pl.CostEstimate(flops=2_000_000, bytes_accessed=4_000_000, transcendentals=0),
        )(*held)

    field = P(None, "strike", "dip", "depth")
    cellwise = P("strike", "dip", "depth")
    return jax.shard_map(
        body,
        mesh=mesh,
        in_specs=(field,) * 3 + (cellwise,) * 5 + (P("strike", None, None, None), P(), P(), P()),
        out_specs=(field,) * 3,
        check_vma=False,
    )
```

```python
import functools

import jax
import jax.numpy as jnp
from jax import lax
from jax.experimental import pallas as pl
from jax.experimental.pallas import tpu as pltpu
from jax.sharding import PartitionSpec as P

MESH = pl.DeviceIdType.MESH
TB = 8
STEPS = 2
R24 = 0.12 / 24.0
XP = 2
YP = 8
NA = 2

X_GROUPS = {"s": ((0, 1, 1, 2), (3, 2, 2, 1)), "v": ((0, 1, 2, 1), (1, 2, 1, 2))}
Y_FIELDS = {"s": ((3, True), (5, True), (1, False)), "v": ((1, True), (0, False), (2, False))}
Z_FIELDS = {"s": (4, 5, 2), "v": (0, 1, 2)}
Z_BACK = {"s": (True, True, False), "v": (False, False, True)}


def stress_tiles(x, m, sizes, tiles, Sf, Vf, M, deep, material, put):
    CY, ROW = sizes
    for j in tiles:
        at = (x + XP) * ROW + YP + j
        rows = pl.ds(j, 8)

        def get(c, n, at=at):
            return Vf[c, pl.ds(at + n, 8), :]

        vx = [get(0, n * ROW) for n in range(-2, 3)]
        vy = [get(1, n * ROW) for n in range(-1, 4)]
        vz = [get(2, n * ROW) for n in range(-1, 4)]
        for p in range(2):
            o = p * ROW
            lam, mu, relax, ane = material(m + p, rows)
            shear = R24 * mu
            twice = 2.0 * shear
            part = (1.0 - relax) * ane
            vx_at, vy_at, vz_at = vx[2 + p], vy[1 + p], vz[1 + p]
            xx = 27.0 * (vx_at - vx[1 + p]) - (vx[3 + p] - vx[p])
            yy = 27.0 * (vy_at - get(1, o - 1)) - (get(1, o + 1) - get(1, o - 2))
            zz = deep[2, x + p, rows, :]
            normal = R24 * lam * (xx + yy + zz)
            xy = 27.0 * ((get(0, o + 1) - vx_at) + (vy[2 + p] - vy_at)) - (
                (get(0, o + 2) - get(0, o - 1)) + (vy[3 + p] - vy[p]))
            xz = 27.0 * (vz[2 + p] - vz_at) - (vz[3 + p] - vz[p]) + deep[0, x + p, rows, :]
            yz = 27.0 * (get(2, o + 1) - vz_at) - (get(2, o + 2) - get(2, o - 1)) + deep[1, x + p, rows, :]
            grown = (
                normal + twice * xx, normal + twice * yy, normal + twice * zz,
                shear * xy, shear * xz, shear * yz,
            )
            for c in range(6):
                old = M[c, x + p, rows, :]
                new = relax * old + part * grown[c]
                stress = Sf[c, pl.ds(pl.multiple_of(at + o, 8), 8), :] + grown[c] - 0.5 * (old + new)
                put(c, x + p, at + o, rows, stress, new)


def finish(dims, S, V, M, deep, edge, plane, vel_out, str_out, mem_out, stress, memory, sem):
    CX, CY = dims
    ROW = CY + 2 * YP
    own = pl.ds(YP, CY)
    middle = pl.ds(2, CX - 4)
    copies = [
        pltpu.make_async_copy(V.at[:, pl.ds(XP, CX), own], vel_out, sem.at[0]),
        pltpu.make_async_copy(S.at[:, pl.ds(XP + 2, CX - 4), own], str_out.at[:, middle], sem.at[1]),
        pltpu.make_async_copy(M.at[:, middle], mem_out.at[:, middle], sem.at[2]),
    ]
    for copy in copies:
        copy.start()
    Sf = S.reshape(6, (CX + 2 * XP) * ROW, 128)
    Vf = V.reshape(3, (CX + 2 * XP) * ROW, 128)

    @pl.loop(0, 2)
    def _(i):
        x = i * (CX - 2)

        def material(m, rows):
            return tuple(edge[n, m, rows, :] for n in range(4))

        def put(c, at_x, at, rows, s, m):
            place = at_x - i * (CX - 4)
            stress[c, place, rows, :] = s
            memory[c, place, rows, :] = m

        stress_tiles(x, 2 * i, (CY, ROW), range(0, CY, 8), Sf, Vf, M, deep, material, put)

    for c in range(6):
        for n, x in enumerate((0, 1, CX - 2, CX - 1)):
            stress[c, n, 0:1, :] = stress[c, n, 0:1, :] - plane[c * CX + x:c * CX + x + 1, :]
    for n in range(2):
        here, there = pl.ds(2 * n, 2), pl.ds(n * (CX - 2), 2)
        copies.append(pltpu.make_async_copy(stress.at[:, here], str_out.at[:, there], sem.at[3 + 2 * n]))
        copies.append(pltpu.make_async_copy(memory.at[:, here], mem_out.at[:, there], sem.at[4 + 2 * n]))
    for copy in copies[3:]:
        copy.start()
    for copy in copies:
        copy.wait()


def kernel(
    dims,
    vel_hbm, str_hbm, mem_hbm, lam_hbm, mu_hbm, buo_hbm, rel_hbm, ane_hbm, rate_hbm, cell_hbm,
    active_hbm, offset_hbm,
    S, V, M, deep, edge, last_plane,
    lam, mu, buo, rel, ane, rate, cells, active, offset,
    ysend_up, ysend_dn, yrecv_up, yrecv_dn, zsend, zrecv_up, zrecv_dn, band,
    cand, pair, chosen, gathered, acc, plane,
    ld_sem, xs_sem, xr_sem, ys_sem, yr_sem, zs_sem, zr_sem,
    c_send, c_recv, p_send, p_recv, g_send, g_recv,
):
    NS, ND, NH, CX, CY, SUBF = dims
    ROW = CY + 2 * YP
    HALF = CY // 2
    NB = NS // NA
    s = lax.axis_index("strike")
    k = lax.axis_index("dip")
    d = lax.axis_index("depth")
    fault = ND // 2
    on_fault = k == fault
    group, parity = lax.div(s, NA), lax.rem(s, NA)
    chunk = k * NH + d

    def near(axis, pos, size, step):
        return {axis: jnp.clip(pos + step, 0, size - 1)}

    s_up, s_dn = near("strike", s, NS, 1), near("strike", s, NS, -1)
    k_up, k_dn = near("dip", k, ND, 1), near("dip", k, ND, -1)
    d_up, d_dn = near("depth", d, NH, 1), near("depth", d, NH, -1)
    has = {
        "s_up": s < NS - 1, "s_dn": s > 0,
        "k_up": k < ND - 1, "k_dn": k > 0,
        "d_up": d < NH - 1, "d_dn": d > 0,
    }

    inner = (slice(None), pl.ds(XP, CX), pl.ds(YP, CY))
    loads = [
        pltpu.make_async_copy(str_hbm, S.at[inner], ld_sem.at[0]),
        pltpu.make_async_copy(
            rate_hbm.at[0, :, :, pl.ds(pl.multiple_of(chunk * 128, 128), 128)], rate, ld_sem.at[1]
        ),
        pltpu.make_async_copy(vel_hbm, V.at[inner], ld_sem.at[2]),
        pltpu.make_async_copy(buo_hbm, buo, ld_sem.at[3]),
        pltpu.make_async_copy(mem_hbm, M, ld_sem.at[4]),
        pltpu.make_async_copy(lam_hbm, lam, ld_sem.at[5]),
        pltpu.make_async_copy(mu_hbm, mu, ld_sem.at[6]),
        pltpu.make_async_copy(rel_hbm, rel, ld_sem.at[7]),
        pltpu.make_async_copy(ane_hbm, ane, ld_sem.at[8]),
        pltpu.make_async_copy(cell_hbm, cells, ld_sem.at[9]),
    ]
    for n, ref in enumerate((lam_hbm, mu_hbm, rel_hbm, ane_hbm)):
        for m in range(2):
            loads.append(pltpu.make_async_copy(
                ref.at[pl.ds(m * (CX - 2), 2)], edge.at[n, pl.ds(2 * m, 2)], ld_sem.at[10 + 2 * n + m]))
    order = (
        pltpu.make_async_copy(active_hbm, active, ld_sem.at[18]),
        pltpu.make_async_copy(offset_hbm, offset, ld_sem.at[19]),
    )
    for copy in (loads[1], *order, loads[0], loads[2], loads[3]):
        copy.start()

    barrier = pltpu.get_barrier_semaphore()
    count = jnp.int32(0)
    for name, to in (("s_up", s_up), ("s_dn", s_dn), ("k_up", k_up), ("k_dn", k_dn), ("d_up", d_up), ("d_dn", d_dn)):
        there = has[name]
        count = count + there.astype(jnp.int32)

        @pl.when(there)
        def _(to=to):
            pl.semaphore_signal(barrier, inc=1, device_id=to, device_id_type=MESH)

    other = {"strike": group * NA + lax.rem(parity + 1, NA)}
    pl.semaphore_signal(barrier, inc=1, device_id=other, device_id_type=MESH)
    count = count + 1

    @pl.loop(0, NB)
    def _(g):
        @pl.when(g != group)
        def _():
            pl.semaphore_signal(
                barrier, inc=1, device_id={"strike": g * NA + parity}, device_id_type=MESH
            )

    count = count + (NB - 1)

    @pl.loop(0, NH)
    def _(h):
        @pl.when(jnp.logical_not(on_fault & (h == d)))
        def _():
            pl.semaphore_signal(
                barrier, inc=1, device_id={"dip": fault, "depth": h}, device_id_type=MESH
            )

    count = count + NH - on_fault.astype(jnp.int32)

    @pl.when(on_fault)
    def _():
        @pl.loop(0, ND * NH)
        def _(j):
            @pl.when(j != chunk)
            def _():
                pl.semaphore_signal(
                    barrier, inc=1,
                    device_id={"dip": lax.div(j, NH), "depth": lax.rem(j, NH)},
                    device_id_type=MESH,
                )

    count = count + jnp.where(on_fault, ND * NH - 1, 0)
    pl.semaphore_wait(barrier, count)

    def x_copies(h, half):
        kind = "sv"[h % 2]
        ref = S if kind == "s" else V
        up, dn = [], []
        for n, (c0, nc, lu, ld) in enumerate(X_GROUPS[kind]):
            comps = pl.ds(c0, nc)
            rows = pl.ds(YP + half * HALF, HALF)
            if h == 0:
                whole = pl.ds(half * HALF, HALF)
                src_up = str_hbm.at[comps, pl.ds(CX - lu, lu), whole]
                src_dn = str_hbm.at[comps, pl.ds(0, ld), whole]
            else:
                src_up = ref.at[comps, pl.ds(XP + CX - lu, lu), rows]
                src_dn = ref.at[comps, pl.ds(XP, ld), rows]
            up.append(pltpu.make_async_remote_copy(
                src_up, ref.at[comps, pl.ds(XP - lu, lu), rows],
                xs_sem.at[h, half, n], xr_sem.at[h, half, n], device_id=s_up, device_id_type=MESH))
            dn.append(pltpu.make_async_remote_copy(
                src_dn, ref.at[comps, pl.ds(XP + CX, ld), rows],
                xs_sem.at[h, half, 2 + n], xr_sem.at[h, half, 2 + n], device_id=s_dn, device_id_type=MESH))
        return up, dn

    def each(there, copies, act):
        @pl.when(there)
        def _():
            for copy in copies:
                act(copy)

    def x_start(h, half):
        up, dn = x_copies(h, half)
        each(has["s_up"], up, lambda c: c.start())
        each(has["s_dn"], dn, lambda c: c.start())

    def x_wait_recv(h, half):
        up, dn = x_copies(h, half)
        each(has["s_dn"], up, lambda c: c.wait_recv())
        each(has["s_up"], dn, lambda c: c.wait_recv())

    def x_wait_send(h):
        for half in range(2):
            up, dn = x_copies(h, half)
            each(has["s_up"], up, lambda c: c.wait_send())
            each(has["s_dn"], dn, lambda c: c.wait_send())

    x_start(0, 0)
    x_start(0, 1)

    Sf = S.reshape(6, (CX + 2 * XP) * ROW, 128)
    Vf = V.reshape(3, (CX + 2 * XP) * ROW, 128)
    flat = {"s": Sf, "v": Vf}

    for F, nc in ((S, 6), (V, 3)):
        zero_x = jnp.zeros((nc, XP, CY, 128), jnp.float32)

        @pl.when(s == 0)
        def _(F=F, zero_x=zero_x):
            F[:, 0:XP, YP:YP + CY, :] = zero_x

        @pl.when(s == NS - 1)
        def _(F=F, zero_x=zero_x):
            F[:, XP + CX:, YP:YP + CY, :] = zero_x

    zero_y = jnp.zeros(yrecv_up.shape, jnp.float32)
    zero_z = jnp.zeros(zrecv_up.shape, jnp.float32)
    for there, ref, zero in (
        (has["k_dn"], yrecv_up, zero_y), (has["k_up"], yrecv_dn, zero_y),
        (has["d_dn"], zrecv_up, zero_z), (has["d_up"], zrecv_dn, zero_z),
    ):
        @pl.when(jnp.logical_not(there))
        def _(ref=ref, zero=zero):
            ref[...] = zero

    def y_layers(kind):
        up, dn = [], []
        for c, back in Y_FIELDS[kind]:
            up += [(c, CY - 2), (c, CY - 1)] if back else [(c, CY - 1)]
            dn += [(c, 0)] if back else [(c, 0), (c, 1)]
        return up, dn

    def y_copies(h):
        up, dn = y_layers("sv"[h % 2])
        nu, nd = len(up), len(dn)
        return (
            pltpu.make_async_remote_copy(
                ysend_up.at[h, pl.ds(0, nu)], yrecv_up.at[h, pl.ds(0, nu)],
                ys_sem.at[h, 0], yr_sem.at[h, 0], device_id=k_up, device_id_type=MESH),
            pltpu.make_async_remote_copy(
                ysend_dn.at[h, pl.ds(0, nd)], yrecv_dn.at[h, pl.ds(0, nd)],
                ys_sem.at[h, 1], yr_sem.at[h, 1], device_id=k_dn, device_id_type=MESH),
        )

    def z_copies(h):
        return (
            pltpu.make_async_remote_copy(
                zsend.at[h], zrecv_up.at[h],
                zs_sem.at[h, 0], zr_sem.at[h, 0], device_id=d_up, device_id_type=MESH),
            pltpu.make_async_remote_copy(
                zsend.at[h], zrecv_dn.at[h],
                zs_sem.at[h, 1], zr_sem.at[h, 1], device_id=d_dn, device_id_type=MESH),
        )

    lane = lax.broadcasted_iota(jnp.int32, (CY, 128), 1)
    slot = lane >> 2
    quarter = lane & 3

    def turn(value, n):
        return pltpu.roll(value, n % 128, 1)

    def yz_send(h):
        kind = "sv"[h % 2]
        F = flat[kind]
        up, dn = y_layers(kind)
        base = XP * ROW + YP
        for n, (c, row) in enumerate(up):
            ysend_up[h, n] = F[c, pl.ds(base + row, CX, stride=ROW), :]
        for n, (c, row) in enumerate(dn):
            ysend_dn[h, n] = F[c, pl.ds(base + row, CX, stride=ROW), :]
        up, dn = y_copies(h)
        each(has["k_up"], [up], lambda c: c.start())
        each(has["k_dn"], [dn], lambda c: c.start())

        first = second = jnp.zeros((CY, 128), jnp.float32)
        for x in range(CX):
            a, b, c = (F[comp, pl.ds((x + XP) * ROW + YP, CY), :] for comp in Z_FIELDS[kind])
            first = jnp.where(slot == x, turn(a, 4 * x + 2), first)
            first = jnp.where(slot == x + CX, turn(b, 4 * x + 66), first)
            second = jnp.where(slot == x, turn(c, 4 * x + 2), second)
        zsend[h, 0] = first
        zsend[h, 1] = second
        up, dn = z_copies(h)
        each(has["d_up"], [up], lambda c: c.start())
        each(has["d_dn"], [dn], lambda c: c.start())

    def yz_recv(h):
        kind = "sv"[h % 2]
        F = flat[kind]
        up, dn = y_copies(h)
        each(has["k_dn"], [up], lambda c: c.wait_recv())
        each(has["k_up"], [dn], lambda c: c.wait_recv())
        up, dn = y_layers(kind)
        base = XP * ROW + YP
        for n, (c, row) in enumerate(up):
            F[c, pl.ds(base + row - CY, CX, stride=ROW), :] = yrecv_up[h, n]
        for n, (c, row) in enumerate(dn):
            F[c, pl.ds(base + row + CY, CX, stride=ROW), :] = yrecv_dn[h, n]
        up, dn = z_copies(h)
        each(has["d_dn"], [up], lambda c: c.wait_recv())
        each(has["d_up"], [dn], lambda c: c.wait_recv())
        fixes = []
        for n in range(2):
            mix = jnp.where(quarter < 2, zrecv_up[h, n], zrecv_dn[h, n])
            below, two_after = turn(mix, 1), turn(mix, -2)
            if Z_BACK[kind][2 * n]:
                fix = jnp.where(quarter == 0, -two_after, jnp.where(quarter == 1, below - 27.0 * mix, below))
            else:
                fix = jnp.where(quarter == 1, 27.0 * turn(mix, -1) - two_after, jnp.where(quarter == 0, -two_after, below))
            fixes.append(jnp.where(quarter == 3, 0.0, fix))
        for place, back in enumerate(Z_BACK[kind]):
            ends = (lane == 127) | (lane < 2) if back else (lane > 125) | (lane == 0)
            for x in range(CX):
                moved = turn(fixes[place // 2], (127 if back else 126) - 4 * x - 64 * (place % 2))
                deep[place, x] = deep[place, x] + jnp.where(ends, moved, 0.0)

    def deep_all(h):
        kind = "sv"[h % 2]
        F = S if kind == "s" else V
        for place, (comp, back) in enumerate(zip(Z_FIELDS[kind], Z_BACK[kind])):
            f = F[comp, XP:XP + CX, YP:YP + CY, :].reshape(CX * CY, 128)
            high = f.astype(jnp.bfloat16)
            low = (f - high.astype(jnp.float32)).astype(jnp.bfloat16)
            out = lax.dot_general(
                jnp.concatenate([high, low], axis=1), band[1 if back else 0],
                (((1,), (0,)), ((), ())), preferred_element_type=jnp.float32)
            deep[place] = out.reshape(CX, CY, 128)

    def velocity_pair(x, tiles):
        for j in tiles:
            at = (x + XP) * ROW + YP + j

            def get(c, n, Sf=Sf, at=at):
                return Sf[c, pl.ds(at + n, 8), :]

            xx = [get(0, n * ROW) for n in range(-1, 4)]
            xy = [get(3, n * ROW) for n in range(-2, 3)]
            xz = [get(4, n * ROW) for n in range(-2, 3)]
            for p in range(2):
                o = p * ROW
                gain = R24 * buo[x + p, pl.ds(j, 8), :]
                xy_at, yy, yz = xy[2 + p], [get(1, o + n) for n in range(-1, 3)], [get(5, o + n) for n in range(-2, 2)]
                close = (
                    (xx[2 + p] - xx[1 + p]) + (xy_at - get(3, o - 1)),
                    (xy_at - xy[1 + p]) + (yy[2] - yy[1]),
                    (xz[2 + p] - xz[1 + p]) + (yz[2] - yz[1]),
                )
                far = (
                    (xx[3 + p] - xx[p]) + (get(3, o + 1) - get(3, o - 2)),
                    (xy[3 + p] - xy[p]) + (yy[3] - yy[0]),
                    (xz[3 + p] - xz[p]) + (yz[3] - yz[0]),
                )
                for c in range(3):
                    own = pl.ds(pl.multiple_of(at + o, 8), 8)
                    Vf[c, own, :] = Vf[c, own, :] + gain * (
                        27.0 * close[c] - far[c] + deep[c, x + p, pl.ds(j, 8), :])

    def stress_pair(x, tiles):
        def material(x, rows):
            return lam[x, rows, :], mu[x, rows, :], rel[x, rows, :], ane[x, rows, :]

        def put(c, x, at, rows, stress, memory):
            Sf[c, pl.ds(pl.multiple_of(at, 8), 8), :] = stress
            M[c, x, rows, :] = memory

        stress_tiles(x, x, (CY, ROW), tiles, Sf, Vf, M, deep, material, put)

    def interior(one):
        @pl.loop(0, (CX - 4) // 2)
        def _(i):
            one(2 * i + 2, range(0, CY, 8))

    def boundary(one, half):
        @pl.loop(0, 2)
        def _(i):
            one(i * (CX - 2), range(half * HALF, (half + 1) * HALF, 8))

    def candidates():
        row = lax.broadcasted_iota(jnp.int32, (TB, 128), 0)
        weights = jnp.where((row == 0) | (row == TB - 1), 0.5 / (TB - 1), 1.0 / (TB - 1))
        for t in range(STEPS):
            o = offset[t]
            for c in range(6):
                samples = rate[c, pl.ds(o, TB), :]
                cand[group, t, c:c + 1, :] = jnp.sum(samples * weights, axis=0, keepdims=True)
            cand[group, t, 6:8, :] = jnp.zeros((2, 128), jnp.float32)

    def c_copy(sender, receiver):
        return pltpu.make_async_remote_copy(
            cand.at[sender], cand.at[sender], c_send.at[receiver], c_recv.at[sender],
            device_id={"strike": receiver * NA + parity}, device_id_type=MESH)

    def over_groups(act):
        @pl.loop(0, NB)
        def _(g):
            @pl.when(g != group)
            def _():
                act(g)

    def pair_copy(which):
        return pltpu.make_async_remote_copy(
            pair.at[which], pair.at[which], p_send, p_recv, device_id=other, device_id_type=MESH)

    def g_copy(which, h):
        return pltpu.make_async_remote_copy(
            chosen, gathered.at[which], g_send.at[h], g_recv.at[which],
            device_id={"dip": fault, "depth": h}, device_id_type=MESH)

    def over_fault(act):
        @pl.loop(0, NH)
        def _(h):
            @pl.when(jnp.logical_not(on_fault & (h == d)))
            def _():
                act(h)

    def source_first():
        loads[1].wait()
        for copy in order:
            copy.wait()
        candidates()
        over_groups(lambda g: c_copy(group, g).start())

    def source_second():
        over_groups(lambda g: c_copy(g, group).wait_recv())
        for t in range(STEPS):
            pair[parity, t] = cand[lax.div(active[t], NA), t]
        pair_copy(parity).start()

    def source_third():
        pair_copy(lax.rem(parity + 1, NA)).wait_recv()
        for t in range(STEPS):
            value = pair[lax.rem(active[t], NA), t]
            chosen[t] = value

            @pl.when(on_fault)
            def _(t=t, value=value):
                gathered[chunk, t] = value

        over_fault(lambda h: g_copy(chunk, h).start())

    def source_gather():
        @pl.when(on_fault)
        def _():
            @pl.loop(0, ND * NH)
            def _(j):
                @pl.when(j != chunk)
                def _():
                    g_copy(j, 0).wait_recv()

    def source_plane(t):
        @pl.when(on_fault)
        def _():
            seg = active[t]
            depth_total = 128 * NH
            acc[...] = jnp.zeros_like(acc)
            wide = 8 * 128

            @pl.loop(0, SUBF // wide)
            def _(i):
                cell = cells[pl.ds(seg, 1), pl.ds(pl.multiple_of(i * wide, wide), wide)]
                cell_x = lax.div(cell, depth_total)
                cell_z = cell - cell_x * depth_total - d * 128
                cell_x = cell_x - s * CX
                hot_z = (lax.broadcasted_iota(jnp.int32, (128, wide), 0) == cell_z).astype(jnp.float32).astype(jnp.bfloat16)
                hot_x = lax.broadcasted_iota(jnp.int32, (CX, wide), 0) == cell_x
                value = jnp.concatenate([gathered[8 * i + n, t] for n in range(8)], axis=1)
                parts = []
                for _ in range(3):
                    part = value.astype(jnp.bfloat16).astype(jnp.float32)
                    parts.append(part)
                    value = value - part
                rows = [
                    jnp.where(hot_x, part[c:c + 1, :], 0.0).astype(jnp.bfloat16)
                    for part in parts for c in range(6)
                ]
                acc[...] += lax.dot_general(
                    jnp.concatenate(rows, axis=0), hot_z, (((1,), (1,)), ((), ())),
                    preferred_element_type=jnp.float32)

            n = 6 * CX
            (plane if t == 0 else last_plane)[...] = acc[0:n] + acc[n:2 * n] + acc[2 * n:3 * n]

    def apply_source(ref, spans):
        @pl.when(on_fault)
        def _():
            for c in range(6):
                for x0, n in spans:
                    at = pl.ds((x0 + XP) * ROW + YP, n, stride=ROW)
                    Sf[c, at, :] = Sf[c, at, :] - ref[c * CX + x0:c * CX + x0 + n, :]

    edges = ((0, 2), (CX - 2, 2))
    middle = ((2, CX - 4),)

    i, j = (lax.broadcasted_iota(jnp.int32, (256, 128), n) for n in range(2))
    off = (i & 127) - j
    for n, (a, b) in enumerate(((1, 0), (0, -1))):
        weight = jnp.where(off == a, 27.0, jnp.where(off == b, -27.0, jnp.where(
            off == a + 1, -1.0, jnp.where(off == b - 1, 1.0, 0.0))))
        band[n] = weight.astype(jnp.bfloat16)

    @pl.when(jnp.logical_not(on_fault))
    def _():
        last_plane[...] = jnp.zeros_like(last_plane)

    source_first()
    loads[0].wait()
    for copy in loads[4:]:
        copy.start()
    yz_send(0)
    deep_all(0)
    source_second()
    loads[2].wait()
    loads[3].wait()
    yz_recv(0)
    interior(velocity_pair)
    source_third()
    for half in range(2):
        x_wait_recv(0, half)
        boundary(velocity_pair, half)
        x_start(1, half)
    yz_send(1)
    deep_all(1)
    for copy in loads[4:]:
        copy.wait()
    source_gather()
    source_plane(0)
    yz_recv(1)
    interior(stress_pair)
    apply_source(plane, middle)
    x_wait_send(0)
    for half in range(2):
        x_wait_recv(1, half)
        boundary(stress_pair, half)
        if half == 0:
            apply_source(plane, edges)
        x_start(2, half)
    yz_send(2)
    deep_all(2)
    source_plane(1)
    x_wait_send(1)
    yz_recv(2)
    interior(velocity_pair)
    for half in range(2):
        x_wait_recv(2, half)
        boundary(velocity_pair, half)
        x_start(3, half)
    yz_send(3)
    deep_all(3)
    yz_recv(3)
    interior(stress_pair)
    apply_source(last_plane, middle)
    for half in range(2):
        x_wait_recv(3, half)

    x_wait_send(2)
    x_wait_send(3)
    for h in range(4):
        up, dn = y_copies(h)
        each(has["k_up"], [up], lambda c: c.wait_send())
        each(has["k_dn"], [dn], lambda c: c.wait_send())
        up, dn = z_copies(h)
        each(has["d_up"], [up], lambda c: c.wait_send())
        each(has["d_dn"], [dn], lambda c: c.wait_send())
    over_groups(lambda g: c_copy(group, g).wait_send())
    pair_copy(parity).wait_send()
    over_fault(lambda h: g_copy(chunk, h).wait_send())


def solution(mesh):
    ns, nd, nh = (mesh.shape[a] for a in ("strike", "dip", "depth"))

    def body(velocity, stress, memory, lam, mu, buo, rel, ane, rate, cell, active, offset):
        cx, cy, cz = lam.shape
        subf = cell.shape[1]
        assert cz == 128 and subf == 128 * nd * nh
        planes, rows = cx + 2 * XP, cy + 2 * YP
        f32 = jnp.float32
        block = pltpu.VMEM((cx, cy, cz), f32)
        dma = pltpu.SemaphoreType.DMA
        hbm = pl.BlockSpec(memory_space=pltpu.HBM)
        vmem = pl.BlockSpec(memory_space=pltpu.VMEM)
        between = (
            pltpu.VMEM((6, planes, rows, cz), f32),
            pltpu.VMEM((3, planes, rows, cz), f32),
            pltpu.VMEM((6, cx, cy, cz), f32),
            pltpu.VMEM((3, cx, cy, cz), f32),
            pltpu.VMEM((4, 4, cy, cz), f32),
            pltpu.VMEM((6 * cx, cz), f32),
        )
        held = pl.pallas_call(
            functools.partial(kernel, (ns, nd, nh, cx, cy, subf)),
            out_shape=between,
            in_specs=[hbm] * 12,
            out_specs=(vmem,) * 6,
            scratch_shapes=[
                block, block, block, block, block,
                pltpu.VMEM((6, rate.shape[1], 128), f32),
                pltpu.VMEM(cell.shape, jnp.int32),
                pltpu.SMEM(active.shape, jnp.int32),
                pltpu.SMEM(offset.shape, jnp.int32),
                pltpu.VMEM((4, 5, cx, cz), f32),
                pltpu.VMEM((4, 5, cx, cz), f32),
                pltpu.VMEM((4, 5, cx, cz), f32),
                pltpu.VMEM((4, 5, cx, cz), f32),
                pltpu.VMEM((4, 2, cy, cz), f32),
                pltpu.VMEM((4, 2, cy, cz), f32),
                pltpu.VMEM((4, 2, cy, cz), f32),
                pltpu.VMEM((2, 2 * cz, cz), jnp.bfloat16),
                pltpu.VMEM((ns // NA, STEPS, 8, 128), f32),
                pltpu.VMEM((NA, STEPS, 8, 128), f32),
                pltpu.VMEM((STEPS, 8, 128), f32),
                pltpu.VMEM((nd * nh, STEPS, 8, 128), f32),
                pltpu.VMEM((3 * 6 * cx, cz), f32),
                pltpu.VMEM((6 * cx, cz), f32),
                dma((20,)), dma((4, 2, 4)), dma((4, 2, 4)), dma((4, 2)), dma((4, 2)), dma((4, 2)), dma((4, 2)),
                dma((ns // NA,)), dma((ns // NA,)), dma, dma, dma((nh,)), dma((nd * nh,)),
            ],
            compiler_params=pltpu.CompilerParams(
                collective_id=0, has_side_effects=True, vmem_limit_bytes=40 * 1024 * 1024
            ),
            cost_estimate=pl.CostEstimate(flops=30_000_000, bytes_accessed=6_000_000, transcendentals=0),
        )(*(
            pltpu.with_memory_space_constraint(a, pltpu.HBM)
            for a in (velocity, stress, memory, lam, mu, buo, rel, ane, jnp.transpose(rate, (0, 2, 1, 3)), cell, active, offset)
        ))
        return pl.pallas_call(
            functools.partial(finish, (cx, cy)),
            out_shape=tuple(jax.ShapeDtypeStruct(a.shape, f32) for a in (velocity, stress, memory)),
            in_specs=[vmem] * 6,
            out_specs=(hbm,) * 3,
            scratch_shapes=[
                pltpu.VMEM((6, 4, cy, cz), f32),
                pltpu.VMEM((6, 4, cy, cz), f32),
                dma((7,)),
            ],
            compiler_params=pltpu.CompilerParams(vmem_limit_bytes=40 * 1024 * 1024),
            cost_estimate=pl.CostEstimate(flops=2_000_000, bytes_accessed=4_000_000, transcendentals=0),
        )(*held)

    field = P(None, "strike", "dip", "depth")
    cellwise = P("strike", "dip", "depth")
    return jax.shard_map(
        body,
        mesh=mesh,
        in_specs=(field,) * 3 + (cellwise,) * 5 + (P("strike", None, None, None), P(), P(), P()),
        out_specs=(field,) * 3,
        check_vma=False,
    )
```

```python
import functools

import jax
import jax.numpy as jnp
from jax import lax
from jax.experimental import pallas as pl
from jax.experimental.pallas import tpu as pltpu
from jax.sharding import PartitionSpec as P

MESH = pl.DeviceIdType.MESH
TB = 8
STEPS = 2
R24 = 0.12 / 24.0
XP = 2
YP = 8
NA = 2

X_GROUPS = {"s": ((0, 1, 1, 2), (3, 2, 2, 1)), "v": ((0, 1, 2, 1), (1, 2, 1, 2))}
Y_FIELDS = {"s": ((3, True), (5, True), (1, False)), "v": ((1, True), (0, False), (2, False))}
Z_FIELDS = {"s": (4, 5, 2), "v": (0, 1, 2)}
Z_BACK = {"s": (True, True, False), "v": (False, False, True)}


def stress_tiles(x, m, sizes, tiles, Sf, Vf, M, deep, material, put):
    CY, ROW = sizes
    for j in tiles:
        at = (x + XP) * ROW + YP + j
        rows = pl.ds(j, 8)

        def get(c, n, at=at):
            return Vf[c, pl.ds(at + n, 8), :]

        vx = [get(0, n * ROW) for n in range(-2, 3)]
        vy = [get(1, n * ROW) for n in range(-1, 4)]
        vz = [get(2, n * ROW) for n in range(-1, 4)]
        for p in range(2):
            o = p * ROW
            lam, mu, relax, ane = material(m + p, rows)
            shear = R24 * mu
            twice = 2.0 * shear
            part = (1.0 - relax) * ane
            vx_at, vy_at, vz_at = vx[2 + p], vy[1 + p], vz[1 + p]
            xx = 27.0 * (vx_at - vx[1 + p]) - (vx[3 + p] - vx[p])
            yy = 27.0 * (vy_at - get(1, o - 1)) - (get(1, o + 1) - get(1, o - 2))
            zz = deep[2, x + p, rows, :]
            normal = R24 * lam * (xx + yy + zz)
            xy = 27.0 * ((get(0, o + 1) - vx_at) + (vy[2 + p] - vy_at)) - (
                (get(0, o + 2) - get(0, o - 1)) + (vy[3 + p] - vy[p]))
            xz = 27.0 * (vz[2 + p] - vz_at) - (vz[3 + p] - vz[p]) + deep[0, x + p, rows, :]
            yz = 27.0 * (get(2, o + 1) - vz_at) - (get(2, o + 2) - get(2, o - 1)) + deep[1, x + p, rows, :]
            grown = (
                normal + twice * xx, normal + twice * yy, normal + twice * zz,
                shear * xy, shear * xz, shear * yz,
            )
            for c in range(6):
                old = M[c, x + p, rows, :]
                new = relax * old + part * grown[c]
                stress = Sf[c, pl.ds(pl.multiple_of(at + o, 8), 8), :] + grown[c] - 0.5 * (old + new)
                put(c, x + p, at + o, rows, stress, new)


def finish(dims, S, V, M, deep, lam, mu, rel, ane, plane, vel_out, str_out, mem_out, stress, memory, sem):
    CX, CY = dims
    ROW = CY + 2 * YP
    own = pl.ds(YP, CY)
    middle = pl.ds(2, CX - 4)
    copies = [
        pltpu.make_async_copy(V.at[:, pl.ds(XP, CX), own], vel_out, sem.at[0]),
        pltpu.make_async_copy(S.at[:, pl.ds(XP + 2, CX - 4), own], str_out.at[:, middle], sem.at[1]),
        pltpu.make_async_copy(M.at[:, middle], mem_out.at[:, middle], sem.at[2]),
    ]
    for copy in copies:
        copy.start()
    Sf = S.reshape(6, (CX + 2 * XP) * ROW, 128)
    Vf = V.reshape(3, (CX + 2 * XP) * ROW, 128)

    @pl.loop(0, 2)
    def _(i):
        x = i * (CX - 2)

        def material(m, rows):
            return tuple(ref[m, rows, :] for ref in (lam, mu, rel, ane))

        def put(c, at_x, at, rows, s, m):
            place = at_x - i * (CX - 4)
            stress[c, place, rows, :] = s
            memory[c, place, rows, :] = m

        stress_tiles(x, x, (CY, ROW), range(0, CY, 8), Sf, Vf, M, deep, material, put)

    for c in range(6):
        for n, x in enumerate((0, 1, CX - 2, CX - 1)):
            stress[c, n, 0:1, :] = stress[c, n, 0:1, :] - plane[c * CX + x:c * CX + x + 1, :]
    for n in range(2):
        here, there = pl.ds(2 * n, 2), pl.ds(n * (CX - 2), 2)
        copies.append(pltpu.make_async_copy(stress.at[:, here], str_out.at[:, there], sem.at[3 + 2 * n]))
        copies.append(pltpu.make_async_copy(memory.at[:, here], mem_out.at[:, there], sem.at[4 + 2 * n]))
    for copy in copies[3:]:
        copy.start()
    for copy in copies:
        copy.wait()


def kernel(
    dims,
    vel_hbm, str_hbm, mem_hbm, lam_hbm, mu_hbm, buo_hbm, rel_hbm, ane_hbm, rate_hbm, cell_hbm,
    active_hbm, offset_hbm,
    S, V, M, deep, lam, mu, rel, ane, last_plane,
    buo, rate, cells, active, offset,
    ysend_up, ysend_dn, yrecv_up, yrecv_dn, zsend, zrecv_up, zrecv_dn, band,
    cand, pair, chosen, gathered, acc, plane,
    ld_sem, xs_sem, xr_sem, ys_sem, yr_sem, zs_sem, zr_sem,
    c_send, c_recv, p_send, p_recv, g_send, g_recv,
):
    NS, ND, NH, CX, CY, SUBF = dims
    ROW = CY + 2 * YP
    NB = NS // NA
    s = lax.axis_index("strike")
    k = lax.axis_index("dip")
    d = lax.axis_index("depth")
    fault = ND // 2
    on_fault = k == fault
    group, parity = lax.div(s, NA), lax.rem(s, NA)
    chunk = k * NH + d

    def near(axis, pos, size, step):
        return {axis: jnp.clip(pos + step, 0, size - 1)}

    s_up, s_dn = near("strike", s, NS, 1), near("strike", s, NS, -1)
    k_up, k_dn = near("dip", k, ND, 1), near("dip", k, ND, -1)
    d_up, d_dn = near("depth", d, NH, 1), near("depth", d, NH, -1)
    has = {
        "s_up": s < NS - 1, "s_dn": s > 0,
        "k_up": k < ND - 1, "k_dn": k > 0,
        "d_up": d < NH - 1, "d_dn": d > 0,
    }

    inner = (slice(None), pl.ds(XP, CX), pl.ds(YP, CY))
    loads = [
        pltpu.make_async_copy(str_hbm, S.at[inner], ld_sem.at[0]),
        pltpu.make_async_copy(
            rate_hbm.at[0, :, :, pl.ds(pl.multiple_of(chunk * 128, 128), 128)], rate, ld_sem.at[1]
        ),
        pltpu.make_async_copy(vel_hbm, V.at[inner], ld_sem.at[2]),
        pltpu.make_async_copy(buo_hbm, buo, ld_sem.at[3]),
        pltpu.make_async_copy(mem_hbm, M, ld_sem.at[4]),
        pltpu.make_async_copy(lam_hbm, lam, ld_sem.at[5]),
        pltpu.make_async_copy(mu_hbm, mu, ld_sem.at[6]),
        pltpu.make_async_copy(rel_hbm, rel, ld_sem.at[7]),
        pltpu.make_async_copy(ane_hbm, ane, ld_sem.at[8]),
        pltpu.make_async_copy(cell_hbm, cells, ld_sem.at[9]),
    ]
    order = (
        pltpu.make_async_copy(active_hbm, active, ld_sem.at[10]),
        pltpu.make_async_copy(offset_hbm, offset, ld_sem.at[11]),
    )
    for copy in (loads[1], *order, loads[0], loads[2], loads[3]):
        copy.start()

    barrier = pltpu.get_barrier_semaphore()
    count = jnp.int32(0)
    for name, to in (("s_up", s_up), ("s_dn", s_dn), ("k_up", k_up), ("k_dn", k_dn), ("d_up", d_up), ("d_dn", d_dn)):
        there = has[name]
        count = count + there.astype(jnp.int32)

        @pl.when(there)
        def _(to=to):
            pl.semaphore_signal(barrier, inc=1, device_id=to, device_id_type=MESH)

    other = {"strike": group * NA + lax.rem(parity + 1, NA)}
    pl.semaphore_signal(barrier, inc=1, device_id=other, device_id_type=MESH)
    count = count + 1

    @pl.loop(0, NB)
    def _(g):
        @pl.when(g != group)
        def _():
            pl.semaphore_signal(
                barrier, inc=1, device_id={"strike": g * NA + parity}, device_id_type=MESH
            )

    count = count + (NB - 1)

    @pl.loop(0, NH)
    def _(h):
        @pl.when(jnp.logical_not(on_fault & (h == d)))
        def _():
            pl.semaphore_signal(
                barrier, inc=1, device_id={"dip": fault, "depth": h}, device_id_type=MESH
            )

    count = count + NH - on_fault.astype(jnp.int32)

    @pl.when(on_fault)
    def _():
        @pl.loop(0, ND * NH)
        def _(j):
            @pl.when(j != chunk)
            def _():
                pl.semaphore_signal(
                    barrier, inc=1,
                    device_id={"dip": lax.div(j, NH), "depth": lax.rem(j, NH)},
                    device_id_type=MESH,
                )

    count = count + jnp.where(on_fault, ND * NH - 1, 0)
    pl.semaphore_wait(barrier, count)

    def x_copies(h):
        kind = "sv"[h % 2]
        ref = S if kind == "s" else V
        up, dn = [], []
        for n, (c0, nc, lu, ld) in enumerate(X_GROUPS[kind]):
            comps = pl.ds(c0, nc)
            rows = pl.ds(YP, CY)
            if h == 0:
                src_up = str_hbm.at[comps, pl.ds(CX - lu, lu)]
                src_dn = str_hbm.at[comps, pl.ds(0, ld)]
            else:
                src_up = ref.at[comps, pl.ds(XP + CX - lu, lu), rows]
                src_dn = ref.at[comps, pl.ds(XP, ld), rows]
            up.append(pltpu.make_async_remote_copy(
                src_up, ref.at[comps, pl.ds(XP - lu, lu), rows],
                xs_sem.at[h, n], xr_sem.at[h, n], device_id=s_up, device_id_type=MESH))
            dn.append(pltpu.make_async_remote_copy(
                src_dn, ref.at[comps, pl.ds(XP + CX, ld), rows],
                xs_sem.at[h, 2 + n], xr_sem.at[h, 2 + n], device_id=s_dn, device_id_type=MESH))
        return up, dn

    def each(there, copies, act):
        @pl.when(there)
        def _():
            for copy in copies:
                act(copy)

    def x_start(h):
        up, dn = x_copies(h)
        each(has["s_up"], up, lambda c: c.start())
        each(has["s_dn"], dn, lambda c: c.start())

    def x_wait_recv(h):
        up, dn = x_copies(h)
        each(has["s_dn"], up, lambda c: c.wait_recv())
        each(has["s_up"], dn, lambda c: c.wait_recv())

    def x_wait_send(h):
        up, dn = x_copies(h)
        each(has["s_up"], up, lambda c: c.wait_send())
        each(has["s_dn"], dn, lambda c: c.wait_send())

    x_start(0)

    Sf = S.reshape(6, (CX + 2 * XP) * ROW, 128)
    Vf = V.reshape(3, (CX + 2 * XP) * ROW, 128)
    flat = {"s": Sf, "v": Vf}

    for F, nc in ((S, 6), (V, 3)):
        zero_x = jnp.zeros((nc, XP, CY, 128), jnp.float32)

        @pl.when(s == 0)
        def _(F=F, zero_x=zero_x):
            F[:, 0:XP, YP:YP + CY, :] = zero_x

        @pl.when(s == NS - 1)
        def _(F=F, zero_x=zero_x):
            F[:, XP + CX:, YP:YP + CY, :] = zero_x

    for there, refs in (
        (has["k_dn"], yrecv_up), (has["k_up"], yrecv_dn), (has["d_dn"], zrecv_up), (has["d_up"], zrecv_dn),
    ):
        @pl.when(jnp.logical_not(there))
        def _(refs=refs):
            for ref in refs:
                ref[...] = jnp.zeros(ref.shape, jnp.float32)

    for refs in (ysend_up, ysend_dn):
        for ref in refs:
            ref[:, ref.shape[1] - 8:, :] = jnp.zeros((4, 8, 128), jnp.float32)

    def y_layers(kind):
        up, dn = [], []
        for c, back in Y_FIELDS[kind]:
            up += [(c, CY - 2), (c, CY - 1)] if back else [(c, CY - 1)]
            dn += [(c, 0)] if back else [(c, 0), (c, 1)]
        return up, dn

    PLANES = (tuple(range(2, CX - 2)), (0, 1, CX - 2, CX - 1))
    SPANS = (((2, CX - 4),), ((0, 2), (CX - 2, 2)))

    def y_copies(h, part):
        size = len(PLANES[part])
        nu, nd = (-(-len(layers) * size // 8) * 8 for layers in y_layers("sv"[h % 2]))
        return (
            pltpu.make_async_remote_copy(
                ysend_up[part].at[h, pl.ds(0, nu)], yrecv_up[part].at[h, pl.ds(0, nu)],
                ys_sem.at[h, part, 0], yr_sem.at[h, part, 0], device_id=k_up, device_id_type=MESH),
            pltpu.make_async_remote_copy(
                ysend_dn[part].at[h, pl.ds(0, nd)], yrecv_dn[part].at[h, pl.ds(0, nd)],
                ys_sem.at[h, part, 1], yr_sem.at[h, part, 1], device_id=k_dn, device_id_type=MESH),
        )

    def z_copies(h, part):
        return (
            pltpu.make_async_remote_copy(
                zsend[part].at[h], zrecv_up[part].at[h],
                zs_sem.at[h, part, 0], zr_sem.at[h, part, 0], device_id=d_up, device_id_type=MESH),
            pltpu.make_async_remote_copy(
                zsend[part].at[h], zrecv_dn[part].at[h],
                zs_sem.at[h, part, 1], zr_sem.at[h, part, 1], device_id=d_dn, device_id_type=MESH),
        )

    lane = lax.broadcasted_iota(jnp.int32, (CY, 128), 1)
    slot = lane >> 2
    quarter = lane & 3

    def turn(value, n):
        return pltpu.roll(value, n % 128, 1)

    def z_slot(part, place, n):
        if part == 0:
            return place // 2, n + 16 * (place % 2)
        return 0, n + 4 * place

    def yz_send(h, part):
        kind = "sv"[h % 2]
        F = flat[kind]
        base = XP * ROW + YP
        for layers, refs in zip(y_layers(kind), (ysend_up, ysend_dn)):
            at = 0
            for c, row in layers:
                for x0, n in SPANS[part]:
                    refs[part][h, at:at + n, :] = F[c, pl.ds(base + x0 * ROW + row, n, stride=ROW), :]
                    at += n
        up, dn = y_copies(h, part)
        each(has["k_up"], [up], lambda c: c.start())
        each(has["k_dn"], [dn], lambda c: c.start())
        arrays = [jnp.zeros((CY, 128), jnp.float32)] * (2 - part)
        for place, comp in enumerate(Z_FIELDS[kind]):
            for n, x in enumerate(PLANES[part]):
                where, index = z_slot(part, place, n)
                value = F[comp, pl.ds((x + XP) * ROW + YP, CY), :]
                arrays[where] = jnp.where(slot == index, turn(value, 4 * index + 2), arrays[where])
        for n, value in enumerate(arrays):
            zsend[part][h, n] = value
        up, dn = z_copies(h, part)
        each(has["d_up"], [up], lambda c: c.start())
        each(has["d_dn"], [dn], lambda c: c.start())

    def yz_recv(h, part):
        kind = "sv"[h % 2]
        F = flat[kind]
        up, dn = y_copies(h, part)
        each(has["k_dn"], [up], lambda c: c.wait_recv())
        each(has["k_up"], [dn], lambda c: c.wait_recv())
        base = XP * ROW + YP
        for layers, refs, shift in zip(y_layers(kind), (yrecv_up, yrecv_dn), (-CY, CY)):
            at = 0
            for c, row in layers:
                for x0, n in SPANS[part]:
                    F[c, pl.ds(base + x0 * ROW + row + shift, n, stride=ROW), :] = refs[part][h, at:at + n, :]
                    at += n
        up, dn = z_copies(h, part)
        each(has["d_dn"], [up], lambda c: c.wait_recv())
        each(has["d_up"], [dn], lambda c: c.wait_recv())
        fixes = {}
        for place, back in enumerate(Z_BACK[kind]):
            ends = (lane == 127) | (lane < 2) if back else (lane > 125) | (lane == 0)
            for n, x in enumerate(PLANES[part]):
                where, index = z_slot(part, place, n)
                if (where, back) not in fixes:
                    mix = jnp.where(quarter < 2, zrecv_up[part][h, where], zrecv_dn[part][h, where])
                    below, two_after = turn(mix, 1), turn(mix, -2)
                    if back:
                        fix = jnp.where(quarter == 0, -two_after, jnp.where(quarter == 1, below - 27.0 * mix, below))
                    else:
                        fix = jnp.where(quarter == 1, 27.0 * turn(mix, -1) - two_after, jnp.where(quarter == 0, -two_after, below))
                    fixes[where, back] = jnp.where(quarter == 3, 0.0, fix)
                moved = turn(fixes[where, back], (127 if back else 126) - 4 * index)
                deep[place, x] = deep[place, x] + jnp.where(ends, moved, 0.0)

    def deep_part(h, part):
        kind = "sv"[h % 2]
        F = S if kind == "s" else V
        for place, (comp, back) in enumerate(zip(Z_FIELDS[kind], Z_BACK[kind])):
            f = jnp.concatenate(
                [F[comp, XP + x0:XP + x0 + n, YP:YP + CY, :].reshape(n * CY, 128) for x0, n in SPANS[part]], axis=0)
            high = f.astype(jnp.bfloat16)
            low = (f - high.astype(jnp.float32)).astype(jnp.bfloat16)
            out = lax.dot_general(
                jnp.concatenate([high, low], axis=1), band[1 if back else 0],
                (((1,), (0,)), ((), ())), preferred_element_type=jnp.float32)
            at = 0
            for x0, n in SPANS[part]:
                deep[place, x0:x0 + n] = out[at:at + n * CY].reshape(n, CY, 128)
                at += n * CY

    def velocity_pair(x, tiles):
        for j in tiles:
            at = (x + XP) * ROW + YP + j

            def get(c, n, Sf=Sf, at=at):
                return Sf[c, pl.ds(at + n, 8), :]

            xx = [get(0, n * ROW) for n in range(-1, 4)]
            xy = [get(3, n * ROW) for n in range(-2, 3)]
            xz = [get(4, n * ROW) for n in range(-2, 3)]
            for p in range(2):
                o = p * ROW
                gain = R24 * buo[x + p, pl.ds(j, 8), :]
                xy_at, yy, yz = xy[2 + p], [get(1, o + n) for n in range(-1, 3)], [get(5, o + n) for n in range(-2, 2)]
                close = (
                    (xx[2 + p] - xx[1 + p]) + (xy_at - get(3, o - 1)),
                    (xy_at - xy[1 + p]) + (yy[2] - yy[1]),
                    (xz[2 + p] - xz[1 + p]) + (yz[2] - yz[1]),
                )
                far = (
                    (xx[3 + p] - xx[p]) + (get(3, o + 1) - get(3, o - 2)),
                    (xy[3 + p] - xy[p]) + (yy[3] - yy[0]),
                    (xz[3 + p] - xz[p]) + (yz[3] - yz[0]),
                )
                for c in range(3):
                    own = pl.ds(pl.multiple_of(at + o, 8), 8)
                    Vf[c, own, :] = Vf[c, own, :] + gain * (
                        27.0 * close[c] - far[c] + deep[c, x + p, pl.ds(j, 8), :])

    def stress_pair(x, tiles):
        def material(x, rows):
            return lam[x, rows, :], mu[x, rows, :], rel[x, rows, :], ane[x, rows, :]

        def put(c, x, at, rows, stress, memory):
            Sf[c, pl.ds(pl.multiple_of(at, 8), 8), :] = stress
            M[c, x, rows, :] = memory

        stress_tiles(x, x, (CY, ROW), tiles, Sf, Vf, M, deep, material, put)

    def interior(one):
        @pl.loop(0, (CX - 4) // 2)
        def _(i):
            one(2 * i + 2, range(0, CY, 8))

    def boundary(one):
        @pl.loop(0, 2)
        def _(i):
            one(i * (CX - 2), range(0, CY, 8))

    def candidates():
        row = lax.broadcasted_iota(jnp.int32, (TB, 128), 0)
        weights = jnp.where((row == 0) | (row == TB - 1), 0.5 / (TB - 1), 1.0 / (TB - 1))
        for t in range(STEPS):
            o = offset[t]
            for c in range(6):
                samples = rate[c, pl.ds(o, TB), :]
                cand[group, t, c:c + 1, :] = jnp.sum(samples * weights, axis=0, keepdims=True)
            cand[group, t, 6:8, :] = jnp.zeros((2, 128), jnp.float32)

    def c_copy(sender, receiver):
        return pltpu.make_async_remote_copy(
            cand.at[sender], cand.at[sender], c_send.at[receiver], c_recv.at[sender],
            device_id={"strike": receiver * NA + parity}, device_id_type=MESH)

    def over_groups(act):
        @pl.loop(0, NB)
        def _(g):
            @pl.when(g != group)
            def _():
                act(g)

    def pair_copy(which):
        return pltpu.make_async_remote_copy(
            pair.at[which], pair.at[which], p_send, p_recv, device_id=other, device_id_type=MESH)

    def g_copy(which, h):
        return pltpu.make_async_remote_copy(
            chosen, gathered.at[which], g_send.at[h], g_recv.at[which],
            device_id={"dip": fault, "depth": h}, device_id_type=MESH)

    def over_fault(act):
        @pl.loop(0, NH)
        def _(h):
            @pl.when(jnp.logical_not(on_fault & (h == d)))
            def _():
                act(h)

    def source_first():
        loads[1].wait()
        for copy in order:
            copy.wait()
        candidates()
        over_groups(lambda g: c_copy(group, g).start())

    def source_second():
        over_groups(lambda g: c_copy(g, group).wait_recv())
        for t in range(STEPS):
            pair[parity, t] = cand[lax.div(active[t], NA), t]
        pair_copy(parity).start()

    def source_third():
        pair_copy(lax.rem(parity + 1, NA)).wait_recv()
        for t in range(STEPS):
            value = pair[lax.rem(active[t], NA), t]
            chosen[t] = value

            @pl.when(on_fault)
            def _(t=t, value=value):
                gathered[chunk, t] = value

        over_fault(lambda h: g_copy(chunk, h).start())

    def source_gather():
        @pl.when(on_fault)
        def _():
            @pl.loop(0, ND * NH)
            def _(j):
                @pl.when(j != chunk)
                def _():
                    g_copy(j, 0).wait_recv()

    def source_plane(t):
        @pl.when(on_fault)
        def _():
            seg = active[t]
            depth_total = 128 * NH
            acc[...] = jnp.zeros_like(acc)
            wide = 8 * 128

            @pl.loop(0, SUBF // wide)
            def _(i):
                cell = cells[pl.ds(seg, 1), pl.ds(pl.multiple_of(i * wide, wide), wide)]
                cell_x = lax.div(cell, depth_total)
                cell_z = cell - cell_x * depth_total - d * 128
                cell_x = cell_x - s * CX
                hot_z = (lax.broadcasted_iota(jnp.int32, (128, wide), 0) == cell_z).astype(jnp.float32).astype(jnp.bfloat16)
                hot_x = lax.broadcasted_iota(jnp.int32, (CX, wide), 0) == cell_x
                value = jnp.concatenate([gathered[8 * i + n, t] for n in range(8)], axis=1)
                parts = []
                for _ in range(3):
                    part = value.astype(jnp.bfloat16).astype(jnp.float32)
                    parts.append(part)
                    value = value - part
                rows = [
                    jnp.where(hot_x, part[c:c + 1, :], 0.0).astype(jnp.bfloat16)
                    for part in parts for c in range(6)
                ]
                acc[...] += lax.dot_general(
                    jnp.concatenate(rows, axis=0), hot_z, (((1,), (1,)), ((), ())),
                    preferred_element_type=jnp.float32)

            n = 6 * CX
            (plane if t == 0 else last_plane)[...] = acc[0:n] + acc[n:2 * n] + acc[2 * n:3 * n]

    def apply_source(ref, spans):
        @pl.when(on_fault)
        def _():
            for c in range(6):
                for x0, n in spans:
                    at = pl.ds((x0 + XP) * ROW + YP, n, stride=ROW)
                    Sf[c, at, :] = Sf[c, at, :] - ref[c * CX + x0:c * CX + x0 + n, :]

    edges = ((0, 2), (CX - 2, 2))
    middle = ((2, CX - 4),)

    i, j = (lax.broadcasted_iota(jnp.int32, (256, 128), n) for n in range(2))
    off = (i & 127) - j
    for n, (a, b) in enumerate(((1, 0), (0, -1))):
        weight = jnp.where(off == a, 27.0, jnp.where(off == b, -27.0, jnp.where(
            off == a + 1, -1.0, jnp.where(off == b - 1, 1.0, 0.0))))
        band[n] = weight.astype(jnp.bfloat16)

    @pl.when(jnp.logical_not(on_fault))
    def _():
        last_plane[...] = jnp.zeros_like(last_plane)

    source_first()
    loads[0].wait()
    for copy in loads[4:]:
        copy.start()
    yz_send(0, 0)
    yz_send(0, 1)
    deep_part(0, 0)
    deep_part(0, 1)
    loads[2].wait()
    loads[3].wait()
    yz_recv(0, 0)
    source_second()
    interior(velocity_pair)
    yz_send(1, 0)
    source_third()
    deep_part(1, 0)
    yz_recv(0, 1)
    x_wait_recv(0)
    boundary(velocity_pair)
    x_start(1)
    yz_send(1, 1)
    for copy in loads[4:]:
        copy.wait()
    yz_recv(1, 0)
    interior(stress_pair)
    source_gather()
    source_plane(0)
    apply_source(plane, middle)
    yz_send(2, 0)
    deep_part(1, 1)
    deep_part(2, 0)
    x_wait_send(0)
    yz_recv(1, 1)
    x_wait_recv(1)
    boundary(stress_pair)
    apply_source(plane, edges)
    x_start(2)
    yz_send(2, 1)
    yz_recv(2, 0)
    interior(velocity_pair)
    yz_send(3, 0)
    deep_part(2, 1)
    deep_part(3, 0)
    source_plane(1)
    x_wait_send(1)
    yz_recv(2, 1)
    x_wait_recv(2)
    boundary(velocity_pair)
    x_start(3)
    yz_send(3, 1)
    yz_recv(3, 0)
    interior(stress_pair)
    apply_source(last_plane, middle)
    deep_part(3, 1)
    yz_recv(3, 1)
    x_wait_recv(3)

    x_wait_send(2)
    x_wait_send(3)
    for h in range(4):
        for part in range(2):
            for there, pair_of in (("k", y_copies(h, part)), ("d", z_copies(h, part))):
                each(has[there + "_up"], [pair_of[0]], lambda c: c.wait_send())
                each(has[there + "_dn"], [pair_of[1]], lambda c: c.wait_send())
    over_groups(lambda g: c_copy(group, g).wait_send())
    pair_copy(parity).wait_send()
    over_fault(lambda h: g_copy(chunk, h).wait_send())


def solution(mesh):
    ns, nd, nh = (mesh.shape[a] for a in ("strike", "dip", "depth"))

    def body(velocity, stress, memory, lam, mu, buo, rel, ane, rate, cell, active, offset):
        cx, cy, cz = lam.shape
        subf = cell.shape[1]
        assert cz == 128 and subf == 128 * nd * nh
        planes, rows = cx + 2 * XP, cy + 2 * YP
        f32 = jnp.float32
        block = pltpu.VMEM((cx, cy, cz), f32)
        dma = pltpu.SemaphoreType.DMA
        hbm = pl.BlockSpec(memory_space=pltpu.HBM)
        vmem = pl.BlockSpec(memory_space=pltpu.VMEM)
        between = (
            pltpu.VMEM((6, planes, rows, cz), f32),
            pltpu.VMEM((3, planes, rows, cz), f32),
            pltpu.VMEM((6, cx, cy, cz), f32),
            pltpu.VMEM((3, cx, cy, cz), f32),
            block, block, block, block,
            pltpu.VMEM((6 * cx, cz), f32),
        )
        held = pl.pallas_call(
            functools.partial(kernel, (ns, nd, nh, cx, cy, subf)),
            out_shape=between,
            in_specs=[hbm] * 12,
            out_specs=(vmem,) * 9,
            scratch_shapes=[
                block,
                pltpu.VMEM((6, rate.shape[1], 128), f32),
                pltpu.VMEM(cell.shape, jnp.int32),
                pltpu.SMEM(active.shape, jnp.int32),
                pltpu.SMEM(offset.shape, jnp.int32),
                *[(pltpu.VMEM((4, 64, cz), f32), pltpu.VMEM((4, 24, cz), f32))] * 4,
                *[(pltpu.VMEM((4, 2, cy, cz), f32), pltpu.VMEM((4, 1, cy, cz), f32))] * 3,
                pltpu.VMEM((2, 2 * cz, cz), jnp.bfloat16),
                pltpu.VMEM((ns // NA, STEPS, 8, 128), f32),
                pltpu.VMEM((NA, STEPS, 8, 128), f32),
                pltpu.VMEM((STEPS, 8, 128), f32),
                pltpu.VMEM((nd * nh, STEPS, 8, 128), f32),
                pltpu.VMEM((3 * 6 * cx, cz), f32),
                pltpu.VMEM((6 * cx, cz), f32),
                dma((12,)), dma((4, 4)), dma((4, 4)), dma((4, 2, 2)), dma((4, 2, 2)), dma((4, 2, 2)), dma((4, 2, 2)),
                dma((ns // NA,)), dma((ns // NA,)), dma, dma, dma((nh,)), dma((nd * nh,)),
            ],
            compiler_params=pltpu.CompilerParams(
                collective_id=0, has_side_effects=True, vmem_limit_bytes=40 * 1024 * 1024
            ),
            cost_estimate=pl.CostEstimate(flops=30_000_000, bytes_accessed=6_000_000, transcendentals=0),
        )(*(
            pltpu.with_memory_space_constraint(a, pltpu.HBM)
            for a in (velocity, stress, memory, lam, mu, buo, rel, ane, jnp.transpose(rate, (0, 2, 1, 3)), cell, active, offset)
        ))
        return pl.pallas_call(
            functools.partial(finish, (cx, cy)),
            out_shape=tuple(jax.ShapeDtypeStruct(a.shape, f32) for a in (velocity, stress, memory)),
            in_specs=[vmem] * 9,
            out_specs=(hbm,) * 3,
            scratch_shapes=[
                pltpu.VMEM((6, 4, cy, cz), f32),
                pltpu.VMEM((6, 4, cy, cz), f32),
                dma((7,)),
            ],
            compiler_params=pltpu.CompilerParams(vmem_limit_bytes=40 * 1024 * 1024),
            cost_estimate=pl.CostEstimate(flops=2_000_000, bytes_accessed=4_000_000, transcendentals=0),
        )(*held)

    field = P(None, "strike", "dip", "depth")
    cellwise = P("strike", "dip", "depth")
    return jax.shard_map(
        body,
        mesh=mesh,
        in_specs=(field,) * 3 + (cellwise,) * 5 + (P("strike", None, None, None), P(), P(), P()),
        out_specs=(field,) * 3,
        check_vma=False,
    )
```

```python
import functools

import jax
import jax.numpy as jnp
from jax import lax
from jax.experimental import pallas as pl
from jax.experimental.pallas import tpu as pltpu
from jax.sharding import PartitionSpec as P

MESH = pl.DeviceIdType.MESH
TB = 8
STEPS = 2
R24 = 0.12 / 24.0
XP = 2
YP = 8
NA = 2
CORES = 2

X_GROUPS = {"s": ((0, 1, 1, 2), (3, 2, 2, 1)), "v": ((0, 1, 2, 1), (1, 2, 1, 2))}
Y_FIELDS = {"s": ((3, True), (5, True), (1, False)), "v": ((1, True), (0, False), (2, False))}
Z_FIELDS = {"s": (4, 5, 2), "v": (0, 1, 2)}
Z_BACK = {"s": (True, True, False), "v": (False, False, True)}


def stress_tiles(x, m, sizes, tiles, Sf, Vf, M, deep, material, put):
    CY, ROW = sizes
    for j in tiles:
        at = (x + XP) * ROW + YP + j
        rows = pl.ds(j, 8)

        def get(c, n, at=at):
            return Vf[c, pl.ds(at + n, 8), :]

        vx = [get(0, n * ROW) for n in range(-2, 3)]
        vy = [get(1, n * ROW) for n in range(-1, 4)]
        vz = [get(2, n * ROW) for n in range(-1, 4)]
        for p in range(2):
            o = p * ROW
            lam, mu, relax, ane = material(m + p, rows)
            shear = R24 * mu
            twice = 2.0 * shear
            part = (1.0 - relax) * ane
            vx_at, vy_at, vz_at = vx[2 + p], vy[1 + p], vz[1 + p]
            xx = 27.0 * (vx_at - vx[1 + p]) - (vx[3 + p] - vx[p])
            yy = 27.0 * (vy_at - get(1, o - 1)) - (get(1, o + 1) - get(1, o - 2))
            zz = deep[2, x + p, rows, :]
            normal = R24 * lam * (xx + yy + zz)
            xy = 27.0 * ((get(0, o + 1) - vx_at) + (vy[2 + p] - vy_at)) - (
                (get(0, o + 2) - get(0, o - 1)) + (vy[3 + p] - vy[p]))
            xz = 27.0 * (vz[2 + p] - vz_at) - (vz[3 + p] - vz[p]) + deep[0, x + p, rows, :]
            yz = 27.0 * (get(2, o + 1) - vz_at) - (get(2, o + 2) - get(2, o - 1)) + deep[1, x + p, rows, :]
            grown = (
                normal + twice * xx, normal + twice * yy, normal + twice * zz,
                shear * xy, shear * xz, shear * yz,
            )
            for c in range(6):
                old = M[c, x + p, rows, :]
                new = relax * old + part * grown[c]
                stress = Sf[c, pl.ds(pl.multiple_of(at + o, 8), 8), :] + grown[c] - 0.5 * (old + new)
                put(c, x + p, at + o, rows, stress, new)


def finish(dims, S, V, M, deep, lam, mu, rel, ane, plane, vel_out, str_out, mem_out, stress, memory, sem):
    CX, CY = dims
    ROW = CY + 2 * YP
    own = pl.ds(YP, CY)
    middle = pl.ds(2, CX - 4)
    copies = [
        pltpu.make_async_copy(V.at[:, pl.ds(XP, CX), own], vel_out, sem.at[0]),
        pltpu.make_async_copy(S.at[:, pl.ds(XP + 2, CX - 4), own], str_out.at[:, middle], sem.at[1]),
        pltpu.make_async_copy(M.at[:, middle], mem_out.at[:, middle], sem.at[2]),
    ]
    for copy in copies:
        copy.start()
    Sf = S.reshape(6, (CX + 2 * XP) * ROW, 128)
    Vf = V.reshape(3, (CX + 2 * XP) * ROW, 128)

    @pl.loop(0, 2)
    def _(i):
        x = i * (CX - 2)

        def material(m, rows):
            return tuple(ref[m, rows, :] for ref in (lam, mu, rel, ane))

        def put(c, at_x, at, rows, s, m):
            place = at_x - i * (CX - 4)
            stress[c, place, rows, :] = s
            memory[c, place, rows, :] = m

        stress_tiles(x, x, (CY, ROW), range(0, CY, 8), Sf, Vf, M, deep, material, put)

    for c in range(6):
        for n, x in enumerate((0, 1, CX - 2, CX - 1)):
            stress[c, n, 0:1, :] = stress[c, n, 0:1, :] - plane[c * CX + x:c * CX + x + 1, :]
    for n in range(2):
        here, there = pl.ds(2 * n, 2), pl.ds(n * (CX - 2), 2)
        copies.append(pltpu.make_async_copy(stress.at[:, here], str_out.at[:, there], sem.at[3 + 2 * n]))
        copies.append(pltpu.make_async_copy(memory.at[:, here], mem_out.at[:, there], sem.at[4 + 2 * n]))
    for copy in copies[3:]:
        copy.start()
    for copy in copies:
        copy.wait()


def kernel(
    dims,
    vel_hbm, str_hbm, mem_hbm, lam_hbm, mu_hbm, buo_hbm, rel_hbm, ane_hbm, rate_hbm, cell_hbm,
    active_hbm, offset_hbm,
    S, V, M, deep, lam, mu, rel, ane, last_plane,
    buo, rate, cells, active, offset,
    ysend_up, ysend_dn, yrecv_up, yrecv_dn, zsend, zrecv_up, zrecv_dn, band,
    relay_0, relay_1, cand, pair, chosen, gathered, acc, plane,
    fs_sem, fr_sem, ld_sem, xs_sem, xr_sem, ys_sem, yr_sem, zs_sem, zr_sem,
    c_send, c_recv, p_send, p_recv, g_send, g_recv,
):
    NS, ND, NH, CX, CY, SUBF = dims
    ROW = CY + 2 * YP
    NB = NS // NA
    s = lax.axis_index("strike")
    k = lax.axis_index("dip")
    d = lax.axis_index("depth")
    fault = ND // 2
    on_fault = k == fault
    group, parity = lax.div(s, NA), lax.rem(s, NA)
    chunk = k * NH + d

    def near(axis, pos, size, step):
        return {axis: jnp.clip(pos + step, 0, size - 1)}

    s_up, s_dn = near("strike", s, NS, 1), near("strike", s, NS, -1)
    k_up, k_dn = near("dip", k, ND, 1), near("dip", k, ND, -1)
    d_up, d_dn = near("depth", d, NH, 1), near("depth", d, NH, -1)
    has = {
        "s_up": s < NS - 1, "s_dn": s > 0,
        "k_up": k < ND - 1, "k_dn": k > 0,
        "d_up": d < NH - 1, "d_dn": d > 0,
    }

    low_chip = lax.div(d, CORES) == 0
    even = parity == 0
    via = {
        "strike": jnp.where(low_chip, s, jnp.where(even, jnp.minimum(s + 1, NS - 1), jnp.maximum(s - 1, 0))),
        "depth": jnp.where(low_chip, d + CORES, d - CORES),
    }
    from_s = jnp.where(low_chip, jnp.where(even, jnp.minimum(s + 1, NS - 1), jnp.maximum(s - 1, 0)), s)
    from_d = jnp.where(low_chip, d + CORES, d - CORES)
    forwards = from_s < NS - 1
    sender = {"strike": from_s, "depth": from_d}
    onward = {"strike": jnp.minimum(from_s + 1, NS - 1), "depth": from_d}
    came_by = {
        "strike": jnp.maximum(jnp.where(low_chip, s - 1, jnp.where(even, s - 2, s)), 0),
        "depth": jnp.where(low_chip, d + CORES, d - CORES),
    }

    inner = (slice(None), pl.ds(XP, CX), pl.ds(YP, CY))
    loads = [
        pltpu.make_async_copy(str_hbm, S.at[inner], ld_sem.at[0]),
        pltpu.make_async_copy(
            rate_hbm.at[0, :, :, pl.ds(pl.multiple_of(chunk * 128, 128), 128)], rate, ld_sem.at[1]
        ),
        pltpu.make_async_copy(vel_hbm, V.at[inner], ld_sem.at[2]),
        pltpu.make_async_copy(buo_hbm, buo, ld_sem.at[3]),
        pltpu.make_async_copy(mem_hbm, M, ld_sem.at[4]),
        pltpu.make_async_copy(lam_hbm, lam, ld_sem.at[5]),
        pltpu.make_async_copy(mu_hbm, mu, ld_sem.at[6]),
        pltpu.make_async_copy(rel_hbm, rel, ld_sem.at[7]),
        pltpu.make_async_copy(ane_hbm, ane, ld_sem.at[8]),
        pltpu.make_async_copy(cell_hbm, cells, ld_sem.at[9]),
    ]
    order = (
        pltpu.make_async_copy(active_hbm, active, ld_sem.at[10]),
        pltpu.make_async_copy(offset_hbm, offset, ld_sem.at[11]),
    )
    for copy in (loads[1], *order, loads[0], loads[2], loads[3]):
        copy.start()

    barrier = pltpu.get_barrier_semaphore()
    count = jnp.int32(0)
    for name, to in (("s_up", s_up), ("s_dn", s_dn), ("k_up", k_up), ("k_dn", k_dn), ("d_up", d_up), ("d_dn", d_dn)):
        there = has[name]
        count = count + there.astype(jnp.int32)

        @pl.when(there)
        def _(to=to):
            pl.semaphore_signal(barrier, inc=1, device_id=to, device_id_type=MESH)

    count = count + has["s_up"].astype(jnp.int32) + forwards.astype(jnp.int32)

    @pl.when(forwards)
    def _():
        pl.semaphore_signal(barrier, inc=1, device_id=sender, device_id_type=MESH)

    @pl.when(has["s_dn"])
    def _():
        pl.semaphore_signal(barrier, inc=1, device_id=came_by, device_id_type=MESH)

    other = {"strike": group * NA + lax.rem(parity + 1, NA)}
    pl.semaphore_signal(barrier, inc=1, device_id=other, device_id_type=MESH)
    count = count + 1

    @pl.loop(0, NB)
    def _(g):
        @pl.when(g != group)
        def _():
            pl.semaphore_signal(
                barrier, inc=1, device_id={"strike": g * NA + parity}, device_id_type=MESH
            )

    count = count + (NB - 1)

    @pl.loop(0, NH)
    def _(h):
        @pl.when(jnp.logical_not(on_fault & (h == d)))
        def _():
            pl.semaphore_signal(
                barrier, inc=1, device_id={"dip": fault, "depth": h}, device_id_type=MESH
            )

    count = count + NH - on_fault.astype(jnp.int32)

    @pl.when(on_fault)
    def _():
        @pl.loop(0, ND * NH)
        def _(j):
            @pl.when(j != chunk)
            def _():
                pl.semaphore_signal(
                    barrier, inc=1,
                    device_id={"dip": lax.div(j, NH), "depth": lax.rem(j, NH)},
                    device_id_type=MESH,
                )

    count = count + jnp.where(on_fault, ND * NH - 1, 0)
    pl.semaphore_wait(barrier, count)

    relays = (relay_0, relay_1)

    def x_copies(h):
        kind = "sv"[h % 2]
        ref = S if kind == "s" else V
        up, dn, on = [], [], []
        for n, (c0, nc, lu, ld) in enumerate(X_GROUPS[kind]):
            comps = pl.ds(c0, nc)
            rows = pl.ds(YP, CY)
            if h == 0:
                src_up = str_hbm.at[comps, pl.ds(CX - lu, lu)]
                src_dn = str_hbm.at[comps, pl.ds(0, ld)]
            else:
                src_up = ref.at[comps, pl.ds(XP + CX - lu, lu), rows]
                src_dn = ref.at[comps, pl.ds(XP, ld), rows]
            stop = relays[n].at[h, :, pl.ds(0, lu)]
            up.append(pltpu.make_async_remote_copy(
                src_up, stop, xs_sem.at[h, n], fr_sem.at[h, n], device_id=via, device_id_type=MESH))
            on.append(pltpu.make_async_remote_copy(
                stop, ref.at[comps, pl.ds(XP - lu, lu), rows],
                fs_sem.at[h, n], xr_sem.at[h, n], device_id=onward, device_id_type=MESH))
            dn.append(pltpu.make_async_remote_copy(
                src_dn, ref.at[comps, pl.ds(XP + CX, ld), rows],
                xs_sem.at[h, 2 + n], xr_sem.at[h, 2 + n], device_id=s_dn, device_id_type=MESH))
        return up, dn, on

    def each(there, copies, act):
        @pl.when(there)
        def _():
            for copy in copies:
                act(copy)

    def x_start(h):
        up, dn, _ = x_copies(h)
        each(has["s_up"], up, lambda c: c.start())
        each(has["s_dn"], dn, lambda c: c.start())

    def x_forward(h):
        up, _, on = x_copies(h)

        @pl.when(forwards)
        def _():
            for came, goes in zip(up, on):
                came.wait_recv()
                goes.start()

    def x_wait_recv(h):
        _, dn, on = x_copies(h)
        each(has["s_dn"], on, lambda c: c.wait_recv())
        each(has["s_up"], dn, lambda c: c.wait_recv())

    def x_wait_send(h):
        up, dn, on = x_copies(h)
        each(has["s_up"], up, lambda c: c.wait_send())
        each(has["s_dn"], dn, lambda c: c.wait_send())
        each(forwards, on, lambda c: c.wait_send())

    x_start(0)

    Sf = S.reshape(6, (CX + 2 * XP) * ROW, 128)
    Vf = V.reshape(3, (CX + 2 * XP) * ROW, 128)
    flat = {"s": Sf, "v": Vf}

    for F, nc in ((S, 6), (V, 3)):
        zero_x = jnp.zeros((nc, XP, CY, 128), jnp.float32)

        @pl.when(s == 0)
        def _(F=F, zero_x=zero_x):
            F[:, 0:XP, YP:YP + CY, :] = zero_x

        @pl.when(s == NS - 1)
        def _(F=F, zero_x=zero_x):
            F[:, XP + CX:, YP:YP + CY, :] = zero_x

    for there, refs in (
        (has["k_dn"], yrecv_up), (has["k_up"], yrecv_dn), (has["d_dn"], zrecv_up), (has["d_up"], zrecv_dn),
    ):
        @pl.when(jnp.logical_not(there))
        def _(refs=refs):
            for ref in refs:
                ref[...] = jnp.zeros(ref.shape, jnp.float32)

    for refs in (ysend_up, ysend_dn):
        for ref in refs:
            ref[:, ref.shape[1] - 8:, :] = jnp.zeros((4, 8, 128), jnp.float32)

    def y_layers(kind):
        up, dn = [], []
        for c, back in Y_FIELDS[kind]:
            up += [(c, CY - 2), (c, CY - 1)] if back else [(c, CY - 1)]
            dn += [(c, 0)] if back else [(c, 0), (c, 1)]
        return up, dn

    PLANES = (tuple(range(2, CX - 2)), (0, 1, CX - 2, CX - 1))
    SPANS = (((2, CX - 4),), ((0, 2), (CX - 2, 2)))

    def y_copies(h, part):
        size = len(PLANES[part])
        nu, nd = (-(-len(layers) * size // 8) * 8 for layers in y_layers("sv"[h % 2]))
        return (
            pltpu.make_async_remote_copy(
                ysend_up[part].at[h, pl.ds(0, nu)], yrecv_up[part].at[h, pl.ds(0, nu)],
                ys_sem.at[h, part, 0], yr_sem.at[h, part, 0], device_id=k_up, device_id_type=MESH),
            pltpu.make_async_remote_copy(
                ysend_dn[part].at[h, pl.ds(0, nd)], yrecv_dn[part].at[h, pl.ds(0, nd)],
                ys_sem.at[h, part, 1], yr_sem.at[h, part, 1], device_id=k_dn, device_id_type=MESH),
        )

    def z_copies(h, part):
        return (
            pltpu.make_async_remote_copy(
                zsend[part].at[h], zrecv_up[part].at[h],
                zs_sem.at[h, part, 0], zr_sem.at[h, part, 0], device_id=d_up, device_id_type=MESH),
            pltpu.make_async_remote_copy(
                zsend[part].at[h], zrecv_dn[part].at[h],
                zs_sem.at[h, part, 1], zr_sem.at[h, part, 1], device_id=d_dn, device_id_type=MESH),
        )

    lane = lax.broadcasted_iota(jnp.int32, (CY, 128), 1)
    slot = lane >> 2
    quarter = lane & 3

    def turn(value, n):
        return pltpu.roll(value, n % 128, 1)

    def z_slot(part, place, n):
        if part == 0:
            return place // 2, n + 16 * (place % 2)
        return 0, n + 4 * place

    def yz_send(h, part):
        kind = "sv"[h % 2]
        F = flat[kind]
        base = XP * ROW + YP
        for layers, refs in zip(y_layers(kind), (ysend_up, ysend_dn)):
            at = 0
            for c, row in layers:
                for x0, n in SPANS[part]:
                    refs[part][h, at:at + n, :] = F[c, pl.ds(base + x0 * ROW + row, n, stride=ROW), :]
                    at += n
        up, dn = y_copies(h, part)
        each(has["k_up"], [up], lambda c: c.start())
        each(has["k_dn"], [dn], lambda c: c.start())
        arrays = [jnp.zeros((CY, 128), jnp.float32)] * (2 - part)
        for place, comp in enumerate(Z_FIELDS[kind]):
            for n, x in enumerate(PLANES[part]):
                where, index = z_slot(part, place, n)
                value = F[comp, pl.ds((x + XP) * ROW + YP, CY), :]
                arrays[where] = jnp.where(slot == index, turn(value, 4 * index + 2), arrays[where])
        for n, value in enumerate(arrays):
            zsend[part][h, n] = value
        up, dn = z_copies(h, part)
        each(has["d_up"], [up], lambda c: c.start())
        each(has["d_dn"], [dn], lambda c: c.start())

    def yz_recv(h, part):
        kind = "sv"[h % 2]
        F = flat[kind]
        up, dn = y_copies(h, part)
        each(has["k_dn"], [up], lambda c: c.wait_recv())
        each(has["k_up"], [dn], lambda c: c.wait_recv())
        base = XP * ROW + YP
        for layers, refs, shift in zip(y_layers(kind), (yrecv_up, yrecv_dn), (-CY, CY)):
            at = 0
            for c, row in layers:
                for x0, n in SPANS[part]:
                    F[c, pl.ds(base + x0 * ROW + row + shift, n, stride=ROW), :] = refs[part][h, at:at + n, :]
                    at += n
        up, dn = z_copies(h, part)
        each(has["d_dn"], [up], lambda c: c.wait_recv())
        each(has["d_up"], [dn], lambda c: c.wait_recv())
        fixes = {}
        for place, back in enumerate(Z_BACK[kind]):
            ends = (lane == 127) | (lane < 2) if back else (lane > 125) | (lane == 0)
            for n, x in enumerate(PLANES[part]):
                where, index = z_slot(part, place, n)
                if (where, back) not in fixes:
                    mix = jnp.where(quarter < 2, zrecv_up[part][h, where], zrecv_dn[part][h, where])
                    below, two_after = turn(mix, 1), turn(mix, -2)
                    if back:
                        fix = jnp.where(quarter == 0, -two_after, jnp.where(quarter == 1, below - 27.0 * mix, below))
                    else:
                        fix = jnp.where(quarter == 1, 27.0 * turn(mix, -1) - two_after, jnp.where(quarter == 0, -two_after, below))
                    fixes[where, back] = jnp.where(quarter == 3, 0.0, fix)
                moved = turn(fixes[where, back], (127 if back else 126) - 4 * index)
                deep[place, x] = deep[place, x] + jnp.where(ends, moved, 0.0)

    def deep_part(h, part):
        kind = "sv"[h % 2]
        F = S if kind == "s" else V
        for place, (comp, back) in enumerate(zip(Z_FIELDS[kind], Z_BACK[kind])):
            f = jnp.concatenate(
                [F[comp, XP + x0:XP + x0 + n, YP:YP + CY, :].reshape(n * CY, 128) for x0, n in SPANS[part]], axis=0)
            high = f.astype(jnp.bfloat16)
            low = (f - high.astype(jnp.float32)).astype(jnp.bfloat16)
            out = lax.dot_general(
                jnp.concatenate([high, low], axis=1), band[1 if back else 0],
                (((1,), (0,)), ((), ())), preferred_element_type=jnp.float32)
            at = 0
            for x0, n in SPANS[part]:
                deep[place, x0:x0 + n] = out[at:at + n * CY].reshape(n, CY, 128)
                at += n * CY

    def velocity_pair(x, tiles):
        for j in tiles:
            at = (x + XP) * ROW + YP + j

            def get(c, n, Sf=Sf, at=at):
                return Sf[c, pl.ds(at + n, 8), :]

            xx = [get(0, n * ROW) for n in range(-1, 4)]
            xy = [get(3, n * ROW) for n in range(-2, 3)]
            xz = [get(4, n * ROW) for n in range(-2, 3)]
            for p in range(2):
                o = p * ROW
                gain = R24 * buo[x + p, pl.ds(j, 8), :]
                xy_at, yy, yz = xy[2 + p], [get(1, o + n) for n in range(-1, 3)], [get(5, o + n) for n in range(-2, 2)]
                close = (
                    (xx[2 + p] - xx[1 + p]) + (xy_at - get(3, o - 1)),
                    (xy_at - xy[1 + p]) + (yy[2] - yy[1]),
                    (xz[2 + p] - xz[1 + p]) + (yz[2] - yz[1]),
                )
                far = (
                    (xx[3 + p] - xx[p]) + (get(3, o + 1) - get(3, o - 2)),
                    (xy[3 + p] - xy[p]) + (yy[3] - yy[0]),
                    (xz[3 + p] - xz[p]) + (yz[3] - yz[0]),
                )
                for c in range(3):
                    own = pl.ds(pl.multiple_of(at + o, 8), 8)
                    Vf[c, own, :] = Vf[c, own, :] + gain * (
                        27.0 * close[c] - far[c] + deep[c, x + p, pl.ds(j, 8), :])

    def stress_pair(x, tiles):
        def material(x, rows):
            return lam[x, rows, :], mu[x, rows, :], rel[x, rows, :], ane[x, rows, :]

        def put(c, x, at, rows, stress, memory):
            Sf[c, pl.ds(pl.multiple_of(at, 8), 8), :] = stress
            M[c, x, rows, :] = memory

        stress_tiles(x, x, (CY, ROW), tiles, Sf, Vf, M, deep, material, put)

    def interior(one):
        @pl.loop(0, (CX - 4) // 2)
        def _(i):
            one(2 * i + 2, range(0, CY, 8))

    def boundary(one):
        @pl.loop(0, 2)
        def _(i):
            one(i * (CX - 2), range(0, CY, 8))

    def candidates():
        row = lax.broadcasted_iota(jnp.int32, (TB, 128), 0)
        weights = jnp.where((row == 0) | (row == TB - 1), 0.5 / (TB - 1), 1.0 / (TB - 1))
        for t in range(STEPS):
            o = offset[t]
            for c in range(6):
                samples = rate[c, pl.ds(o, TB), :]
                cand[group, t, c:c + 1, :] = jnp.sum(samples * weights, axis=0, keepdims=True)
            cand[group, t, 6:8, :] = jnp.zeros((2, 128), jnp.float32)

    def c_copy(sender, receiver):
        return pltpu.make_async_remote_copy(
            cand.at[sender], cand.at[sender], c_send.at[receiver], c_recv.at[sender],
            device_id={"strike": receiver * NA + parity}, device_id_type=MESH)

    def over_groups(act):
        @pl.loop(0, NB)
        def _(g):
            @pl.when(g != group)
            def _():
                act(g)

    def pair_copy(which):
        return pltpu.make_async_remote_copy(
            pair.at[which], pair.at[which], p_send, p_recv, device_id=other, device_id_type=MESH)

    def g_copy(which, h):
        return pltpu.make_async_remote_copy(
            chosen, gathered.at[which], g_send.at[h], g_recv.at[which],
            device_id={"dip": fault, "depth": h}, device_id_type=MESH)

    def over_fault(act):
        @pl.loop(0, NH)
        def _(h):
            @pl.when(jnp.logical_not(on_fault & (h == d)))
            def _():
                act(h)

    def source_first():
        loads[1].wait()
        for copy in order:
            copy.wait()
        candidates()
        over_groups(lambda g: c_copy(group, g).start())

    def source_second():
        over_groups(lambda g: c_copy(g, group).wait_recv())
        for t in range(STEPS):
            pair[parity, t] = cand[lax.div(active[t], NA), t]
        pair_copy(parity).start()

    def source_third():
        pair_copy(lax.rem(parity + 1, NA)).wait_recv()
        for t in range(STEPS):
            value = pair[lax.rem(active[t], NA), t]
            chosen[t] = value

            @pl.when(on_fault)
            def _(t=t, value=value):
                gathered[chunk, t] = value

        over_fault(lambda h: g_copy(chunk, h).start())

    def source_gather():
        @pl.when(on_fault)
        def _():
            @pl.loop(0, ND * NH)
            def _(j):
                @pl.when(j != chunk)
                def _():
                    g_copy(j, 0).wait_recv()

    def source_plane(t):
        @pl.when(on_fault)
        def _():
            seg = active[t]
            depth_total = 128 * NH
            acc[...] = jnp.zeros_like(acc)
            wide = 8 * 128

            @pl.loop(0, SUBF // wide)
            def _(i):
                cell = cells[pl.ds(seg, 1), pl.ds(pl.multiple_of(i * wide, wide), wide)]
                cell_x = lax.div(cell, depth_total)
                cell_z = cell - cell_x * depth_total - d * 128
                cell_x = cell_x - s * CX
                hot_z = (lax.broadcasted_iota(jnp.int32, (128, wide), 0) == cell_z).astype(jnp.float32).astype(jnp.bfloat16)
                hot_x = lax.broadcasted_iota(jnp.int32, (CX, wide), 0) == cell_x
                value = jnp.concatenate([gathered[8 * i + n, t] for n in range(8)], axis=1)
                parts = []
                for _ in range(3):
                    part = value.astype(jnp.bfloat16).astype(jnp.float32)
                    parts.append(part)
                    value = value - part
                rows = [
                    jnp.where(hot_x, part[c:c + 1, :], 0.0).astype(jnp.bfloat16)
                    for part in parts for c in range(6)
                ]
                acc[...] += lax.dot_general(
                    jnp.concatenate(rows, axis=0), hot_z, (((1,), (1,)), ((), ())),
                    preferred_element_type=jnp.float32)

            n = 6 * CX
            (plane if t == 0 else last_plane)[...] = acc[0:n] + acc[n:2 * n] + acc[2 * n:3 * n]

    def apply_source(ref, spans):
        @pl.when(on_fault)
        def _():
            for c in range(6):
                for x0, n in spans:
                    at = pl.ds((x0 + XP) * ROW + YP, n, stride=ROW)
                    Sf[c, at, :] = Sf[c, at, :] - ref[c * CX + x0:c * CX + x0 + n, :]

    edges = ((0, 2), (CX - 2, 2))
    middle = ((2, CX - 4),)

    i, j = (lax.broadcasted_iota(jnp.int32, (256, 128), n) for n in range(2))
    off = (i & 127) - j
    for n, (a, b) in enumerate(((1, 0), (0, -1))):
        weight = jnp.where(off == a, 27.0, jnp.where(off == b, -27.0, jnp.where(
            off == a + 1, -1.0, jnp.where(off == b - 1, 1.0, 0.0))))
        band[n] = weight.astype(jnp.bfloat16)

    @pl.when(jnp.logical_not(on_fault))
    def _():
        last_plane[...] = jnp.zeros_like(last_plane)

    source_first()
    loads[0].wait()
    for copy in loads[4:]:
        copy.start()
    yz_send(0, 0)
    yz_send(0, 1)
    deep_part(0, 0)
    deep_part(0, 1)
    x_forward(0)
    loads[2].wait()
    loads[3].wait()
    yz_recv(0, 0)
    source_second()
    interior(velocity_pair)
    yz_send(1, 0)
    source_third()
    deep_part(1, 0)
    yz_recv(0, 1)
    x_wait_recv(0)
    boundary(velocity_pair)
    x_start(1)
    yz_send(1, 1)
    for copy in loads[4:]:
        copy.wait()
    yz_recv(1, 0)
    interior(stress_pair)
    x_forward(1)
    source_gather()
    source_plane(0)
    apply_source(plane, middle)
    yz_send(2, 0)
    deep_part(1, 1)
    deep_part(2, 0)
    x_wait_send(0)
    yz_recv(1, 1)
    x_wait_recv(1)
    boundary(stress_pair)
    apply_source(plane, edges)
    x_start(2)
    yz_send(2, 1)
    yz_recv(2, 0)
    interior(velocity_pair)
    x_forward(2)
    yz_send(3, 0)
    deep_part(2, 1)
    deep_part(3, 0)
    source_plane(1)
    x_wait_send(1)
    yz_recv(2, 1)
    x_wait_recv(2)
    boundary(velocity_pair)
    x_start(3)
    yz_send(3, 1)
    yz_recv(3, 0)
    interior(stress_pair)
    x_forward(3)
    apply_source(last_plane, middle)
    deep_part(3, 1)
    yz_recv(3, 1)
    x_wait_recv(3)

    x_wait_send(2)
    x_wait_send(3)
    for h in range(4):
        for part in range(2):
            for there, pair_of in (("k", y_copies(h, part)), ("d", z_copies(h, part))):
                each(has[there + "_up"], [pair_of[0]], lambda c: c.wait_send())
                each(has[there + "_dn"], [pair_of[1]], lambda c: c.wait_send())
    over_groups(lambda g: c_copy(group, g).wait_send())
    pair_copy(parity).wait_send()
    over_fault(lambda h: g_copy(chunk, h).wait_send())


def solution(mesh):
    ns, nd, nh = (mesh.shape[a] for a in ("strike", "dip", "depth"))

    def body(velocity, stress, memory, lam, mu, buo, rel, ane, rate, cell, active, offset):
        cx, cy, cz = lam.shape
        subf = cell.shape[1]
        assert cz == 128 and subf == 128 * nd * nh
        planes, rows = cx + 2 * XP, cy + 2 * YP
        f32 = jnp.float32
        block = pltpu.VMEM((cx, cy, cz), f32)
        dma = pltpu.SemaphoreType.DMA
        hbm = pl.BlockSpec(memory_space=pltpu.HBM)
        vmem = pl.BlockSpec(memory_space=pltpu.VMEM)
        between = (
            pltpu.VMEM((6, planes, rows, cz), f32),
            pltpu.VMEM((3, planes, rows, cz), f32),
            pltpu.VMEM((6, cx, cy, cz), f32),
            pltpu.VMEM((3, cx, cy, cz), f32),
            block, block, block, block,
            pltpu.VMEM((6 * cx, cz), f32),
        )
        held = pl.pallas_call(
            functools.partial(kernel, (ns, nd, nh, cx, cy, subf)),
            out_shape=between,
            in_specs=[hbm] * 12,
            out_specs=(vmem,) * 9,
            scratch_shapes=[
                block,
                pltpu.VMEM((6, rate.shape[1], 128), f32),
                pltpu.VMEM(cell.shape, jnp.int32),
                pltpu.SMEM(active.shape, jnp.int32),
                pltpu.SMEM(offset.shape, jnp.int32),
                *[(pltpu.VMEM((4, 64, cz), f32), pltpu.VMEM((4, 24, cz), f32))] * 4,
                *[(pltpu.VMEM((4, 2, cy, cz), f32), pltpu.VMEM((4, 1, cy, cz), f32))] * 3,
                pltpu.VMEM((2, 2 * cz, cz), jnp.bfloat16),
                pltpu.VMEM((4, 1, 2, cy, cz), f32),
                pltpu.VMEM((4, 2, 2, cy, cz), f32),
                pltpu.VMEM((ns // NA, STEPS, 8, 128), f32),
                pltpu.VMEM((NA, STEPS, 8, 128), f32),
                pltpu.VMEM((STEPS, 8, 128), f32),
                pltpu.VMEM((nd * nh, STEPS, 8, 128), f32),
                pltpu.VMEM((3 * 6 * cx, cz), f32),
                pltpu.VMEM((6 * cx, cz), f32),
                dma((4, 2)), dma((4, 2)), dma((12,)), dma((4, 4)), dma((4, 4)), dma((4, 2, 2)), dma((4, 2, 2)), dma((4, 2, 2)), dma((4, 2, 2)),
                dma((ns // NA,)), dma((ns // NA,)), dma, dma, dma((nh,)), dma((nd * nh,)),
            ],
            compiler_params=pltpu.CompilerParams(
                collective_id=0, has_side_effects=True, vmem_limit_bytes=40 * 1024 * 1024
            ),
            cost_estimate=pl.CostEstimate(flops=30_000_000, bytes_accessed=6_000_000, transcendentals=0),
        )(*(
            pltpu.with_memory_space_constraint(a, pltpu.HBM)
            for a in (velocity, stress, memory, lam, mu, buo, rel, ane, jnp.transpose(rate, (0, 2, 1, 3)), cell, active, offset)
        ))
        return pl.pallas_call(
            functools.partial(finish, (cx, cy)),
            out_shape=tuple(jax.ShapeDtypeStruct(a.shape, f32) for a in (velocity, stress, memory)),
            in_specs=[vmem] * 9,
            out_specs=(hbm,) * 3,
            scratch_shapes=[
                pltpu.VMEM((6, 4, cy, cz), f32),
                pltpu.VMEM((6, 4, cy, cz), f32),
                dma((7,)),
            ],
            compiler_params=pltpu.CompilerParams(vmem_limit_bytes=40 * 1024 * 1024),
            cost_estimate=pl.CostEstimate(flops=2_000_000, bytes_accessed=4_000_000, transcendentals=0),
        )(*held)

    field = P(None, "strike", "dip", "depth")
    cellwise = P("strike", "dip", "depth")
    return jax.shard_map(
        body,
        mesh=mesh,
        in_specs=(field,) * 3 + (cellwise,) * 5 + (P("strike", None, None, None), P(), P(), P()),
        out_specs=(field,) * 3,
        check_vma=False,
    )
```

```python
import functools

import jax
import jax.numpy as jnp
from jax import lax
from jax.experimental import pallas as pl
from jax.experimental.pallas import tpu as pltpu
from jax.sharding import PartitionSpec as P

MESH = pl.DeviceIdType.MESH
TB = 8
STEPS = 2
R24 = 0.12 / 24.0
XP = 2
YP = 8
NA = 2

X_GROUPS = {"s": ((0, 1, 1, 2), (3, 2, 2, 1)), "v": ((0, 1, 2, 1), (1, 2, 1, 2))}
Y_FIELDS = {"s": ((3, True), (5, True), (1, False)), "v": ((1, True), (0, False), (2, False))}
Z_FIELDS = {"s": (4, 5, 2), "v": (0, 1, 2)}
Z_BACK = {"s": (True, True, False), "v": (False, False, True)}


def stress_tiles(x, m, sizes, tiles, Sf, Vf, M, deep, material, put):
    CY, ROW = sizes
    for j in tiles:
        at = (x + XP) * ROW + YP + j
        rows = pl.ds(j, 8)

        def get(c, n, at=at):
            return Vf[c, pl.ds(at + n, 8), :]

        vx = [get(0, n * ROW) for n in range(-2, 3)]
        vy = [get(1, n * ROW) for n in range(-1, 4)]
        vz = [get(2, n * ROW) for n in range(-1, 4)]
        for p in range(2):
            o = p * ROW
            lam, mu, relax, ane = material(m + p, rows)
            shear = R24 * mu
            twice = 2.0 * shear
            part = (1.0 - relax) * ane
            vx_at, vy_at, vz_at = vx[2 + p], vy[1 + p], vz[1 + p]
            xx = 27.0 * (vx_at - vx[1 + p]) - (vx[3 + p] - vx[p])
            yy = 27.0 * (vy_at - get(1, o - 1)) - (get(1, o + 1) - get(1, o - 2))
            zz = deep[2, x + p, rows, :]
            normal = R24 * lam * (xx + yy + zz)
            xy = 27.0 * ((get(0, o + 1) - vx_at) + (vy[2 + p] - vy_at)) - (
                (get(0, o + 2) - get(0, o - 1)) + (vy[3 + p] - vy[p]))
            xz = 27.0 * (vz[2 + p] - vz_at) - (vz[3 + p] - vz[p]) + deep[0, x + p, rows, :]
            yz = 27.0 * (get(2, o + 1) - vz_at) - (get(2, o + 2) - get(2, o - 1)) + deep[1, x + p, rows, :]
            grown = (
                normal + twice * xx, normal + twice * yy, normal + twice * zz,
                shear * xy, shear * xz, shear * yz,
            )
            for c in range(6):
                old = M[c, x + p, rows, :]
                new = relax * old + part * grown[c]
                stress = Sf[c, pl.ds(pl.multiple_of(at + o, 8), 8), :] + grown[c] - 0.5 * (old + new)
                put(c, x + p, at + o, rows, stress, new)


def finish(dims, S, V, M, deep, lam, mu, rel, ane, plane, vel_out, str_out, mem_out, stress, memory, sem):
    CX, CY = dims
    ROW = CY + 2 * YP
    own = pl.ds(YP, CY)
    middle = pl.ds(2, CX - 4)
    copies = [
        pltpu.make_async_copy(V.at[:, pl.ds(XP, CX), own], vel_out, sem.at[0]),
        pltpu.make_async_copy(S.at[:, pl.ds(XP + 2, CX - 4), own], str_out.at[:, middle], sem.at[1]),
        pltpu.make_async_copy(M.at[:, middle], mem_out.at[:, middle], sem.at[2]),
    ]
    for copy in copies:
        copy.start()
    Sf = S.reshape(6, (CX + 2 * XP) * ROW, 128)
    Vf = V.reshape(3, (CX + 2 * XP) * ROW, 128)

    @pl.loop(0, 2)
    def _(i):
        x = i * (CX - 2)

        def material(m, rows):
            return tuple(ref[m, rows, :] for ref in (lam, mu, rel, ane))

        def put(c, at_x, at, rows, s, m):
            place = at_x - i * (CX - 4)
            stress[c, place, rows, :] = s
            memory[c, place, rows, :] = m

        stress_tiles(x, x, (CY, ROW), range(0, CY, 8), Sf, Vf, M, deep, material, put)

    for c in range(6):
        for n, x in enumerate((0, 1, CX - 2, CX - 1)):
            stress[c, n, 0:1, :] = stress[c, n, 0:1, :] - plane[c * CX + x:c * CX + x + 1, :]
    for n in range(2):
        here, there = pl.ds(2 * n, 2), pl.ds(n * (CX - 2), 2)
        copies.append(pltpu.make_async_copy(stress.at[:, here], str_out.at[:, there], sem.at[3 + 2 * n]))
        copies.append(pltpu.make_async_copy(memory.at[:, here], mem_out.at[:, there], sem.at[4 + 2 * n]))
    for copy in copies[3:]:
        copy.start()
    for copy in copies:
        copy.wait()


def kernel(
    dims,
    vel_hbm, str_hbm, mem_hbm, lam_hbm, mu_hbm, buo_hbm, rel_hbm, ane_hbm, rate_hbm, cell_hbm,
    active_hbm, offset_hbm,
    S, V, M, deep, lam, mu, rel, ane, last_plane,
    buo, rate, cells, active, offset,
    ysend_up, ysend_dn, yrecv_up, yrecv_dn, zsend, zrecv_up, zrecv_dn, band,
    cand, pair, chosen, gathered, plane,
    ld_sem, xs_sem, xr_sem, ys_sem, yr_sem, zs_sem, zr_sem,
    c_send, c_recv, p_send, p_recv, g_send, g_recv,
):
    NS, ND, NH, CX, CY, SUBF = dims
    ROW = CY + 2 * YP
    NB = NS // NA
    s = lax.axis_index("strike")
    k = lax.axis_index("dip")
    d = lax.axis_index("depth")
    fault = ND // 2
    on_fault = k == fault
    group, parity = lax.div(s, NA), lax.rem(s, NA)
    chunk = k * NH + d

    def near(axis, pos, size, step):
        return {axis: jnp.clip(pos + step, 0, size - 1)}

    s_up, s_dn = near("strike", s, NS, 1), near("strike", s, NS, -1)
    k_up, k_dn = near("dip", k, ND, 1), near("dip", k, ND, -1)
    d_up, d_dn = near("depth", d, NH, 1), near("depth", d, NH, -1)
    has = {
        "s_up": s < NS - 1, "s_dn": s > 0,
        "k_up": k < ND - 1, "k_dn": k > 0,
        "d_up": d < NH - 1, "d_dn": d > 0,
    }

    barrier = pltpu.get_barrier_semaphore()
    count = jnp.int32(0)
    for name, to in (("s_up", s_up), ("s_dn", s_dn), ("k_up", k_up), ("k_dn", k_dn), ("d_up", d_up), ("d_dn", d_dn)):
        there = has[name]
        count = count + there.astype(jnp.int32)

        @pl.when(there)
        def _(to=to):
            pl.semaphore_signal(barrier, inc=1, device_id=to, device_id_type=MESH)

    other = {"strike": group * NA + lax.rem(parity + 1, NA)}
    pl.semaphore_signal(barrier, inc=1, device_id=other, device_id_type=MESH)
    count = count + 1

    @pl.loop(0, NB)
    def _(g):
        @pl.when(g != group)
        def _():
            pl.semaphore_signal(
                barrier, inc=1, device_id={"strike": g * NA + parity}, device_id_type=MESH
            )

    count = count + (NB - 1)

    @pl.loop(0, NH)
    def _(h):
        @pl.when(jnp.logical_not(on_fault & (h == d)))
        def _():
            pl.semaphore_signal(
                barrier, inc=1, device_id={"dip": fault, "depth": h}, device_id_type=MESH
            )

    count = count + NH - on_fault.astype(jnp.int32)

    @pl.when(on_fault)
    def _():
        @pl.loop(0, ND * NH)
        def _(j):
            @pl.when(j != chunk)
            def _():
                pl.semaphore_signal(
                    barrier, inc=1,
                    device_id={"dip": lax.div(j, NH), "depth": lax.rem(j, NH)},
                    device_id_type=MESH,
                )

    count = count + jnp.where(on_fault, ND * NH - 1, 0)
    inner = (slice(None), pl.ds(XP, CX), pl.ds(YP, CY))
    loads = [
        pltpu.make_async_copy(str_hbm, S.at[inner], ld_sem.at[0]),
        pltpu.make_async_copy(
            rate_hbm.at[0, :, :, pl.ds(pl.multiple_of(chunk * 128, 128), 128)], rate, ld_sem.at[1]
        ),
        pltpu.make_async_copy(vel_hbm, V.at[inner], ld_sem.at[2]),
        pltpu.make_async_copy(buo_hbm, buo, ld_sem.at[3]),
        pltpu.make_async_copy(mem_hbm, M, ld_sem.at[4]),
        pltpu.make_async_copy(lam_hbm, lam, ld_sem.at[5]),
        pltpu.make_async_copy(mu_hbm, mu, ld_sem.at[6]),
        pltpu.make_async_copy(rel_hbm, rel, ld_sem.at[7]),
        pltpu.make_async_copy(ane_hbm, ane, ld_sem.at[8]),
        pltpu.make_async_copy(cell_hbm, cells, ld_sem.at[9]),
    ]
    order = (
        pltpu.make_async_copy(active_hbm, active, ld_sem.at[10]),
        pltpu.make_async_copy(offset_hbm, offset, ld_sem.at[11]),
    )
    for copy in (loads[1], *order, loads[0], loads[2], loads[3]):
        copy.start()

    pl.semaphore_wait(barrier, count)

    def x_copies(h):
        kind = "sv"[h % 2]
        ref = S if kind == "s" else V
        up, dn = [], []
        for n, (c0, nc, lu, ld) in enumerate(X_GROUPS[kind]):
            comps = pl.ds(c0, nc)
            rows = pl.ds(YP, CY)
            if h == 0:
                src_up = str_hbm.at[comps, pl.ds(CX - lu, lu)]
                src_dn = str_hbm.at[comps, pl.ds(0, ld)]
            else:
                src_up = ref.at[comps, pl.ds(XP + CX - lu, lu), rows]
                src_dn = ref.at[comps, pl.ds(XP, ld), rows]
            up.append(pltpu.make_async_remote_copy(
                src_up, ref.at[comps, pl.ds(XP - lu, lu), rows],
                xs_sem.at[h, n], xr_sem.at[h, n], device_id=s_up, device_id_type=MESH))
            dn.append(pltpu.make_async_remote_copy(
                src_dn, ref.at[comps, pl.ds(XP + CX, ld), rows],
                xs_sem.at[h, 2 + n], xr_sem.at[h, 2 + n], device_id=s_dn, device_id_type=MESH))
        return up, dn

    def each(there, copies, act):
        @pl.when(there)
        def _():
            for copy in copies:
                act(copy)

    def x_start(h, side):
        there = has["s_up"] if side == 0 else has["s_dn"]
        each(there, x_copies(h)[side], lambda c: c.start())

    def x_wait_recv(h, side):
        there = has["s_dn"] if side == 0 else has["s_up"]
        each(there, x_copies(h)[side], lambda c: c.wait_recv())

    def x_wait_send(h):
        up, dn = x_copies(h)
        each(has["s_up"], up, lambda c: c.wait_send())
        each(has["s_dn"], dn, lambda c: c.wait_send())

    x_start(0, 0)
    x_start(0, 1)

    Sf = S.reshape(6, (CX + 2 * XP) * ROW, 128)
    Vf = V.reshape(3, (CX + 2 * XP) * ROW, 128)
    flat = {"s": Sf, "v": Vf}

    for F, nc in ((S, 6), (V, 3)):
        zero_x = jnp.zeros((nc, XP, CY, 128), jnp.float32)

        @pl.when(s == 0)
        def _(F=F, zero_x=zero_x):
            F[:, 0:XP, YP:YP + CY, :] = zero_x

        @pl.when(s == NS - 1)
        def _(F=F, zero_x=zero_x):
            F[:, XP + CX:, YP:YP + CY, :] = zero_x

    for there, refs in (
        (has["k_dn"], yrecv_up), (has["k_up"], yrecv_dn), (has["d_dn"], zrecv_up), (has["d_up"], zrecv_dn),
    ):
        @pl.when(jnp.logical_not(there))
        def _(refs=refs):
            for ref in refs:
                ref[...] = jnp.zeros(ref.shape, jnp.float32)

    for refs in (ysend_up, ysend_dn):
        for ref in refs:
            ref[:, ref.shape[1] - 8:, :] = jnp.zeros((4, 8, 128), jnp.float32)

    def y_layers(kind):
        up, dn = [], []
        for c, back in Y_FIELDS[kind]:
            up += [(c, CY - 2), (c, CY - 1)] if back else [(c, CY - 1)]
            dn += [(c, 0)] if back else [(c, 0), (c, 1)]
        return up, dn

    PLANES = (tuple(range(2, CX - 2)), (0, 1, CX - 2, CX - 1))
    SPANS = (((2, CX - 4),), ((0, 2), (CX - 2, 2)))

    def y_copies(h, part):
        size = len(PLANES[part])
        nu, nd = (-(-len(layers) * size // 8) * 8 for layers in y_layers("sv"[h % 2]))
        return (
            pltpu.make_async_remote_copy(
                ysend_up[part].at[h, pl.ds(0, nu)], yrecv_up[part].at[h, pl.ds(0, nu)],
                ys_sem.at[h, part, 0], yr_sem.at[h, part, 0], device_id=k_up, device_id_type=MESH),
            pltpu.make_async_remote_copy(
                ysend_dn[part].at[h, pl.ds(0, nd)], yrecv_dn[part].at[h, pl.ds(0, nd)],
                ys_sem.at[h, part, 1], yr_sem.at[h, part, 1], device_id=k_dn, device_id_type=MESH),
        )

    def z_copies(h, part):
        return (
            pltpu.make_async_remote_copy(
                zsend[part].at[h], zrecv_up[part].at[h],
                zs_sem.at[h, part, 0], zr_sem.at[h, part, 0], device_id=d_up, device_id_type=MESH),
            pltpu.make_async_remote_copy(
                zsend[part].at[h], zrecv_dn[part].at[h],
                zs_sem.at[h, part, 1], zr_sem.at[h, part, 1], device_id=d_dn, device_id_type=MESH),
        )

    lane = lax.broadcasted_iota(jnp.int32, (CY, 128), 1)
    slot = lane >> 2
    quarter = lane & 3

    def turn(value, n):
        return pltpu.roll(value, n % 128, 1)

    def z_slot(part, place, n):
        if part == 0:
            return place // 2, n + 16 * (place % 2)
        return 0, n + 4 * place

    def yz_send(h, part):
        kind = "sv"[h % 2]
        F = flat[kind]
        base = XP * ROW + YP
        for layers, refs in zip(y_layers(kind), (ysend_up, ysend_dn)):
            at = 0
            for c, row in layers:
                for x0, n in SPANS[part]:
                    refs[part][h, at:at + n, :] = F[c, pl.ds(base + x0 * ROW + row, n, stride=ROW), :]
                    at += n
        up, dn = y_copies(h, part)
        each(has["k_up"], [up], lambda c: c.start())
        each(has["k_dn"], [dn], lambda c: c.start())
        arrays = [jnp.zeros((CY, 128), jnp.float32)] * (2 - part)
        for place, comp in enumerate(Z_FIELDS[kind]):
            for n, x in enumerate(PLANES[part]):
                where, index = z_slot(part, place, n)
                value = F[comp, pl.ds((x + XP) * ROW + YP, CY), :]
                arrays[where] = jnp.where(slot == index, turn(value, 4 * index + 2), arrays[where])
        for n, value in enumerate(arrays):
            zsend[part][h, n] = value
        up, dn = z_copies(h, part)
        each(has["d_up"], [up], lambda c: c.start())
        each(has["d_dn"], [dn], lambda c: c.start())

    def yz_recv(h, part):
        kind = "sv"[h % 2]
        F = flat[kind]
        up, dn = y_copies(h, part)
        each(has["k_dn"], [up], lambda c: c.wait_recv())
        each(has["k_up"], [dn], lambda c: c.wait_recv())
        base = XP * ROW + YP
        for layers, refs, shift in zip(y_layers(kind), (yrecv_up, yrecv_dn), (-CY, CY)):
            at = 0
            for c, row in layers:
                for x0, n in SPANS[part]:
                    F[c, pl.ds(base + x0 * ROW + row + shift, n, stride=ROW), :] = refs[part][h, at:at + n, :]
                    at += n
        up, dn = z_copies(h, part)
        each(has["d_dn"], [up], lambda c: c.wait_recv())
        each(has["d_up"], [dn], lambda c: c.wait_recv())
        fixes = {}
        for place, back in enumerate(Z_BACK[kind]):
            ends = (lane == 127) | (lane < 2) if back else (lane > 125) | (lane == 0)
            for n, x in enumerate(PLANES[part]):
                where, index = z_slot(part, place, n)
                if (where, back) not in fixes:
                    mix = jnp.where(quarter < 2, zrecv_up[part][h, where], zrecv_dn[part][h, where])
                    below, two_after = turn(mix, 1), turn(mix, -2)
                    if back:
                        fix = jnp.where(quarter == 0, -two_after, jnp.where(quarter == 1, below - 27.0 * mix, below))
                    else:
                        fix = jnp.where(quarter == 1, 27.0 * turn(mix, -1) - two_after, jnp.where(quarter == 0, -two_after, below))
                    fixes[where, back] = jnp.where(quarter == 3, 0.0, fix)
                moved = turn(fixes[where, back], (127 if back else 126) - 4 * index)
                deep[place, x] = deep[place, x] + jnp.where(ends, moved, 0.0)

    def deep_part(h, part):
        kind = "sv"[h % 2]
        F = S if kind == "s" else V
        for place, (comp, back) in enumerate(zip(Z_FIELDS[kind], Z_BACK[kind])):
            f = jnp.concatenate(
                [F[comp, XP + x0:XP + x0 + n, YP:YP + CY, :].reshape(n * CY, 128) for x0, n in SPANS[part]], axis=0)
            high = f.astype(jnp.bfloat16)
            low = (f - high.astype(jnp.float32)).astype(jnp.bfloat16)
            out = lax.dot_general(
                jnp.concatenate([high, low], axis=1), band[1 if back else 0],
                (((1,), (0,)), ((), ())), preferred_element_type=jnp.float32)
            at = 0
            for x0, n in SPANS[part]:
                deep[place, x0:x0 + n] = out[at:at + n * CY].reshape(n, CY, 128)
                at += n * CY

    def velocity_pair(x, tiles):
        for j in tiles:
            at = (x + XP) * ROW + YP + j

            def get(c, n, Sf=Sf, at=at):
                return Sf[c, pl.ds(at + n, 8), :]

            xx = [get(0, n * ROW) for n in range(-1, 4)]
            xy = [get(3, n * ROW) for n in range(-2, 3)]
            xz = [get(4, n * ROW) for n in range(-2, 3)]
            for p in range(2):
                o = p * ROW
                gain = R24 * buo[x + p, pl.ds(j, 8), :]
                xy_at, yy, yz = xy[2 + p], [get(1, o + n) for n in range(-1, 3)], [get(5, o + n) for n in range(-2, 2)]
                close = (
                    (xx[2 + p] - xx[1 + p]) + (xy_at - get(3, o - 1)),
                    (xy_at - xy[1 + p]) + (yy[2] - yy[1]),
                    (xz[2 + p] - xz[1 + p]) + (yz[2] - yz[1]),
                )
                far = (
                    (xx[3 + p] - xx[p]) + (get(3, o + 1) - get(3, o - 2)),
                    (xy[3 + p] - xy[p]) + (yy[3] - yy[0]),
                    (xz[3 + p] - xz[p]) + (yz[3] - yz[0]),
                )
                for c in range(3):
                    own = pl.ds(pl.multiple_of(at + o, 8), 8)
                    Vf[c, own, :] = Vf[c, own, :] + gain * (
                        27.0 * close[c] - far[c] + deep[c, x + p, pl.ds(j, 8), :])

    def stress_pair(x, tiles):
        def material(x, rows):
            return lam[x, rows, :], mu[x, rows, :], rel[x, rows, :], ane[x, rows, :]

        def put(c, x, at, rows, stress, memory):
            Sf[c, pl.ds(pl.multiple_of(at, 8), 8), :] = stress
            M[c, x, rows, :] = memory

        stress_tiles(x, x, (CY, ROW), tiles, Sf, Vf, M, deep, material, put)

    def interior(one):
        @pl.loop(0, (CX - 4) // 2)
        def _(i):
            one(2 * i + 2, range(0, CY, 8))

    nought = jnp.minimum(s, 0)

    def edges(h, one, source=None):
        for side, x in ((0, 0), (1, CX - 2)):
            x_wait_recv(h, side)
            one(nought + x, range(0, CY, 8))
            if source is not None:
                apply_source(source, ((x, 2),))
            x_start(h + 1, 1 - side)

    def candidates():
        row = lax.broadcasted_iota(jnp.int32, (TB, 128), 0)
        weights = jnp.where((row == 0) | (row == TB - 1), 0.5 / (TB - 1), 1.0 / (TB - 1))
        for t in range(STEPS):
            o = offset[t]
            for c in range(6):
                samples = rate[c, pl.ds(o, TB), :]
                cand[group, t, c:c + 1, :] = jnp.sum(samples * weights, axis=0, keepdims=True)
            cand[group, t, 6:8, :] = jnp.zeros((2, 128), jnp.float32)

    def c_copy(sender, receiver):
        return pltpu.make_async_remote_copy(
            cand.at[sender], cand.at[sender], c_send.at[receiver], c_recv.at[sender],
            device_id={"strike": receiver * NA + parity}, device_id_type=MESH)

    def over_groups(act):
        @pl.loop(0, NB)
        def _(g):
            @pl.when(g != group)
            def _():
                act(g)

    def pair_copy(which):
        return pltpu.make_async_remote_copy(
            pair.at[which], pair.at[which], p_send, p_recv, device_id=other, device_id_type=MESH)

    def g_copy(which, h):
        return pltpu.make_async_remote_copy(
            chosen, gathered.at[which], g_send.at[h], g_recv.at[which],
            device_id={"dip": fault, "depth": h}, device_id_type=MESH)

    def over_fault(act):
        @pl.loop(0, NH)
        def _(h):
            @pl.when(jnp.logical_not(on_fault & (h == d)))
            def _():
                act(h)

    def source_first():
        loads[1].wait()
        for copy in order:
            copy.wait()
        candidates()
        over_groups(lambda g: c_copy(group, g).start())

    def source_second():
        over_groups(lambda g: c_copy(g, group).wait_recv())
        for t in range(STEPS):
            pair[parity, t] = cand[lax.div(active[t], NA), t]
        pair_copy(parity).start()

    def source_third():
        pair_copy(lax.rem(parity + 1, NA)).wait_recv()
        for t in range(STEPS):
            value = pair[lax.rem(active[t], NA), t]
            chosen[t] = value

            @pl.when(on_fault)
            def _(t=t, value=value):
                gathered[chunk, t] = value

        over_fault(lambda h: g_copy(chunk, h).start())

    def source_gather():
        @pl.when(on_fault)
        def _():
            @pl.loop(0, ND * NH)
            def _(j):
                @pl.when(j != chunk)
                def _():
                    g_copy(j, 0).wait_recv()

    def source_plane(t, piece):
        @pl.when(on_fault)
        def _():
            seg = active[t]
            depth_total = 128 * NH
            wide = SUBF // 2
            cell = cells[pl.ds(seg, 1), piece * wide:(piece + 1) * wide]
            cell_x = lax.div(cell, depth_total)
            cell_z = cell - cell_x * depth_total - d * 128
            cell_x = cell_x - s * CX
            hot_z = (lax.broadcasted_iota(jnp.int32, (128, wide), 0) == cell_z).astype(jnp.float32).astype(jnp.bfloat16)
            hot_x = lax.broadcasted_iota(jnp.int32, (CX, wide), 0) == cell_x
            first = piece * wide // 128
            value = jnp.concatenate([gathered[first + n, t] for n in range(wide // 128)], axis=1)
            high = value.astype(jnp.bfloat16).astype(jnp.float32)
            rows = [
                jnp.where(hot_x, part[c:c + 1, :], 0.0).astype(jnp.bfloat16)
                for part in (high, value - high) for c in range(6)
            ]
            out = lax.dot_general(
                jnp.concatenate(rows, axis=0), hot_z, (((1,), (1,)), ((), ())),
                preferred_element_type=jnp.float32)
            n = 6 * CX
            out = out[0:n] + out[n:2 * n]
            ref = plane if t == 0 else last_plane
            if piece == 0:
                ref[...] = out
            else:
                ref[...] = ref[...] + out

    def apply_source(ref, spans):
        @pl.when(on_fault)
        def _():
            for c in range(6):
                for x0, n in spans:
                    at = pl.ds((x0 + XP) * ROW + YP, n, stride=ROW)
                    Sf[c, at, :] = Sf[c, at, :] - ref[c * CX + x0:c * CX + x0 + n, :]

    middle = ((2, CX - 4),)

    i, j = (lax.broadcasted_iota(jnp.int32, (256, 128), n) for n in range(2))
    off = (i & 127) - j
    for n, (a, b) in enumerate(((1, 0), (0, -1))):
        weight = jnp.where(off == a, 27.0, jnp.where(off == b, -27.0, jnp.where(
            off == a + 1, -1.0, jnp.where(off == b - 1, 1.0, 0.0))))
        band[n] = weight.astype(jnp.bfloat16)

    @pl.when(jnp.logical_not(on_fault))
    def _():
        last_plane[...] = jnp.zeros_like(last_plane)

    source_first()
    loads[0].wait()
    for copy in loads[4:]:
        copy.start()
    yz_send(0, 0)
    yz_send(0, 1)
    deep_part(0, 0)
    deep_part(0, 1)
    loads[2].wait()
    loads[3].wait()
    yz_recv(0, 0)
    source_second()
    interior(velocity_pair)
    yz_send(1, 0)
    source_third()
    deep_part(1, 0)
    yz_recv(0, 1)
    edges(0, velocity_pair)
    yz_send(1, 1)
    for copy in loads[4:]:
        copy.wait()
    yz_recv(1, 0)
    interior(stress_pair)
    source_gather()
    source_plane(0, 0)
    source_plane(0, 1)
    apply_source(plane, middle)
    yz_send(2, 0)
    deep_part(1, 1)
    deep_part(2, 0)
    x_wait_send(0)
    yz_recv(1, 1)
    edges(1, stress_pair, plane)
    yz_send(2, 1)
    yz_recv(2, 0)
    interior(velocity_pair)
    yz_send(3, 0)
    deep_part(2, 1)
    deep_part(3, 0)
    source_plane(1, 0)
    x_wait_send(1)
    yz_recv(2, 1)
    edges(2, velocity_pair)
    yz_send(3, 1)
    yz_recv(3, 0)
    interior(stress_pair)
    source_plane(1, 1)
    apply_source(last_plane, middle)
    deep_part(3, 1)
    yz_recv(3, 1)
    x_wait_send(2)
    for h in range(4):
        for part in range(2):
            for there, pair_of in (("k", y_copies(h, part)), ("d", z_copies(h, part))):
                each(has[there + "_up"], [pair_of[0]], lambda c: c.wait_send())
                each(has[there + "_dn"], [pair_of[1]], lambda c: c.wait_send())
    over_groups(lambda g: c_copy(group, g).wait_send())
    pair_copy(parity).wait_send()
    over_fault(lambda h: g_copy(chunk, h).wait_send())
    x_wait_recv(3, 0)
    x_wait_recv(3, 1)
    x_wait_send(3)


def solution(mesh):
    ns, nd, nh = (mesh.shape[a] for a in ("strike", "dip", "depth"))

    def body(velocity, stress, memory, lam, mu, buo, rel, ane, rate, cell, active, offset):
        cx, cy, cz = lam.shape
        subf = cell.shape[1]
        assert cz == 128 and subf == 128 * nd * nh
        planes, rows = cx + 2 * XP, cy + 2 * YP
        f32 = jnp.float32
        block = pltpu.VMEM((cx, cy, cz), f32)
        dma = pltpu.SemaphoreType.DMA
        hbm = pl.BlockSpec(memory_space=pltpu.HBM)
        vmem = pl.BlockSpec(memory_space=pltpu.VMEM)
        between = (
            pltpu.VMEM((6, planes, rows, cz), f32),
            pltpu.VMEM((3, planes, rows, cz), f32),
            pltpu.VMEM((6, cx, cy, cz), f32),
            pltpu.VMEM((3, cx, cy, cz), f32),
            block, block, block, block,
            pltpu.VMEM((6 * cx, cz), f32),
        )
        held = pl.pallas_call(
            functools.partial(kernel, (ns, nd, nh, cx, cy, subf)),
            out_shape=between,
            in_specs=[hbm] * 12,
            out_specs=(vmem,) * 9,
            scratch_shapes=[
                block,
                pltpu.VMEM((6, rate.shape[1], 128), f32),
                pltpu.VMEM(cell.shape, jnp.int32),
                pltpu.SMEM(active.shape, jnp.int32),
                pltpu.SMEM(offset.shape, jnp.int32),
                *[(pltpu.VMEM((4, 64, cz), f32), pltpu.VMEM((4, 24, cz), f32))] * 4,
                *[(pltpu.VMEM((4, 2, cy, cz), f32), pltpu.VMEM((4, 1, cy, cz), f32))] * 3,
                pltpu.VMEM((2, 2 * cz, cz), jnp.bfloat16),
                pltpu.VMEM((ns // NA, STEPS, 8, 128), f32),
                pltpu.VMEM((NA, STEPS, 8, 128), f32),
                pltpu.VMEM((STEPS, 8, 128), f32),
                pltpu.VMEM((nd * nh, STEPS, 8, 128), f32),
                pltpu.VMEM((6 * cx, cz), f32),
                dma((12,)), dma((4, 4)), dma((4, 4)), dma((4, 2, 2)), dma((4, 2, 2)), dma((4, 2, 2)), dma((4, 2, 2)),
                dma((ns // NA,)), dma((ns // NA,)), dma, dma, dma((nh,)), dma((nd * nh,)),
            ],
            compiler_params=pltpu.CompilerParams(
                collective_id=0, has_side_effects=True, vmem_limit_bytes=40 * 1024 * 1024
            ),
            cost_estimate=pl.CostEstimate(flops=30_000_000, bytes_accessed=6_000_000, transcendentals=0),
        )(*(
            pltpu.with_memory_space_constraint(a, pltpu.HBM)
            for a in (velocity, stress, memory, lam, mu, buo, rel, ane, jnp.transpose(rate, (0, 2, 1, 3)), cell, active, offset)
        ))
        return pl.pallas_call(
            functools.partial(finish, (cx, cy)),
            out_shape=tuple(jax.ShapeDtypeStruct(a.shape, f32) for a in (velocity, stress, memory)),
            in_specs=[vmem] * 9,
            out_specs=(hbm,) * 3,
            scratch_shapes=[
                pltpu.VMEM((6, 4, cy, cz), f32),
                pltpu.VMEM((6, 4, cy, cz), f32),
                dma((7,)),
            ],
            compiler_params=pltpu.CompilerParams(vmem_limit_bytes=40 * 1024 * 1024),
            cost_estimate=pl.CostEstimate(flops=2_000_000, bytes_accessed=4_000_000, transcendentals=0),
        )(*held)

    field = P(None, "strike", "dip", "depth")
    cellwise = P("strike", "dip", "depth")
    return jax.shard_map(
        body,
        mesh=mesh,
        in_specs=(field,) * 3 + (cellwise,) * 5 + (P("strike", None, None, None), P(), P(), P()),
        out_specs=(field,) * 3,
        check_vma=False,
    )
```

```python
import functools

import jax
import jax.numpy as jnp
from jax import lax
from jax.experimental import pallas as pl
from jax.experimental.pallas import tpu as pltpu
from jax.sharding import PartitionSpec as P

MESH = pl.DeviceIdType.MESH
TB = 8
STEPS = 2
R24 = 0.12 / 24.0
XP = 2
YP = 8
NA = 2

X_GROUPS = {"s": ((0, 1, 1, 2), (3, 2, 2, 1)), "v": ((0, 1, 2, 1), (1, 2, 1, 2))}
Y_FIELDS = {"s": ((3, True), (5, True), (1, False)), "v": ((1, True), (0, False), (2, False))}
Z_FIELDS = {"s": (4, 5, 2), "v": (0, 1, 2)}
Z_BACK = {"s": (True, True, False), "v": (False, False, True)}


def stress_tiles(x, m, sizes, tiles, Sf, Vf, M, deep, material, put):
    CY, ROW = sizes
    for j in tiles:
        at = (x + XP) * ROW + YP + j
        rows = pl.ds(j, 8)

        def get(c, n, at=at):
            return Vf[c, pl.ds(at + n, 8), :]

        vx = [get(0, n * ROW) for n in range(-2, 3)]
        vy = [get(1, n * ROW) for n in range(-1, 4)]
        vz = [get(2, n * ROW) for n in range(-1, 4)]
        for p in range(2):
            o = p * ROW
            lam, mu, relax, ane = material(m + p, rows)
            shear = R24 * mu
            twice = 2.0 * shear
            part = (1.0 - relax) * ane
            vx_at, vy_at, vz_at = vx[2 + p], vy[1 + p], vz[1 + p]
            xx = 27.0 * (vx_at - vx[1 + p]) - (vx[3 + p] - vx[p])
            yy = 27.0 * (vy_at - get(1, o - 1)) - (get(1, o + 1) - get(1, o - 2))
            zz = deep[2, x + p, rows, :]
            normal = R24 * lam * (xx + yy + zz)
            xy = 27.0 * ((get(0, o + 1) - vx_at) + (vy[2 + p] - vy_at)) - (
                (get(0, o + 2) - get(0, o - 1)) + (vy[3 + p] - vy[p]))
            xz = 27.0 * (vz[2 + p] - vz_at) - (vz[3 + p] - vz[p]) + deep[0, x + p, rows, :]
            yz = 27.0 * (get(2, o + 1) - vz_at) - (get(2, o + 2) - get(2, o - 1)) + deep[1, x + p, rows, :]
            grown = (
                normal + twice * xx, normal + twice * yy, normal + twice * zz,
                shear * xy, shear * xz, shear * yz,
            )
            for c in range(6):
                old = M[c, x + p, rows, :]
                new = relax * old + part * grown[c]
                stress = Sf[c, pl.ds(pl.multiple_of(at + o, 8), 8), :] + grown[c] - 0.5 * (old + new)
                put(c, x + p, at + o, rows, stress, new)


def finish(dims, S, V, M, deep, lam, mu, rel, ane, plane, vel_out, str_out, mem_out, stress, memory, sem):
    CX, CY = dims
    ROW = CY + 2 * YP
    own = pl.ds(YP, CY)
    middle = pl.ds(2, CX - 4)
    copies = [
        pltpu.make_async_copy(V.at[:, pl.ds(XP, CX), own], vel_out, sem.at[0]),
        pltpu.make_async_copy(S.at[:, pl.ds(XP + 2, CX - 4), own], str_out.at[:, middle], sem.at[1]),
        pltpu.make_async_copy(M.at[:, middle], mem_out.at[:, middle], sem.at[2]),
    ]
    for copy in copies:
        copy.start()
    Sf = S.reshape(6, (CX + 2 * XP) * ROW, 128)
    Vf = V.reshape(3, (CX + 2 * XP) * ROW, 128)

    @pl.loop(0, 2)
    def _(i):
        x = i * (CX - 2)

        def material(m, rows):
            return tuple(ref[m, rows, :] for ref in (lam, mu, rel, ane))

        def put(c, at_x, at, rows, s, m):
            place = at_x - i * (CX - 4)
            stress[c, place, rows, :] = s
            memory[c, place, rows, :] = m

        stress_tiles(x, x, (CY, ROW), range(0, CY, 8), Sf, Vf, M, deep, material, put)

    for c in range(6):
        for n, x in enumerate((0, 1, CX - 2, CX - 1)):
            stress[c, n, 0:1, :] = stress[c, n, 0:1, :] - plane[c * CX + x:c * CX + x + 1, :]
    for n in range(2):
        here, there = pl.ds(2 * n, 2), pl.ds(n * (CX - 2), 2)
        copies.append(pltpu.make_async_copy(stress.at[:, here], str_out.at[:, there], sem.at[3 + 2 * n]))
        copies.append(pltpu.make_async_copy(memory.at[:, here], mem_out.at[:, there], sem.at[4 + 2 * n]))
    for copy in copies[3:]:
        copy.start()
    for copy in copies:
        copy.wait()


def kernel(
    dims,
    vel_hbm, str_hbm, mem_hbm, lam_hbm, mu_hbm, buo_hbm, rel_hbm, ane_hbm, rate_hbm, cell_hbm,
    active_hbm, offset_hbm,
    S, V, M, deep, lam, mu, rel, ane, last_plane,
    buo, rate, cells, active, offset,
    ysend_up, ysend_dn, yrecv_up, yrecv_dn, zsend, zrecv_up, zrecv_dn, band,
    cand, pair, chosen, gathered, plane,
    ld_sem, xs_sem, xr_sem, ys_sem, yr_sem, zs_sem, zr_sem,
    c_send, c_recv, p_send, p_recv, g_send, g_recv,
):
    NS, ND, NH, CX, CY, SUBF = dims
    ROW = CY + 2 * YP
    NB = NS // NA
    s = lax.axis_index("strike")
    k = lax.axis_index("dip")
    d = lax.axis_index("depth")
    fault = ND // 2
    on_fault = k == fault
    group, parity = lax.div(s, NA), lax.rem(s, NA)
    chunk = k * NH + d

    def near(axis, pos, size, step):
        return {axis: jnp.clip(pos + step, 0, size - 1)}

    s_up, s_dn = near("strike", s, NS, 1), near("strike", s, NS, -1)
    k_up, k_dn = near("dip", k, ND, 1), near("dip", k, ND, -1)
    d_up, d_dn = near("depth", d, NH, 1), near("depth", d, NH, -1)
    has = {
        "s_up": s < NS - 1, "s_dn": s > 0,
        "k_up": k < ND - 1, "k_dn": k > 0,
        "d_up": d < NH - 1, "d_dn": d > 0,
    }

    barrier = pltpu.get_barrier_semaphore()
    count = jnp.int32(0)
    for name, to in (("s_up", s_up), ("s_dn", s_dn), ("k_up", k_up), ("k_dn", k_dn), ("d_up", d_up), ("d_dn", d_dn)):
        there = has[name]
        count = count + there.astype(jnp.int32)

        @pl.when(there)
        def _(to=to):
            pl.semaphore_signal(barrier, inc=1, device_id=to, device_id_type=MESH)

    other = {"strike": group * NA + lax.rem(parity + 1, NA)}
    pl.semaphore_signal(barrier, inc=1, device_id=other, device_id_type=MESH)
    count = count + 1

    @pl.loop(0, NB)
    def _(g):
        @pl.when(g != group)
        def _():
            pl.semaphore_signal(
                barrier, inc=1, device_id={"strike": g * NA + parity}, device_id_type=MESH
            )

    count = count + (NB - 1)

    @pl.loop(0, NH)
    def _(h):
        @pl.when(jnp.logical_not(on_fault & (h == d)))
        def _():
            pl.semaphore_signal(
                barrier, inc=1, device_id={"dip": fault, "depth": h}, device_id_type=MESH
            )

    count = count + NH - on_fault.astype(jnp.int32)

    @pl.when(on_fault)
    def _():
        @pl.loop(0, ND * NH)
        def _(j):
            @pl.when(j != chunk)
            def _():
                pl.semaphore_signal(
                    barrier, inc=1,
                    device_id={"dip": lax.div(j, NH), "depth": lax.rem(j, NH)},
                    device_id_type=MESH,
                )

    count = count + jnp.where(on_fault, ND * NH - 1, 0)
    inner = (slice(None), pl.ds(XP, CX), pl.ds(YP, CY))
    loads = [
        pltpu.make_async_copy(str_hbm, S.at[inner], ld_sem.at[0]),
        pltpu.make_async_copy(
            rate_hbm.at[0, :, :, pl.ds(pl.multiple_of(chunk * 128, 128), 128)], rate, ld_sem.at[1]
        ),
        pltpu.make_async_copy(vel_hbm, V.at[inner], ld_sem.at[2]),
        pltpu.make_async_copy(buo_hbm, buo, ld_sem.at[3]),
        pltpu.make_async_copy(mem_hbm, M, ld_sem.at[4]),
        pltpu.make_async_copy(lam_hbm, lam, ld_sem.at[5]),
        pltpu.make_async_copy(mu_hbm, mu, ld_sem.at[6]),
        pltpu.make_async_copy(rel_hbm, rel, ld_sem.at[7]),
        pltpu.make_async_copy(ane_hbm, ane, ld_sem.at[8]),
        pltpu.make_async_copy(cell_hbm, cells, ld_sem.at[9]),
    ]
    order = (
        pltpu.make_async_copy(active_hbm, active, ld_sem.at[10]),
        pltpu.make_async_copy(offset_hbm, offset, ld_sem.at[11]),
    )
    for copy in (loads[1], *order, loads[0], loads[2], loads[3]):
        copy.start()

    pl.semaphore_wait(barrier, count)

    def x_copies(h):
        kind = "sv"[h % 2]
        ref = S if kind == "s" else V
        up, dn = [], []
        for n, (c0, nc, lu, ld) in enumerate(X_GROUPS[kind]):
            comps = pl.ds(c0, nc)
            rows = pl.ds(YP, CY)
            if h == 0:
                src_up = str_hbm.at[comps, pl.ds(CX - lu, lu)]
                src_dn = str_hbm.at[comps, pl.ds(0, ld)]
            else:
                src_up = ref.at[comps, pl.ds(XP + CX - lu, lu), rows]
                src_dn = ref.at[comps, pl.ds(XP, ld), rows]
            up.append(pltpu.make_async_remote_copy(
                src_up, ref.at[comps, pl.ds(XP - lu, lu), rows],
                xs_sem.at[h, n], xr_sem.at[h, n], device_id=s_up, device_id_type=MESH))
            dn.append(pltpu.make_async_remote_copy(
                src_dn, ref.at[comps, pl.ds(XP + CX, ld), rows],
                xs_sem.at[h, 2 + n], xr_sem.at[h, 2 + n], device_id=s_dn, device_id_type=MESH))
        return up, dn

    def each(there, copies, act):
        @pl.when(there)
        def _():
            for copy in copies:
                act(copy)

    def x_start(h, side):
        there = has["s_up"] if side == 0 else has["s_dn"]
        each(there, x_copies(h)[side], lambda c: c.start())

    def x_wait_recv(h, side):
        there = has["s_dn"] if side == 0 else has["s_up"]
        each(there, x_copies(h)[side], lambda c: c.wait_recv())

    def x_wait_send(h):
        up, dn = x_copies(h)
        each(has["s_up"], up, lambda c: c.wait_send())
        each(has["s_dn"], dn, lambda c: c.wait_send())

    x_start(0, 0)

    Sf = S.reshape(6, (CX + 2 * XP) * ROW, 128)
    Vf = V.reshape(3, (CX + 2 * XP) * ROW, 128)
    flat = {"s": Sf, "v": Vf}

    for F, nc in ((S, 6), (V, 3)):
        zero_x = jnp.zeros((nc, XP, CY, 128), jnp.float32)

        @pl.when(s == 0)
        def _(F=F, zero_x=zero_x):
            F[:, 0:XP, YP:YP + CY, :] = zero_x

        @pl.when(s == NS - 1)
        def _(F=F, zero_x=zero_x):
            F[:, XP + CX:, YP:YP + CY, :] = zero_x

    for there, refs in (
        (has["k_dn"], yrecv_up), (has["k_up"], yrecv_dn), (has["d_dn"], zrecv_up), (has["d_up"], zrecv_dn),
    ):
        @pl.when(jnp.logical_not(there))
        def _(refs=refs):
            for ref in refs:
                ref[...] = jnp.zeros(ref.shape, jnp.float32)

    for refs in (ysend_up, ysend_dn):
        for ref in refs:
            ref[:, ref.shape[1] - 8:, :] = jnp.zeros((4, 8, 128), jnp.float32)

    def y_layers(kind):
        up, dn = [], []
        for c, back in Y_FIELDS[kind]:
            up += [(c, CY - 2), (c, CY - 1)] if back else [(c, CY - 1)]
            dn += [(c, 0)] if back else [(c, 0), (c, 1)]
        return up, dn

    PLANES = (tuple(range(2, CX - 2)), (0, 1, CX - 2, CX - 1))
    SPANS = (((2, CX - 4),), ((0, 2), (CX - 2, 2)))

    def y_copies(h, part):
        size = len(PLANES[part])
        nu, nd = (-(-len(layers) * size // 8) * 8 for layers in y_layers("sv"[h % 2]))
        return (
            pltpu.make_async_remote_copy(
                ysend_up[part].at[h, pl.ds(0, nu)], yrecv_up[part].at[h, pl.ds(0, nu)],
                ys_sem.at[h, part, 0], yr_sem.at[h, part, 0], device_id=k_up, device_id_type=MESH),
            pltpu.make_async_remote_copy(
                ysend_dn[part].at[h, pl.ds(0, nd)], yrecv_dn[part].at[h, pl.ds(0, nd)],
                ys_sem.at[h, part, 1], yr_sem.at[h, part, 1], device_id=k_dn, device_id_type=MESH),
        )

    def z_copies(h, part):
        return (
            pltpu.make_async_remote_copy(
                zsend[part].at[h], zrecv_up[part].at[h],
                zs_sem.at[h, part, 0], zr_sem.at[h, part, 0], device_id=d_up, device_id_type=MESH),
            pltpu.make_async_remote_copy(
                zsend[part].at[h], zrecv_dn[part].at[h],
                zs_sem.at[h, part, 1], zr_sem.at[h, part, 1], device_id=d_dn, device_id_type=MESH),
        )

    lane = lax.broadcasted_iota(jnp.int32, (CY, 128), 1)
    slot = lane >> 2
    quarter = lane & 3

    def turn(value, n):
        return pltpu.roll(value, n % 128, 1)

    def z_slot(part, place, n):
        if part == 0:
            return place // 2, n + 16 * (place % 2)
        return 0, n + 4 * place

    def yz_send(h, part):
        kind = "sv"[h % 2]
        F = flat[kind]
        base = XP * ROW + YP
        for layers, refs in zip(y_layers(kind), (ysend_up, ysend_dn)):
            at = 0
            for c, row in layers:
                for x0, n in SPANS[part]:
                    refs[part][h, at:at + n, :] = F[c, pl.ds(base + x0 * ROW + row, n, stride=ROW), :]
                    at += n
        up, dn = y_copies(h, part)
        each(has["k_up"], [up], lambda c: c.start())
        each(has["k_dn"], [dn], lambda c: c.start())
        arrays = [jnp.zeros((CY, 128), jnp.float32)] * (2 - part)
        for place, comp in enumerate(Z_FIELDS[kind]):
            for n, x in enumerate(PLANES[part]):
                where, index = z_slot(part, place, n)
                value = F[comp, pl.ds((x + XP) * ROW + YP, CY), :]
                arrays[where] = jnp.where(slot == index, turn(value, 4 * index + 2), arrays[where])
        for n, value in enumerate(arrays):
            zsend[part][h, n] = value
        up, dn = z_copies(h, part)
        each(has["d_up"], [up], lambda c: c.start())
        each(has["d_dn"], [dn], lambda c: c.start())

    def yz_recv(h, part):
        kind = "sv"[h % 2]
        F = flat[kind]
        up, dn = y_copies(h, part)
        each(has["k_dn"], [up], lambda c: c.wait_recv())
        each(has["k_up"], [dn], lambda c: c.wait_recv())
        base = XP * ROW + YP
        for layers, refs, shift in zip(y_layers(kind), (yrecv_up, yrecv_dn), (-CY, CY)):
            at = 0
            for c, row in layers:
                for x0, n in SPANS[part]:
                    F[c, pl.ds(base + x0 * ROW + row + shift, n, stride=ROW), :] = refs[part][h, at:at + n, :]
                    at += n
        up, dn = z_copies(h, part)
        each(has["d_dn"], [up], lambda c: c.wait_recv())
        each(has["d_up"], [dn], lambda c: c.wait_recv())
        fixes = {}
        for place, back in enumerate(Z_BACK[kind]):
            ends = (lane == 127) | (lane < 2) if back else (lane > 125) | (lane == 0)
            for n, x in enumerate(PLANES[part]):
                where, index = z_slot(part, place, n)
                if (where, back) not in fixes:
                    mix = jnp.where(quarter < 2, zrecv_up[part][h, where], zrecv_dn[part][h, where])
                    below, two_after = turn(mix, 1), turn(mix, -2)
                    if back:
                        fix = jnp.where(quarter == 0, -two_after, jnp.where(quarter == 1, below - 27.0 * mix, below))
                    else:
                        fix = jnp.where(quarter == 1, 27.0 * turn(mix, -1) - two_after, jnp.where(quarter == 0, -two_after, below))
                    fixes[where, back] = jnp.where(quarter == 3, 0.0, fix)
                moved = turn(fixes[where, back], (127 if back else 126) - 4 * index)
                deep[place, x] = deep[place, x] + jnp.where(ends, moved, 0.0)

    def deep_part(h, part):
        kind = "sv"[h % 2]
        F = S if kind == "s" else V
        for place, (comp, back) in enumerate(zip(Z_FIELDS[kind], Z_BACK[kind])):
            f = jnp.concatenate(
                [F[comp, XP + x0:XP + x0 + n, YP:YP + CY, :].reshape(n * CY, 128) for x0, n in SPANS[part]], axis=0)
            high = f.astype(jnp.bfloat16)
            low = (f - high.astype(jnp.float32)).astype(jnp.bfloat16)
            out = lax.dot_general(
                jnp.concatenate([high, low], axis=1), band[1 if back else 0],
                (((1,), (0,)), ((), ())), preferred_element_type=jnp.float32)
            at = 0
            for x0, n in SPANS[part]:
                deep[place, x0:x0 + n] = out[at:at + n * CY].reshape(n, CY, 128)
                at += n * CY

    def velocity_pair(x, tiles):
        for j in tiles:
            at = (x + XP) * ROW + YP + j

            def get(c, n, Sf=Sf, at=at):
                return Sf[c, pl.ds(at + n, 8), :]

            xx = [get(0, n * ROW) for n in range(-1, 4)]
            xy = [get(3, n * ROW) for n in range(-2, 3)]
            xz = [get(4, n * ROW) for n in range(-2, 3)]
            for p in range(2):
                o = p * ROW
                gain = R24 * buo[x + p, pl.ds(j, 8), :]
                xy_at, yy, yz = xy[2 + p], [get(1, o + n) for n in range(-1, 3)], [get(5, o + n) for n in range(-2, 2)]
                close = (
                    (xx[2 + p] - xx[1 + p]) + (xy_at - get(3, o - 1)),
                    (xy_at - xy[1 + p]) + (yy[2] - yy[1]),
                    (xz[2 + p] - xz[1 + p]) + (yz[2] - yz[1]),
                )
                far = (
                    (xx[3 + p] - xx[p]) + (get(3, o + 1) - get(3, o - 2)),
                    (xy[3 + p] - xy[p]) + (yy[3] - yy[0]),
                    (xz[3 + p] - xz[p]) + (yz[3] - yz[0]),
                )
                for c in range(3):
                    own = pl.ds(pl.multiple_of(at + o, 8), 8)
                    Vf[c, own, :] = Vf[c, own, :] + gain * (
                        27.0 * close[c] - far[c] + deep[c, x + p, pl.ds(j, 8), :])

    def stress_pair(x, tiles):
        def material(x, rows):
            return lam[x, rows, :], mu[x, rows, :], rel[x, rows, :], ane[x, rows, :]

        def put(c, x, at, rows, stress, memory):
            Sf[c, pl.ds(pl.multiple_of(at, 8), 8), :] = stress
            M[c, x, rows, :] = memory

        stress_tiles(x, x, (CY, ROW), tiles, Sf, Vf, M, deep, material, put)

    def interior(one):
        @pl.loop(0, (CX - 4) // 2)
        def _(i):
            one(2 * i + 2, range(0, CY, 8))

    nought = jnp.minimum(s, 0)

    def edges(h, one, source=None):
        sides = ((0, 0), (1, CX - 2))
        for side, x in sides if h % 2 == 0 else sides[::-1]:
            x_wait_recv(h, side)
            one(nought + x, range(0, CY, 8))
            if source is not None:
                apply_source(source, ((x, 2),))
            x_start(h + 1, 1 - side)

    def candidates():
        row = lax.broadcasted_iota(jnp.int32, (TB, 128), 0)
        weights = jnp.where((row == 0) | (row == TB - 1), 0.5 / (TB - 1), 1.0 / (TB - 1))
        for t in range(STEPS):
            o = offset[t]
            for c in range(6):
                samples = rate[c, pl.ds(o, TB), :]
                cand[group, t, c:c + 1, :] = jnp.sum(samples * weights, axis=0, keepdims=True)
            cand[group, t, 6:8, :] = jnp.zeros((2, 128), jnp.float32)

    def c_copy(sender, receiver):
        return pltpu.make_async_remote_copy(
            cand.at[sender], cand.at[sender], c_send.at[receiver], c_recv.at[sender],
            device_id={"strike": receiver * NA + parity}, device_id_type=MESH)

    def over_groups(act):
        @pl.loop(0, NB)
        def _(g):
            @pl.when(g != group)
            def _():
                act(g)

    def pair_copy(which):
        return pltpu.make_async_remote_copy(
            pair.at[which], pair.at[which], p_send, p_recv, device_id=other, device_id_type=MESH)

    def g_copy(which, h):
        return pltpu.make_async_remote_copy(
            chosen, gathered.at[which], g_send.at[h], g_recv.at[which],
            device_id={"dip": fault, "depth": h}, device_id_type=MESH)

    def over_fault(act):
        @pl.loop(0, NH)
        def _(h):
            @pl.when(jnp.logical_not(on_fault & (h == d)))
            def _():
                act(h)

    def source_first():
        loads[1].wait()
        for copy in order:
            copy.wait()
        candidates()
        over_groups(lambda g: c_copy(group, g).start())

    def source_second():
        over_groups(lambda g: c_copy(g, group).wait_recv())
        for t in range(STEPS):
            pair[parity, t] = cand[lax.div(active[t], NA), t]
        pair_copy(parity).start()

    def source_third():
        pair_copy(lax.rem(parity + 1, NA)).wait_recv()
        for t in range(STEPS):
            value = pair[lax.rem(active[t], NA), t]
            chosen[t] = value

            @pl.when(on_fault)
            def _(t=t, value=value):
                gathered[chunk, t] = value

        over_fault(lambda h: g_copy(chunk, h).start())

    def source_gather():
        @pl.when(on_fault)
        def _():
            @pl.loop(0, ND * NH)
            def _(j):
                @pl.when(j != chunk)
                def _():
                    g_copy(j, 0).wait_recv()

    def source_plane(t, piece):
        @pl.when(on_fault)
        def _():
            seg = active[t]
            depth_total = 128 * NH
            wide = SUBF // 2
            cell = cells[pl.ds(seg, 1), piece * wide:(piece + 1) * wide]
            cell_x = lax.div(cell, depth_total)
            cell_z = cell - cell_x * depth_total - d * 128
            cell_x = cell_x - s * CX
            hot_z = (lax.broadcasted_iota(jnp.int32, (128, wide), 0) == cell_z).astype(jnp.float32).astype(jnp.bfloat16)
            hot_x = lax.broadcasted_iota(jnp.int32, (CX, wide), 0) == cell_x
            first = piece * wide // 128
            value = jnp.concatenate([gathered[first + n, t] for n in range(wide // 128)], axis=1)
            high = value.astype(jnp.bfloat16).astype(jnp.float32)
            rows = [
                jnp.where(hot_x, part[c:c + 1, :], 0.0).astype(jnp.bfloat16)
                for part in (high, value - high) for c in range(6)
            ]
            out = lax.dot_general(
                jnp.concatenate(rows, axis=0), hot_z, (((1,), (1,)), ((), ())),
                preferred_element_type=jnp.float32)
            n = 6 * CX
            out = out[0:n] + out[n:2 * n]
            ref = plane if t == 0 else last_plane
            if piece == 0:
                ref[...] = out
            else:
                ref[...] = ref[...] + out

    def apply_source(ref, spans):
        @pl.when(on_fault)
        def _():
            for c in range(6):
                for x0, n in spans:
                    at = pl.ds((x0 + XP) * ROW + YP, n, stride=ROW)
                    Sf[c, at, :] = Sf[c, at, :] - ref[c * CX + x0:c * CX + x0 + n, :]

    middle = ((2, CX - 4),)

    i, j = (lax.broadcasted_iota(jnp.int32, (256, 128), n) for n in range(2))
    off = (i & 127) - j
    for n, (a, b) in enumerate(((1, 0), (0, -1))):
        weight = jnp.where(off == a, 27.0, jnp.where(off == b, -27.0, jnp.where(
            off == a + 1, -1.0, jnp.where(off == b - 1, 1.0, 0.0))))
        band[n] = weight.astype(jnp.bfloat16)

    @pl.when(jnp.logical_not(on_fault))
    def _():
        last_plane[...] = jnp.zeros_like(last_plane)

    source_first()
    loads[0].wait()
    for copy in loads[4:]:
        copy.start()
    yz_send(0, 0)
    yz_send(0, 1)
    x_start(0, 1)
    deep_part(0, 0)
    deep_part(0, 1)
    loads[2].wait()
    loads[3].wait()
    yz_recv(0, 0)
    source_second()
    interior(velocity_pair)
    yz_send(1, 0)
    source_third()
    deep_part(1, 0)
    yz_recv(0, 1)
    edges(0, velocity_pair)
    yz_send(1, 1)
    for copy in loads[4:]:
        copy.wait()
    yz_recv(1, 0)
    interior(stress_pair)
    source_gather()
    source_plane(0, 0)
    source_plane(0, 1)
    apply_source(plane, middle)
    yz_send(2, 0)
    deep_part(1, 1)
    deep_part(2, 0)
    x_wait_send(0)
    yz_recv(1, 1)
    edges(1, stress_pair, plane)
    yz_send(2, 1)
    yz_recv(2, 0)
    interior(velocity_pair)
    yz_send(3, 0)
    deep_part(2, 1)
    deep_part(3, 0)
    source_plane(1, 0)
    x_wait_send(1)
    yz_recv(2, 1)
    edges(2, velocity_pair)
    yz_send(3, 1)
    yz_recv(3, 0)
    interior(stress_pair)
    source_plane(1, 1)
    apply_source(last_plane, middle)
    deep_part(3, 1)
    yz_recv(3, 1)
    x_wait_send(2)
    for h in range(4):
        for part in range(2):
            for there, pair_of in (("k", y_copies(h, part)), ("d", z_copies(h, part))):
                each(has[there + "_up"], [pair_of[0]], lambda c: c.wait_send())
                each(has[there + "_dn"], [pair_of[1]], lambda c: c.wait_send())
    over_groups(lambda g: c_copy(group, g).wait_send())
    pair_copy(parity).wait_send()
    over_fault(lambda h: g_copy(chunk, h).wait_send())
    x_wait_recv(3, 0)
    x_wait_recv(3, 1)
    x_wait_send(3)


def solution(mesh):
    ns, nd, nh = (mesh.shape[a] for a in ("strike", "dip", "depth"))

    def body(velocity, stress, memory, lam, mu, buo, rel, ane, rate, cell, active, offset):
        cx, cy, cz = lam.shape
        subf = cell.shape[1]
        assert cz == 128 and subf == 128 * nd * nh
        planes, rows = cx + 2 * XP, cy + 2 * YP
        f32 = jnp.float32
        block = pltpu.VMEM((cx, cy, cz), f32)
        dma = pltpu.SemaphoreType.DMA
        hbm = pl.BlockSpec(memory_space=pltpu.HBM)
        vmem = pl.BlockSpec(memory_space=pltpu.VMEM)
        between = (
            pltpu.VMEM((6, planes, rows, cz), f32),
            pltpu.VMEM((3, planes, rows, cz), f32),
            pltpu.VMEM((6, cx, cy, cz), f32),
            pltpu.VMEM((3, cx, cy, cz), f32),
            block, block, block, block,
            pltpu.VMEM((6 * cx, cz), f32),
        )
        held = pl.pallas_call(
            functools.partial(kernel, (ns, nd, nh, cx, cy, subf)),
            out_shape=between,
            in_specs=[hbm] * 12,
            out_specs=(vmem,) * 9,
            scratch_shapes=[
                block,
                pltpu.VMEM((6, rate.shape[1], 128), f32),
                pltpu.VMEM(cell.shape, jnp.int32),
                pltpu.SMEM(active.shape, jnp.int32),
                pltpu.SMEM(offset.shape, jnp.int32),
                *[(pltpu.VMEM((4, 64, cz), f32), pltpu.VMEM((4, 24, cz), f32))] * 4,
                *[(pltpu.VMEM((4, 2, cy, cz), f32), pltpu.VMEM((4, 1, cy, cz), f32))] * 3,
                pltpu.VMEM((2, 2 * cz, cz), jnp.bfloat16),
                pltpu.VMEM((ns // NA, STEPS, 8, 128), f32),
                pltpu.VMEM((NA, STEPS, 8, 128), f32),
                pltpu.VMEM((STEPS, 8, 128), f32),
                pltpu.VMEM((nd * nh, STEPS, 8, 128), f32),
                pltpu.VMEM((6 * cx, cz), f32),
                dma((12,)), dma((4, 4)), dma((4, 4)), dma((4, 2, 2)), dma((4, 2, 2)), dma((4, 2, 2)), dma((4, 2, 2)),
                dma((ns // NA,)), dma((ns // NA,)), dma, dma, dma((nh,)), dma((nd * nh,)),
            ],
            compiler_params=pltpu.CompilerParams(
                collective_id=0, has_side_effects=True, vmem_limit_bytes=40 * 1024 * 1024
            ),
            cost_estimate=pl.CostEstimate(flops=30_000_000, bytes_accessed=6_000_000, transcendentals=0),
        )(*(
            pltpu.with_memory_space_constraint(a, pltpu.HBM)
            for a in (velocity, stress, memory, lam, mu, buo, rel, ane, jnp.transpose(rate, (0, 2, 1, 3)), cell, active, offset)
        ))
        return pl.pallas_call(
            functools.partial(finish, (cx, cy)),
            out_shape=tuple(jax.ShapeDtypeStruct(a.shape, f32) for a in (velocity, stress, memory)),
            in_specs=[vmem] * 9,
            out_specs=(hbm,) * 3,
            scratch_shapes=[
                pltpu.VMEM((6, 4, cy, cz), f32),
                pltpu.VMEM((6, 4, cy, cz), f32),
                dma((7,)),
            ],
            compiler_params=pltpu.CompilerParams(vmem_limit_bytes=40 * 1024 * 1024),
            cost_estimate=pl.CostEstimate(flops=2_000_000, bytes_accessed=4_000_000, transcendentals=0),
        )(*held)

    field = P(None, "strike", "dip", "depth")
    cellwise = P("strike", "dip", "depth")
    return jax.shard_map(
        body,
        mesh=mesh,
        in_specs=(field,) * 3 + (cellwise,) * 5 + (P("strike", None, None, None), P(), P(), P()),
        out_specs=(field,) * 3,
        check_vma=False,
    )
```

```python
import functools

import jax
import jax.numpy as jnp
from jax import lax
from jax.experimental import pallas as pl
from jax.experimental.pallas import tpu as pltpu
from jax.sharding import PartitionSpec as P

MESH = pl.DeviceIdType.MESH
TB = 8
STEPS = 2
R24 = 0.12 / 24.0
XP = 2
YP = 8
NA = 2

X_GROUPS = {"s": ((0, 1, 1, 2), (3, 2, 2, 1)), "v": ((0, 3, 2, 2),)}
Y_FIELDS = {"s": ((3, True), (5, True), (1, False)), "v": ((1, True), (0, False), (2, False))}
Z_FIELDS = {"s": (4, 5, 2), "v": (0, 1, 2)}
Z_BACK = {"s": (True, True, False), "v": (False, False, True)}


def stress_tiles(x, m, sizes, tiles, Sf, Vf, M, deep, material, put):
    CY, ROW = sizes
    for j in tiles:
        at = (x + XP) * ROW + YP + j
        rows = pl.ds(j, 8)

        def get(c, n, at=at):
            return Vf[c, pl.ds(at + n, 8), :]

        vx = [get(0, n * ROW) for n in range(-2, 3)]
        vy = [get(1, n * ROW) for n in range(-1, 4)]
        vz = [get(2, n * ROW) for n in range(-1, 4)]
        for p in range(2):
            o = p * ROW
            lam, mu, relax, ane = material(m + p, rows)
            shear = R24 * mu
            twice = 2.0 * shear
            part = (1.0 - relax) * ane
            vx_at, vy_at, vz_at = vx[2 + p], vy[1 + p], vz[1 + p]
            xx = 27.0 * (vx_at - vx[1 + p]) - (vx[3 + p] - vx[p])
            yy = 27.0 * (vy_at - get(1, o - 1)) - (get(1, o + 1) - get(1, o - 2))
            zz = deep[2, x + p, rows, :]
            normal = R24 * lam * (xx + yy + zz)
            xy = 27.0 * ((get(0, o + 1) - vx_at) + (vy[2 + p] - vy_at)) - (
                (get(0, o + 2) - get(0, o - 1)) + (vy[3 + p] - vy[p]))
            xz = 27.0 * (vz[2 + p] - vz_at) - (vz[3 + p] - vz[p]) + deep[0, x + p, rows, :]
            yz = 27.0 * (get(2, o + 1) - vz_at) - (get(2, o + 2) - get(2, o - 1)) + deep[1, x + p, rows, :]
            grown = (
                normal + twice * xx, normal + twice * yy, normal + twice * zz,
                shear * xy, shear * xz, shear * yz,
            )
            for c in range(6):
                old = M[c, x + p, rows, :]
                new = relax * old + part * grown[c]
                stress = Sf[c, pl.ds(pl.multiple_of(at + o, 8), 8), :] + grown[c] - 0.5 * (old + new)
                put(c, x + p, at + o, rows, stress, new)


def finish(dims, S, V, M, deep, lam, mu, rel, ane, plane, vel_out, str_out, mem_out, stress, memory, sem):
    CX, CY = dims
    ROW = CY + 2 * YP
    own = pl.ds(YP, CY)
    middle = pl.ds(2, CX - 4)
    copies = [
        pltpu.make_async_copy(V.at[:, pl.ds(XP, CX), own], vel_out, sem.at[0]),
        pltpu.make_async_copy(S.at[:, pl.ds(XP + 2, CX - 4), own], str_out.at[:, middle], sem.at[1]),
        pltpu.make_async_copy(M.at[:, middle], mem_out.at[:, middle], sem.at[2]),
    ]
    for copy in copies:
        copy.start()
    Sf = S.reshape(6, (CX + 2 * XP) * ROW, 128)
    Vf = V.reshape(3, (CX + 2 * XP) * ROW, 128)

    @pl.loop(0, 2)
    def _(i):
        x = i * (CX - 2)

        def material(m, rows):
            return tuple(ref[m, rows, :] for ref in (lam, mu, rel, ane))

        def put(c, at_x, at, rows, s, m):
            place = at_x - i * (CX - 4)
            stress[c, place, rows, :] = s
            memory[c, place, rows, :] = m

        stress_tiles(x, x, (CY, ROW), range(0, CY, 8), Sf, Vf, M, deep, material, put)

    for c in range(6):
        for n, x in enumerate((0, 1, CX - 2, CX - 1)):
            stress[c, n, 0:1, :] = stress[c, n, 0:1, :] - plane[c * CX + x:c * CX + x + 1, :]
    for n in range(2):
        here, there = pl.ds(2 * n, 2), pl.ds(n * (CX - 2), 2)
        copies.append(pltpu.make_async_copy(stress.at[:, here], str_out.at[:, there], sem.at[3 + 2 * n]))
        copies.append(pltpu.make_async_copy(memory.at[:, here], mem_out.at[:, there], sem.at[4 + 2 * n]))
    for copy in copies[3:]:
        copy.start()
    for copy in copies:
        copy.wait()


def kernel(
    dims,
    vel_hbm, str_hbm, mem_hbm, lam_hbm, mu_hbm, buo_hbm, rel_hbm, ane_hbm, rate_hbm, cell_hbm,
    active_hbm, offset_hbm,
    S, V, M, deep, lam, mu, rel, ane, last_plane,
    buo, rate, cells, active, offset,
    ysend_up, ysend_dn, yrecv_up, yrecv_dn, zsend, zrecv_up, zrecv_dn, band,
    cand, pair, chosen, gathered, plane,
    ld_sem, xs_sem, xr_sem, ys_sem, yr_sem, zs_sem, zr_sem,
    c_send, c_recv, p_send, p_recv, g_send, g_recv,
):
    NS, ND, NH, CX, CY, SUBF = dims
    ROW = CY + 2 * YP
    NB = NS // NA
    s = lax.axis_index("strike")
    k = lax.axis_index("dip")
    d = lax.axis_index("depth")
    fault = ND // 2
    on_fault = k == fault
    group, parity = lax.div(s, NA), lax.rem(s, NA)
    chunk = k * NH + d

    def near(axis, pos, size, step):
        return {axis: jnp.clip(pos + step, 0, size - 1)}

    s_up, s_dn = near("strike", s, NS, 1), near("strike", s, NS, -1)
    k_up, k_dn = near("dip", k, ND, 1), near("dip", k, ND, -1)
    d_up, d_dn = near("depth", d, NH, 1), near("depth", d, NH, -1)
    has = {
        "s_up": s < NS - 1, "s_dn": s > 0,
        "k_up": k < ND - 1, "k_dn": k > 0,
        "d_up": d < NH - 1, "d_dn": d > 0,
    }

    barrier = pltpu.get_barrier_semaphore()
    count = jnp.int32(0)
    for name, to in (("s_up", s_up), ("s_dn", s_dn), ("k_up", k_up), ("k_dn", k_dn), ("d_up", d_up), ("d_dn", d_dn)):
        there = has[name]
        count = count + there.astype(jnp.int32)

        @pl.when(there)
        def _(to=to):
            pl.semaphore_signal(barrier, inc=1, device_id=to, device_id_type=MESH)

    other = {"strike": group * NA + lax.rem(parity + 1, NA)}

    @pl.loop(0, NB)
    def _(g):
        @pl.when(g != group)
        def _():
            pl.semaphore_signal(
                barrier, inc=1, device_id={"strike": g * NA + parity}, device_id_type=MESH
            )

    count = count + (NB - 1)

    count = count + NH - on_fault.astype(jnp.int32)

    @pl.when(on_fault)
    def _():
        @pl.loop(0, ND * NH)
        def _(j):
            @pl.when(j != chunk)
            def _():
                pl.semaphore_signal(
                    barrier, inc=1,
                    device_id={"dip": lax.div(j, NH), "depth": lax.rem(j, NH)},
                    device_id_type=MESH,
                )

    inner = (slice(None), pl.ds(XP, CX), pl.ds(YP, CY))
    loads = [
        pltpu.make_async_copy(str_hbm, S.at[inner], ld_sem.at[0]),
        pltpu.make_async_copy(
            rate_hbm.at[0, :, :, pl.ds(pl.multiple_of(chunk * 128, 128), 128)], rate, ld_sem.at[1]
        ),
        pltpu.make_async_copy(vel_hbm, V.at[inner], ld_sem.at[2]),
        pltpu.make_async_copy(buo_hbm, buo, ld_sem.at[3]),
        pltpu.make_async_copy(mem_hbm, M, ld_sem.at[4]),
        pltpu.make_async_copy(lam_hbm, lam, ld_sem.at[5]),
        pltpu.make_async_copy(mu_hbm, mu, ld_sem.at[6]),
        pltpu.make_async_copy(rel_hbm, rel, ld_sem.at[7]),
        pltpu.make_async_copy(ane_hbm, ane, ld_sem.at[8]),
        pltpu.make_async_copy(cell_hbm, cells, ld_sem.at[9]),
    ]
    order = (
        pltpu.make_async_copy(active_hbm, active, ld_sem.at[10]),
        pltpu.make_async_copy(offset_hbm, offset, ld_sem.at[11]),
    )
    for copy in (loads[1], *order, loads[0], loads[2], loads[3]):
        copy.start()

    pl.semaphore_wait(barrier, count)

    def x_copies(h):
        kind = "sv"[h % 2]
        ref = S if kind == "s" else V
        up, dn = [], []
        for n, (c0, nc, lu, ld) in enumerate(X_GROUPS[kind]):
            comps = pl.ds(c0, nc)
            rows = pl.ds(YP, CY)
            if h == 0:
                src_up = str_hbm.at[comps, pl.ds(CX - lu, lu)]
                src_dn = str_hbm.at[comps, pl.ds(0, ld)]
            else:
                src_up = ref.at[comps, pl.ds(XP + CX - lu, lu), rows]
                src_dn = ref.at[comps, pl.ds(XP, ld), rows]
            up.append(pltpu.make_async_remote_copy(
                src_up, ref.at[comps, pl.ds(XP - lu, lu), rows],
                xs_sem.at[h, n], xr_sem.at[h, n], device_id=s_up, device_id_type=MESH))
            dn.append(pltpu.make_async_remote_copy(
                src_dn, ref.at[comps, pl.ds(XP + CX, ld), rows],
                xs_sem.at[h, 2 + n], xr_sem.at[h, 2 + n], device_id=s_dn, device_id_type=MESH))
        return up, dn

    def each(there, copies, act):
        @pl.when(there)
        def _():
            for copy in copies:
                act(copy)

    def x_start(h, side):
        there = has["s_up"] if side == 0 else has["s_dn"]
        each(there, x_copies(h)[side], lambda c: c.start())

    def x_wait_recv(h, side):
        there = has["s_dn"] if side == 0 else has["s_up"]
        each(there, x_copies(h)[side], lambda c: c.wait_recv())

    def x_wait_send(h):
        up, dn = x_copies(h)
        each(has["s_up"], up, lambda c: c.wait_send())
        each(has["s_dn"], dn, lambda c: c.wait_send())

    x_start(0, 0)

    Sf = S.reshape(6, (CX + 2 * XP) * ROW, 128)
    Vf = V.reshape(3, (CX + 2 * XP) * ROW, 128)
    flat = {"s": Sf, "v": Vf}

    for F, nc in ((S, 6), (V, 3)):
        zero_x = jnp.zeros((nc, XP, CY, 128), jnp.float32)

        @pl.when(s == 0)
        def _(F=F, zero_x=zero_x):
            F[:, 0:XP, YP:YP + CY, :] = zero_x

        @pl.when(s == NS - 1)
        def _(F=F, zero_x=zero_x):
            F[:, XP + CX:, YP:YP + CY, :] = zero_x

    for there, refs in (
        (has["k_dn"], yrecv_up), (has["k_up"], yrecv_dn), (has["d_dn"], zrecv_up), (has["d_up"], zrecv_dn),
    ):
        @pl.when(jnp.logical_not(there))
        def _(refs=refs):
            for ref in refs:
                ref[...] = jnp.zeros(ref.shape, jnp.float32)

    for refs in (ysend_up, ysend_dn):
        for ref in refs:
            ref[:, ref.shape[1] - 8:, :] = jnp.zeros((4, 8, 128), jnp.float32)

    def y_layers(kind):
        up, dn = [], []
        for c, back in Y_FIELDS[kind]:
            up += [(c, CY - 2), (c, CY - 1)] if back else [(c, CY - 1)]
            dn += [(c, 0)] if back else [(c, 0), (c, 1)]
        return up, dn

    PLANES = (tuple(range(2, CX - 2)), (0, 1, CX - 2, CX - 1))
    SPANS = (((2, CX - 4),), ((0, 2), (CX - 2, 2)))

    def y_copies(h, part):
        size = len(PLANES[part])
        nu, nd = (-(-len(layers) * size // 8) * 8 for layers in y_layers("sv"[h % 2]))
        return (
            pltpu.make_async_remote_copy(
                ysend_up[part].at[h, pl.ds(0, nu)], yrecv_up[part].at[h, pl.ds(0, nu)],
                ys_sem.at[h, part, 0], yr_sem.at[h, part, 0], device_id=k_up, device_id_type=MESH),
            pltpu.make_async_remote_copy(
                ysend_dn[part].at[h, pl.ds(0, nd)], yrecv_dn[part].at[h, pl.ds(0, nd)],
                ys_sem.at[h, part, 1], yr_sem.at[h, part, 1], device_id=k_dn, device_id_type=MESH),
        )

    def z_copies(h, part):
        return (
            pltpu.make_async_remote_copy(
                zsend[part].at[h], zrecv_up[part].at[h],
                zs_sem.at[h, part, 0], zr_sem.at[h, part, 0], device_id=d_up, device_id_type=MESH),
            pltpu.make_async_remote_copy(
                zsend[part].at[h], zrecv_dn[part].at[h],
                zs_sem.at[h, part, 1], zr_sem.at[h, part, 1], device_id=d_dn, device_id_type=MESH),
        )

    lane = lax.broadcasted_iota(jnp.int32, (CY, 128), 1)
    slot = lane >> 2
    quarter = lane & 3

    def turn(value, n):
        return pltpu.roll(value, n % 128, 1)

    def z_slot(part, place, n):
        if part == 0:
            return place // 2, n + 16 * (place % 2)
        return 0, n + 4 * place

    def yz_send(h, part):
        kind = "sv"[h % 2]
        F = flat[kind]
        base = XP * ROW + YP
        for layers, refs in zip(y_layers(kind), (ysend_up, ysend_dn)):
            at = 0
            for c, row in layers:
                for x0, n in SPANS[part]:
                    refs[part][h, at:at + n, :] = F[c, pl.ds(base + x0 * ROW + row, n, stride=ROW), :]
                    at += n
        up, dn = y_copies(h, part)
        each(has["k_up"], [up], lambda c: c.start())
        each(has["k_dn"], [dn], lambda c: c.start())
        arrays = [jnp.zeros((CY, 128), jnp.float32)] * (2 - part)
        for place, comp in enumerate(Z_FIELDS[kind]):
            for n, x in enumerate(PLANES[part]):
                where, index = z_slot(part, place, n)
                value = F[comp, pl.ds((x + XP) * ROW + YP, CY), :]
                arrays[where] = jnp.where(slot == index, turn(value, 4 * index + 2), arrays[where])
        for n, value in enumerate(arrays):
            zsend[part][h, n] = value
        up, dn = z_copies(h, part)
        each(has["d_up"], [up], lambda c: c.start())
        each(has["d_dn"], [dn], lambda c: c.start())

    def yz_recv(h, part):
        kind = "sv"[h % 2]
        F = flat[kind]
        up, dn = y_copies(h, part)
        each(has["k_dn"], [up], lambda c: c.wait_recv())
        each(has["k_up"], [dn], lambda c: c.wait_recv())
        base = XP * ROW + YP
        for layers, refs, shift in zip(y_layers(kind), (yrecv_up, yrecv_dn), (-CY, CY)):
            at = 0
            for c, row in layers:
                for x0, n in SPANS[part]:
                    F[c, pl.ds(base + x0 * ROW + row + shift, n, stride=ROW), :] = refs[part][h, at:at + n, :]
                    at += n
        up, dn = z_copies(h, part)
        each(has["d_dn"], [up], lambda c: c.wait_recv())
        each(has["d_up"], [dn], lambda c: c.wait_recv())
        fixes = {}
        for place, back in enumerate(Z_BACK[kind]):
            ends = (lane == 127) | (lane < 2) if back else (lane > 125) | (lane == 0)
            for n, x in enumerate(PLANES[part]):
                where, index = z_slot(part, place, n)
                if (where, back) not in fixes:
                    mix = jnp.where(quarter < 2, zrecv_up[part][h, where], zrecv_dn[part][h, where])
                    below, two_after = turn(mix, 1), turn(mix, -2)
                    if back:
                        fix = jnp.where(quarter == 0, -two_after, jnp.where(quarter == 1, below - 27.0 * mix, below))
                    else:
                        fix = jnp.where(quarter == 1, 27.0 * turn(mix, -1) - two_after, jnp.where(quarter == 0, -two_after, below))
                    fixes[where, back] = jnp.where(quarter == 3, 0.0, fix)
                moved = turn(fixes[where, back], (127 if back else 126) - 4 * index)
                deep[place, x] = deep[place, x] + jnp.where(ends, moved, 0.0)

    def deep_part(h, part):
        kind = "sv"[h % 2]
        F = S if kind == "s" else V
        for place, (comp, back) in enumerate(zip(Z_FIELDS[kind], Z_BACK[kind])):
            f = jnp.concatenate(
                [F[comp, XP + x0:XP + x0 + n, YP:YP + CY, :].reshape(n * CY, 128) for x0, n in SPANS[part]], axis=0)
            high = f.astype(jnp.bfloat16)
            low = (f - high.astype(jnp.float32)).astype(jnp.bfloat16)
            out = lax.dot_general(
                jnp.concatenate([high, low], axis=1), band[1 if back else 0],
                (((1,), (0,)), ((), ())), preferred_element_type=jnp.float32)
            at = 0
            for x0, n in SPANS[part]:
                deep[place, x0:x0 + n] = out[at:at + n * CY].reshape(n, CY, 128)
                at += n * CY

    def velocity_pair(x, tiles):
        for j in tiles:
            at = (x + XP) * ROW + YP + j

            def get(c, n, Sf=Sf, at=at):
                return Sf[c, pl.ds(at + n, 8), :]

            xx = [get(0, n * ROW) for n in range(-1, 4)]
            xy = [get(3, n * ROW) for n in range(-2, 3)]
            xz = [get(4, n * ROW) for n in range(-2, 3)]
            for p in range(2):
                o = p * ROW
                gain = R24 * buo[x + p, pl.ds(j, 8), :]
                xy_at, yy, yz = xy[2 + p], [get(1, o + n) for n in range(-1, 3)], [get(5, o + n) for n in range(-2, 2)]
                close = (
                    (xx[2 + p] - xx[1 + p]) + (xy_at - get(3, o - 1)),
                    (xy_at - xy[1 + p]) + (yy[2] - yy[1]),
                    (xz[2 + p] - xz[1 + p]) + (yz[2] - yz[1]),
                )
                far = (
                    (xx[3 + p] - xx[p]) + (get(3, o + 1) - get(3, o - 2)),
                    (xy[3 + p] - xy[p]) + (yy[3] - yy[0]),
                    (xz[3 + p] - xz[p]) + (yz[3] - yz[0]),
                )
                for c in range(3):
                    own = pl.ds(pl.multiple_of(at + o, 8), 8)
                    Vf[c, own, :] = Vf[c, own, :] + gain * (
                        27.0 * close[c] - far[c] + deep[c, x + p, pl.ds(j, 8), :])

    def stress_pair(x, tiles):
        def material(x, rows):
            return lam[x, rows, :], mu[x, rows, :], rel[x, rows, :], ane[x, rows, :]

        def put(c, x, at, rows, stress, memory):
            Sf[c, pl.ds(pl.multiple_of(at, 8), 8), :] = stress
            M[c, x, rows, :] = memory

        stress_tiles(x, x, (CY, ROW), tiles, Sf, Vf, M, deep, material, put)

    def interior(one):
        @pl.loop(0, (CX - 4) // 2)
        def _(i):
            one(2 * i + 2, range(0, CY, 8))

    nought = jnp.minimum(s, 0)

    def edges(h, one, source=None):
        sides = ((0, 0), (1, CX - 2))
        for side, x in sides if h % 2 == 0 else sides[::-1]:
            x_wait_recv(h, side)
            one(nought + x, range(0, CY, 8))
            if source is not None:
                apply_source(source, ((x, 2),))
            x_start(h + 1, 1 - side)

    def candidates():
        row = lax.broadcasted_iota(jnp.int32, (TB, 128), 0)
        weights = jnp.where((row == 0) | (row == TB - 1), 0.5 / (TB - 1), 1.0 / (TB - 1))
        for t in range(STEPS):
            o = offset[t]
            for c in range(6):
                samples = rate[c, pl.ds(o, TB), :]
                cand[group, t, c:c + 1, :] = jnp.sum(samples * weights, axis=0, keepdims=True)
            cand[group, t, 6:8, :] = jnp.zeros((2, 128), jnp.float32)

    def c_copy(sender, receiver):
        return pltpu.make_async_remote_copy(
            cand.at[sender], cand.at[sender], c_send.at[receiver], c_recv.at[sender],
            device_id={"strike": receiver * NA + parity}, device_id_type=MESH)

    def over_groups(act):
        @pl.loop(0, NB)
        def _(g):
            @pl.when(g != group)
            def _():
                act(g)

    def pair_copy(which):
        return pltpu.make_async_remote_copy(
            pair.at[which], pair.at[which], p_send, p_recv, device_id=other, device_id_type=MESH)

    def g_copy(which, h):
        return pltpu.make_async_remote_copy(
            chosen, gathered.at[which], g_send.at[h], g_recv.at[which],
            device_id={"dip": fault, "depth": h}, device_id_type=MESH)

    def over_fault(act):
        @pl.loop(0, NH)
        def _(h):
            @pl.when(jnp.logical_not(on_fault & (h == d)))
            def _():
                act(h)

    def source_first():
        loads[1].wait()
        for copy in order:
            copy.wait()
        candidates()
        over_groups(lambda g: c_copy(group, g).start())

    def source_second():
        over_groups(lambda g: c_copy(g, group).wait_recv())
        for t in range(STEPS):
            pair[parity, t] = cand[lax.div(active[t], NA), t]
        pair_copy(parity).start()

    def source_third():
        pair_copy(lax.rem(parity + 1, NA)).wait_recv()
        for t in range(STEPS):
            value = pair[lax.rem(active[t], NA), t]
            chosen[t] = value

            @pl.when(on_fault)
            def _(t=t, value=value):
                gathered[chunk, t] = value

        over_fault(lambda h: g_copy(chunk, h).start())

    def source_gather():
        @pl.when(on_fault)
        def _():
            @pl.loop(0, ND * NH)
            def _(j):
                @pl.when(j != chunk)
                def _():
                    g_copy(j, 0).wait_recv()

    def source_plane(t, piece):
        @pl.when(on_fault)
        def _():
            seg = active[t]
            depth_total = 128 * NH
            wide = SUBF // 2
            cell = cells[pl.ds(seg, 1), piece * wide:(piece + 1) * wide]
            cell_x = lax.div(cell, depth_total)
            cell_z = cell - cell_x * depth_total - d * 128
            cell_x = cell_x - s * CX
            hot_z = (lax.broadcasted_iota(jnp.int32, (128, wide), 0) == cell_z).astype(jnp.float32).astype(jnp.bfloat16)
            hot_x = lax.broadcasted_iota(jnp.int32, (CX, wide), 0) == cell_x
            first = piece * wide // 128
            value = jnp.concatenate([gathered[first + n, t] for n in range(wide // 128)], axis=1)
            high = value.astype(jnp.bfloat16).astype(jnp.float32)
            rows = [
                jnp.where(hot_x, part[c:c + 1, :], 0.0).astype(jnp.bfloat16)
                for part in (high, value - high) for c in range(6)
            ]
            out = lax.dot_general(
                jnp.concatenate(rows, axis=0), hot_z, (((1,), (1,)), ((), ())),
                preferred_element_type=jnp.float32)
            n = 6 * CX
            out = out[0:n] + out[n:2 * n]
            ref = plane if t == 0 else last_plane
            if piece == 0:
                ref[...] = out
            else:
                ref[...] = ref[...] + out

    def apply_source(ref, spans):
        @pl.when(on_fault)
        def _():
            for c in range(6):
                for x0, n in spans:
                    at = pl.ds((x0 + XP) * ROW + YP, n, stride=ROW)
                    Sf[c, at, :] = Sf[c, at, :] - ref[c * CX + x0:c * CX + x0 + n, :]

    middle = ((2, CX - 4),)

    i, j = (lax.broadcasted_iota(jnp.int32, (256, 128), n) for n in range(2))
    off = (i & 127) - j
    for n, (a, b) in enumerate(((1, 0), (0, -1))):
        weight = jnp.where(off == a, 27.0, jnp.where(off == b, -27.0, jnp.where(
            off == a + 1, -1.0, jnp.where(off == b - 1, 1.0, 0.0))))
        band[n] = weight.astype(jnp.bfloat16)

    @pl.when(jnp.logical_not(on_fault))
    def _():
        last_plane[...] = jnp.zeros_like(last_plane)

    source_first()
    loads[0].wait()
    for copy in loads[4:]:
        copy.start()
    yz_send(0, 0)
    yz_send(0, 1)
    x_start(0, 1)
    deep_part(0, 0)
    deep_part(0, 1)
    loads[2].wait()
    loads[3].wait()
    yz_recv(0, 0)
    source_second()
    interior(velocity_pair)
    yz_send(1, 0)
    source_third()
    deep_part(1, 0)
    yz_recv(0, 1)
    edges(0, velocity_pair)
    yz_send(1, 1)
    for copy in loads[4:]:
        copy.wait()
    yz_recv(1, 0)
    interior(stress_pair)
    source_gather()
    source_plane(0, 0)
    source_plane(0, 1)
    apply_source(plane, middle)
    yz_send(2, 0)
    deep_part(1, 1)
    deep_part(2, 0)
    x_wait_send(0)
    yz_recv(1, 1)
    edges(1, stress_pair, plane)
    yz_send(2, 1)
    yz_recv(2, 0)
    interior(velocity_pair)
    yz_send(3, 0)
    deep_part(2, 1)
    deep_part(3, 0)
    source_plane(1, 0)
    x_wait_send(1)
    yz_recv(2, 1)
    edges(2, velocity_pair)
    yz_send(3, 1)
    yz_recv(3, 0)
    interior(stress_pair)
    source_plane(1, 1)
    apply_source(last_plane, middle)
    deep_part(3, 1)
    yz_recv(3, 1)
    x_wait_send(2)
    for h in range(4):
        for part in range(2):
            for there, pair_of in (("k", y_copies(h, part)), ("d", z_copies(h, part))):
                each(has[there + "_up"], [pair_of[0]], lambda c: c.wait_send())
                each(has[there + "_dn"], [pair_of[1]], lambda c: c.wait_send())
    over_groups(lambda g: c_copy(group, g).wait_send())
    pair_copy(parity).wait_send()
    over_fault(lambda h: g_copy(chunk, h).wait_send())
    x_wait_recv(3, 0)
    x_wait_recv(3, 1)
    x_wait_send(3)


def solution(mesh):
    ns, nd, nh = (mesh.shape[a] for a in ("strike", "dip", "depth"))

    def body(velocity, stress, memory, lam, mu, buo, rel, ane, rate, cell, active, offset):
        cx, cy, cz = lam.shape
        subf = cell.shape[1]
        assert cz == 128 and subf == 128 * nd * nh
        planes, rows = cx + 2 * XP, cy + 2 * YP
        f32 = jnp.float32
        block = pltpu.VMEM((cx, cy, cz), f32)
        dma = pltpu.SemaphoreType.DMA
        hbm = pl.BlockSpec(memory_space=pltpu.HBM)
        vmem = pl.BlockSpec(memory_space=pltpu.VMEM)
        between = (
            pltpu.VMEM((6, planes, rows, cz), f32),
            pltpu.VMEM((3, planes, rows, cz), f32),
            pltpu.VMEM((6, cx, cy, cz), f32),
            pltpu.VMEM((3, cx, cy, cz), f32),
            block, block, block, block,
            pltpu.VMEM((6 * cx, cz), f32),
        )
        held = pl.pallas_call(
            functools.partial(kernel, (ns, nd, nh, cx, cy, subf)),
            out_shape=between,
            in_specs=[hbm] * 12,
            out_specs=(vmem,) * 9,
            scratch_shapes=[
                block,
                pltpu.VMEM((6, rate.shape[1], 128), f32),
                pltpu.VMEM(cell.shape, jnp.int32),
                pltpu.SMEM(active.shape, jnp.int32),
                pltpu.SMEM(offset.shape, jnp.int32),
                *[(pltpu.VMEM((4, 64, cz), f32), pltpu.VMEM((4, 24, cz), f32))] * 4,
                *[(pltpu.VMEM((4, 2, cy, cz), f32), pltpu.VMEM((4, 1, cy, cz), f32))] * 3,
                pltpu.VMEM((2, 2 * cz, cz), jnp.bfloat16),
                pltpu.VMEM((ns // NA, STEPS, 8, 128), f32),
                pltpu.VMEM((NA, STEPS, 8, 128), f32),
                pltpu.VMEM((STEPS, 8, 128), f32),
                pltpu.VMEM((nd * nh, STEPS, 8, 128), f32),
                pltpu.VMEM((6 * cx, cz), f32),
                dma((12,)), dma((4, 4)), dma((4, 4)), dma((4, 2, 2)), dma((4, 2, 2)), dma((4, 2, 2)), dma((4, 2, 2)),
                dma((ns // NA,)), dma((ns // NA,)), dma, dma, dma((nh,)), dma((nd * nh,)),
            ],
            compiler_params=pltpu.CompilerParams(
                collective_id=0, has_side_effects=True, vmem_limit_bytes=40 * 1024 * 1024
            ),
            cost_estimate=pl.CostEstimate(flops=30_000_000, bytes_accessed=6_000_000, transcendentals=0),
        )(*(
            pltpu.with_memory_space_constraint(a, pltpu.HBM)
            for a in (velocity, stress, memory, lam, mu, buo, rel, ane, jnp.transpose(rate, (0, 2, 1, 3)), cell, active, offset)
        ))
        return pl.pallas_call(
            functools.partial(finish, (cx, cy)),
            out_shape=tuple(jax.ShapeDtypeStruct(a.shape, f32) for a in (velocity, stress, memory)),
            in_specs=[vmem] * 9,
            out_specs=(hbm,) * 3,
            scratch_shapes=[
                pltpu.VMEM((6, 4, cy, cz), f32),
                pltpu.VMEM((6, 4, cy, cz), f32),
                dma((7,)),
            ],
            compiler_params=pltpu.CompilerParams(vmem_limit_bytes=40 * 1024 * 1024),
            cost_estimate=pl.CostEstimate(flops=2_000_000, bytes_accessed=4_000_000, transcendentals=0),
        )(*held)

    field = P(None, "strike", "dip", "depth")
    cellwise = P("strike", "dip", "depth")
    return jax.shard_map(
        body,
        mesh=mesh,
        in_specs=(field,) * 3 + (cellwise,) * 5 + (P("strike", None, None, None), P(), P(), P()),
        out_specs=(field,) * 3,
        check_vma=False,
    )
```

```python
import functools

import jax
import jax.numpy as jnp
from jax import lax
from jax.experimental import pallas as pl
from jax.experimental.pallas import tpu as pltpu
from jax.sharding import PartitionSpec as P

MESH = pl.DeviceIdType.MESH
TB = 8
STEPS = 2
R24 = 0.12 / 24.0
XP = 2
YP = 8
NA = 2

X_GROUPS = {"s": ((0, 1, 1, 2), (3, 2, 2, 1)), "v": ((0, 1, 2, 1), (1, 2, 1, 2))}
Y_FIELDS = {"s": ((3, True), (5, True), (1, False)), "v": ((1, True), (0, False), (2, False))}
Z_FIELDS = {"s": (4, 5, 2), "v": (0, 1, 2)}
Z_BACK = {"s": (True, True, False), "v": (False, False, True)}


def stress_tiles(x, m, sizes, tiles, Sf, Vf, M, deep, material, put):
    CY, ROW = sizes
    for j in tiles:
        at = (x + XP) * ROW + YP + j
        rows = pl.ds(j, 8)

        def get(c, n, at=at):
            return Vf[c, pl.ds(at + n, 8), :]

        vx = [get(0, n * ROW) for n in range(-2, 3)]
        vy = [get(1, n * ROW) for n in range(-1, 4)]
        vz = [get(2, n * ROW) for n in range(-1, 4)]
        for p in range(2):
            o = p * ROW
            lam, mu, relax, ane = material(m + p, rows)
            shear = R24 * mu
            twice = 2.0 * shear
            part = (1.0 - relax) * ane
            vx_at, vy_at, vz_at = vx[2 + p], vy[1 + p], vz[1 + p]
            xx = 27.0 * (vx_at - vx[1 + p]) - (vx[3 + p] - vx[p])
            yy = 27.0 * (vy_at - get(1, o - 1)) - (get(1, o + 1) - get(1, o - 2))
            zz = deep[2, x + p, rows, :]
            normal = R24 * lam * (xx + yy + zz)
            xy = 27.0 * ((get(0, o + 1) - vx_at) + (vy[2 + p] - vy_at)) - (
                (get(0, o + 2) - get(0, o - 1)) + (vy[3 + p] - vy[p]))
            xz = 27.0 * (vz[2 + p] - vz_at) - (vz[3 + p] - vz[p]) + deep[0, x + p, rows, :]
            yz = 27.0 * (get(2, o + 1) - vz_at) - (get(2, o + 2) - get(2, o - 1)) + deep[1, x + p, rows, :]
            grown = (
                normal + twice * xx, normal + twice * yy, normal + twice * zz,
                shear * xy, shear * xz, shear * yz,
            )
            for c in range(6):
                old = M[c, x + p, rows, :]
                new = relax * old + part * grown[c]
                stress = Sf[c, pl.ds(pl.multiple_of(at + o, 8), 8), :] + grown[c] - 0.5 * (old + new)
                put(c, x + p, at + o, rows, stress, new)


def finish(dims, S, V, M, deep, lam, mu, rel, ane, plane, vel_out, str_out, mem_out, stress, memory, sem):
    CX, CY = dims
    ROW = CY + 2 * YP
    own = pl.ds(YP, CY)
    middle = pl.ds(2, CX - 4)
    copies = [
        pltpu.make_async_copy(V.at[:, pl.ds(XP, CX), own], vel_out, sem.at[0]),
        pltpu.make_async_copy(S.at[:, pl.ds(XP + 2, CX - 4), own], str_out.at[:, middle], sem.at[1]),
        pltpu.make_async_copy(M.at[:, middle], mem_out.at[:, middle], sem.at[2]),
    ]
    for copy in copies:
        copy.start()
    Sf = S.reshape(6, (CX + 2 * XP) * ROW, 128)
    Vf = V.reshape(3, (CX + 2 * XP) * ROW, 128)

    @pl.loop(0, 2)
    def _(i):
        x = i * (CX - 2)

        def material(m, rows):
            return tuple(ref[m, rows, :] for ref in (lam, mu, rel, ane))

        def put(c, at_x, at, rows, s, m):
            place = at_x - i * (CX - 4)
            stress[c, place, rows, :] = s
            memory[c, place, rows, :] = m

        stress_tiles(x, x, (CY, ROW), range(0, CY, 8), Sf, Vf, M, deep, material, put)

    for c in range(6):
        for n, x in enumerate((0, 1, CX - 2, CX - 1)):
            stress[c, n, 0:1, :] = stress[c, n, 0:1, :] - plane[c * CX + x:c * CX + x + 1, :]
    for n in range(2):
        here, there = pl.ds(2 * n, 2), pl.ds(n * (CX - 2), 2)
        copies.append(pltpu.make_async_copy(stress.at[:, here], str_out.at[:, there], sem.at[3 + 2 * n]))
        copies.append(pltpu.make_async_copy(memory.at[:, here], mem_out.at[:, there], sem.at[4 + 2 * n]))
    for copy in copies[3:]:
        copy.start()
    for copy in copies:
        copy.wait()


def kernel(
    dims,
    vel_hbm, str_hbm, mem_hbm, lam_hbm, mu_hbm, buo_hbm, rel_hbm, ane_hbm, rate_hbm, cell_hbm,
    active_hbm, offset_hbm,
    S, V, M, deep, lam, mu, rel, ane, last_plane,
    buo, rate, cells, active, offset,
    ysend_up, ysend_dn, yrecv_up, yrecv_dn, zsend, zrecv_up, zrecv_dn, band,
    cand, pair, chosen, gathered, plane,
    ld_sem, xs_sem, xr_sem, ys_sem, yr_sem, zs_sem, zr_sem,
    c_send, c_recv, p_send, p_recv, g_send, g_recv,
):
    NS, ND, NH, CX, CY, SUBF = dims
    ROW = CY + 2 * YP
    NB = NS // NA
    s = lax.axis_index("strike")
    k = lax.axis_index("dip")
    d = lax.axis_index("depth")
    fault = ND // 2
    on_fault = k == fault
    group, parity = lax.div(s, NA), lax.rem(s, NA)
    chunk = k * NH + d

    def near(axis, pos, size, step):
        return {axis: jnp.clip(pos + step, 0, size - 1)}

    s_up, s_dn = near("strike", s, NS, 1), near("strike", s, NS, -1)
    k_up, k_dn = near("dip", k, ND, 1), near("dip", k, ND, -1)
    d_up, d_dn = near("depth", d, NH, 1), near("depth", d, NH, -1)
    has = {
        "s_up": s < NS - 1, "s_dn": s > 0,
        "k_up": k < ND - 1, "k_dn": k > 0,
        "d_up": d < NH - 1, "d_dn": d > 0,
    }

    barrier = pltpu.get_barrier_semaphore()
    count = jnp.int32(0)
    for name, to in (("s_up", s_up), ("s_dn", s_dn), ("k_up", k_up), ("k_dn", k_dn), ("d_up", d_up), ("d_dn", d_dn)):
        there = has[name]
        count = count + there.astype(jnp.int32)

        @pl.when(there)
        def _(to=to):
            pl.semaphore_signal(barrier, inc=1, device_id=to, device_id_type=MESH)

    other = {"strike": group * NA + lax.rem(parity + 1, NA)}

    @pl.loop(0, NB)
    def _(g):
        @pl.when(g != group)
        def _():
            pl.semaphore_signal(
                barrier, inc=1, device_id={"strike": g * NA + parity}, device_id_type=MESH
            )

    count = count + (NB - 1)

    count = count + NH - on_fault.astype(jnp.int32)

    @pl.when(on_fault)
    def _():
        @pl.loop(0, ND * NH)
        def _(j):
            @pl.when(j != chunk)
            def _():
                pl.semaphore_signal(
                    barrier, inc=1,
                    device_id={"dip": lax.div(j, NH), "depth": lax.rem(j, NH)},
                    device_id_type=MESH,
                )

    inner = (slice(None), pl.ds(XP, CX), pl.ds(YP, CY))
    loads = [
        pltpu.make_async_copy(str_hbm, S.at[inner], ld_sem.at[0]),
        pltpu.make_async_copy(
            rate_hbm.at[0, :, :, pl.ds(pl.multiple_of(chunk * 128, 128), 128)], rate, ld_sem.at[1]
        ),
        pltpu.make_async_copy(vel_hbm, V.at[inner], ld_sem.at[2]),
        pltpu.make_async_copy(buo_hbm, buo, ld_sem.at[3]),
        pltpu.make_async_copy(mem_hbm, M, ld_sem.at[4]),
        pltpu.make_async_copy(lam_hbm, lam, ld_sem.at[5]),
        pltpu.make_async_copy(mu_hbm, mu, ld_sem.at[6]),
        pltpu.make_async_copy(rel_hbm, rel, ld_sem.at[7]),
        pltpu.make_async_copy(ane_hbm, ane, ld_sem.at[8]),
        pltpu.make_async_copy(cell_hbm, cells, ld_sem.at[9]),
    ]
    order = (
        pltpu.make_async_copy(active_hbm, active, ld_sem.at[10]),
        pltpu.make_async_copy(offset_hbm, offset, ld_sem.at[11]),
    )
    for copy in (loads[1], *order, loads[0], loads[2], loads[3]):
        copy.start()

    pl.semaphore_wait(barrier, count)

    def x_copies(h):
        kind = "sv"[h % 2]
        ref = S if kind == "s" else V
        up, dn = [], []
        for n, (c0, nc, lu, ld) in enumerate(X_GROUPS[kind]):
            comps = pl.ds(c0, nc)
            rows = pl.ds(YP, CY)
            if h == 0:
                src_up = str_hbm.at[comps, pl.ds(CX - lu, lu)]
                src_dn = str_hbm.at[comps, pl.ds(0, ld)]
            else:
                src_up = ref.at[comps, pl.ds(XP + CX - lu, lu), rows]
                src_dn = ref.at[comps, pl.ds(XP, ld), rows]
            up.append(pltpu.make_async_remote_copy(
                src_up, ref.at[comps, pl.ds(XP - lu, lu), rows],
                xs_sem.at[h, n], xr_sem.at[h, n], device_id=s_up, device_id_type=MESH))
            dn.append(pltpu.make_async_remote_copy(
                src_dn, ref.at[comps, pl.ds(XP + CX, ld), rows],
                xs_sem.at[h, 2 + n], xr_sem.at[h, 2 + n], device_id=s_dn, device_id_type=MESH))
        return up, dn

    def each(there, copies, act):
        @pl.when(there)
        def _():
            for copy in copies:
                act(copy)

    def x_start(h, side):
        there = has["s_up"] if side == 0 else has["s_dn"]
        each(there, x_copies(h)[side], lambda c: c.start())

    def x_wait_recv(h, side):
        there = has["s_dn"] if side == 0 else has["s_up"]
        each(there, x_copies(h)[side], lambda c: c.wait_recv())

    def x_wait_send(h):
        up, dn = x_copies(h)
        each(has["s_up"], up, lambda c: c.wait_send())
        each(has["s_dn"], dn, lambda c: c.wait_send())

    x_start(0, 0)

    Sf = S.reshape(6, (CX + 2 * XP) * ROW, 128)
    Vf = V.reshape(3, (CX + 2 * XP) * ROW, 128)
    flat = {"s": Sf, "v": Vf}

    for F, nc in ((S, 6), (V, 3)):
        zero_x = jnp.zeros((nc, XP, CY, 128), jnp.float32)

        @pl.when(s == 0)
        def _(F=F, zero_x=zero_x):
            F[:, 0:XP, YP:YP + CY, :] = zero_x

        @pl.when(s == NS - 1)
        def _(F=F, zero_x=zero_x):
            F[:, XP + CX:, YP:YP + CY, :] = zero_x

    for there, refs in (
        (has["k_dn"], yrecv_up), (has["k_up"], yrecv_dn), (has["d_dn"], zrecv_up), (has["d_up"], zrecv_dn),
    ):
        @pl.when(jnp.logical_not(there))
        def _(refs=refs):
            for ref in refs:
                ref[...] = jnp.zeros(ref.shape, jnp.float32)

    for refs in (ysend_up, ysend_dn):
        for ref in refs:
            ref[:, ref.shape[1] - 8:, :] = jnp.zeros((4, 8, 128), jnp.float32)

    def y_layers(kind):
        up, dn = [], []
        for c, back in Y_FIELDS[kind]:
            up += [(c, CY - 2), (c, CY - 1)] if back else [(c, CY - 1)]
            dn += [(c, 0)] if back else [(c, 0), (c, 1)]
        return up, dn

    PLANES = (tuple(range(2, CX - 2)), (0, 1, CX - 2, CX - 1))
    SPANS = (((2, CX - 4),), ((0, 2), (CX - 2, 2)))

    def y_copies(h, part):
        size = len(PLANES[part])
        nu, nd = (-(-len(layers) * size // 8) * 8 for layers in y_layers("sv"[h % 2]))
        return (
            pltpu.make_async_remote_copy(
                ysend_up[part].at[h, pl.ds(0, nu)], yrecv_up[part].at[h, pl.ds(0, nu)],
                ys_sem.at[h, part, 0], yr_sem.at[h, part, 0], device_id=k_up, device_id_type=MESH),
            pltpu.make_async_remote_copy(
                ysend_dn[part].at[h, pl.ds(0, nd)], yrecv_dn[part].at[h, pl.ds(0, nd)],
                ys_sem.at[h, part, 1], yr_sem.at[h, part, 1], device_id=k_dn, device_id_type=MESH),
        )

    def z_copies(h, part):
        return (
            pltpu.make_async_remote_copy(
                zsend[part].at[h], zrecv_up[part].at[h],
                zs_sem.at[h, part, 0], zr_sem.at[h, part, 0], device_id=d_up, device_id_type=MESH),
            pltpu.make_async_remote_copy(
                zsend[part].at[h], zrecv_dn[part].at[h],
                zs_sem.at[h, part, 1], zr_sem.at[h, part, 1], device_id=d_dn, device_id_type=MESH),
        )

    lane = lax.broadcasted_iota(jnp.int32, (CY, 128), 1)
    slot = lane >> 2
    quarter = lane & 3

    def turn(value, n):
        return pltpu.roll(value, n % 128, 1)

    def z_slot(part, place, n):
        if part == 0:
            return place // 2, n + 16 * (place % 2)
        return 0, n + 4 * place

    def yz_send(h, part):
        kind = "sv"[h % 2]
        F = flat[kind]
        base = XP * ROW + YP
        for layers, refs in zip(y_layers(kind), (ysend_up, ysend_dn)):
            at = 0
            for c, row in layers:
                for x0, n in SPANS[part]:
                    refs[part][h, at:at + n, :] = F[c, pl.ds(base + x0 * ROW + row, n, stride=ROW), :]
                    at += n
        up, dn = y_copies(h, part)
        each(has["k_up"], [up], lambda c: c.start())
        each(has["k_dn"], [dn], lambda c: c.start())
        arrays = [jnp.zeros((CY, 128), jnp.float32)] * (2 - part)
        for place, comp in enumerate(Z_FIELDS[kind]):
            for n, x in enumerate(PLANES[part]):
                where, index = z_slot(part, place, n)
                value = F[comp, pl.ds((x + XP) * ROW + YP, CY), :]
                arrays[where] = jnp.where(slot == index, turn(value, 4 * index + 2), arrays[where])
        for n, value in enumerate(arrays):
            zsend[part][h, n] = value
        up, dn = z_copies(h, part)
        each(has["d_up"], [up], lambda c: c.start())
        each(has["d_dn"], [dn], lambda c: c.start())

    def yz_recv(h, part):
        kind = "sv"[h % 2]
        F = flat[kind]
        up, dn = y_copies(h, part)
        each(has["k_dn"], [up], lambda c: c.wait_recv())
        each(has["k_up"], [dn], lambda c: c.wait_recv())
        base = XP * ROW + YP
        for layers, refs, shift in zip(y_layers(kind), (yrecv_up, yrecv_dn), (-CY, CY)):
            at = 0
            for c, row in layers:
                for x0, n in SPANS[part]:
                    F[c, pl.ds(base + x0 * ROW + row + shift, n, stride=ROW), :] = refs[part][h, at:at + n, :]
                    at += n
        up, dn = z_copies(h, part)
        each(has["d_dn"], [up], lambda c: c.wait_recv())
        each(has["d_up"], [dn], lambda c: c.wait_recv())
        fixes = {}
        for place, back in enumerate(Z_BACK[kind]):
            ends = (lane == 127) | (lane < 2) if back else (lane > 125) | (lane == 0)
            for n, x in enumerate(PLANES[part]):
                where, index = z_slot(part, place, n)
                if (where, back) not in fixes:
                    mix = jnp.where(quarter < 2, zrecv_up[part][h, where], zrecv_dn[part][h, where])
                    below, two_after = turn(mix, 1), turn(mix, -2)
                    if back:
                        fix = jnp.where(quarter == 0, -two_after, jnp.where(quarter == 1, below - 27.0 * mix, below))
                    else:
                        fix = jnp.where(quarter == 1, 27.0 * turn(mix, -1) - two_after, jnp.where(quarter == 0, -two_after, below))
                    fixes[where, back] = jnp.where(quarter == 3, 0.0, fix)
                moved = turn(fixes[where, back], (127 if back else 126) - 4 * index)
                deep[place, x] = deep[place, x] + jnp.where(ends, moved, 0.0)

    def deep_part(h, part):
        kind = "sv"[h % 2]
        F = S if kind == "s" else V
        for place, (comp, back) in enumerate(zip(Z_FIELDS[kind], Z_BACK[kind])):
            f = jnp.concatenate(
                [F[comp, XP + x0:XP + x0 + n, YP:YP + CY, :].reshape(n * CY, 128) for x0, n in SPANS[part]], axis=0)
            high = f.astype(jnp.bfloat16)
            low = (f - high.astype(jnp.float32)).astype(jnp.bfloat16)
            out = lax.dot_general(
                jnp.concatenate([high, low], axis=1), band[1 if back else 0],
                (((1,), (0,)), ((), ())), preferred_element_type=jnp.float32)
            at = 0
            for x0, n in SPANS[part]:
                deep[place, x0:x0 + n] = out[at:at + n * CY].reshape(n, CY, 128)
                at += n * CY

    def velocity_pair(x, tiles):
        for j in tiles:
            at = (x + XP) * ROW + YP + j

            def get(c, n, Sf=Sf, at=at):
                return Sf[c, pl.ds(at + n, 8), :]

            xx = [get(0, n * ROW) for n in range(-1, 4)]
            xy = [get(3, n * ROW) for n in range(-2, 3)]
            xz = [get(4, n * ROW) for n in range(-2, 3)]
            for p in range(2):
                o = p * ROW
                gain = R24 * buo[x + p, pl.ds(j, 8), :]
                xy_at, yy, yz = xy[2 + p], [get(1, o + n) for n in range(-1, 3)], [get(5, o + n) for n in range(-2, 2)]
                close = (
                    (xx[2 + p] - xx[1 + p]) + (xy_at - get(3, o - 1)),
                    (xy_at - xy[1 + p]) + (yy[2] - yy[1]),
                    (xz[2 + p] - xz[1 + p]) + (yz[2] - yz[1]),
                )
                far = (
                    (xx[3 + p] - xx[p]) + (get(3, o + 1) - get(3, o - 2)),
                    (xy[3 + p] - xy[p]) + (yy[3] - yy[0]),
                    (xz[3 + p] - xz[p]) + (yz[3] - yz[0]),
                )
                for c in range(3):
                    own = pl.ds(pl.multiple_of(at + o, 8), 8)
                    Vf[c, own, :] = Vf[c, own, :] + gain * (
                        27.0 * close[c] - far[c] + deep[c, x + p, pl.ds(j, 8), :])

    def stress_pair(x, tiles):
        def material(x, rows):
            return lam[x, rows, :], mu[x, rows, :], rel[x, rows, :], ane[x, rows, :]

        def put(c, x, at, rows, stress, memory):
            Sf[c, pl.ds(pl.multiple_of(at, 8), 8), :] = stress
            M[c, x, rows, :] = memory

        stress_tiles(x, x, (CY, ROW), tiles, Sf, Vf, M, deep, material, put)

    def interior(one):
        @pl.loop(0, (CX - 4) // 2)
        def _(i):
            one(2 * i + 2, range(0, CY, 8))

    nought = jnp.minimum(s, 0)

    def edges(h, one, source=None):
        sides = ((0, 0), (1, CX - 2))
        for side, x in sides if h % 2 == 0 else sides[::-1]:
            x_wait_recv(h, side)
            one(nought + x, range(0, CY, 8))
            if source is not None:
                apply_source(source, ((x, 2),))
            x_start(h + 1, 1 - side)

    def candidates():
        row = lax.broadcasted_iota(jnp.int32, (TB, 128), 0)
        weights = jnp.where((row == 0) | (row == TB - 1), 0.5 / (TB - 1), 1.0 / (TB - 1))
        for t in range(STEPS):
            o = offset[t]
            for c in range(6):
                samples = rate[c, pl.ds(o, TB), :]
                cand[group, t, c:c + 1, :] = jnp.sum(samples * weights, axis=0, keepdims=True)
            cand[group, t, 6:8, :] = jnp.zeros((2, 128), jnp.float32)

    def c_copy(sender, receiver):
        return pltpu.make_async_remote_copy(
            cand.at[sender], cand.at[sender], c_send.at[receiver], c_recv.at[sender],
            device_id={"strike": receiver * NA + parity}, device_id_type=MESH)

    def over_groups(act):
        @pl.loop(0, NB)
        def _(g):
            @pl.when(g != group)
            def _():
                act(g)

    def pair_copy(which):
        return pltpu.make_async_remote_copy(
            pair.at[which], pair.at[which], p_send, p_recv, device_id=other, device_id_type=MESH)

    def g_copy(which, h):
        return pltpu.make_async_remote_copy(
            chosen, gathered.at[which], g_send.at[h], g_recv.at[which],
            device_id={"dip": fault, "depth": h}, device_id_type=MESH)

    def over_fault(act):
        @pl.loop(0, NH)
        def _(h):
            @pl.when(jnp.logical_not(on_fault & (h == d)))
            def _():
                act(h)

    def source_first():
        loads[1].wait()
        for copy in order:
            copy.wait()
        candidates()
        over_groups(lambda g: c_copy(group, g).start())

    def source_second():
        over_groups(lambda g: c_copy(g, group).wait_recv())
        for t in range(STEPS):
            pair[parity, t] = cand[lax.div(active[t], NA), t]
        pair_copy(parity).start()

    def source_third():
        pair_copy(lax.rem(parity + 1, NA)).wait_recv()
        for t in range(STEPS):
            value = pair[lax.rem(active[t], NA), t]
            chosen[t] = value

            @pl.when(on_fault)
            def _(t=t, value=value):
                gathered[chunk, t] = value

        over_fault(lambda h: g_copy(chunk, h).start())

    def source_gather():
        @pl.when(on_fault)
        def _():
            @pl.loop(0, ND * NH)
            def _(j):
                @pl.when(j != chunk)
                def _():
                    g_copy(j, 0).wait_recv()

    def source_plane(t, piece):
        @pl.when(on_fault)
        def _():
            seg = active[t]
            depth_total = 128 * NH
            wide = SUBF // 2
            cell = cells[pl.ds(seg, 1), piece * wide:(piece + 1) * wide]
            cell_x = lax.div(cell, depth_total)
            cell_z = cell - cell_x * depth_total - d * 128
            cell_x = cell_x - s * CX
            hot_z = (lax.broadcasted_iota(jnp.int32, (128, wide), 0) == cell_z).astype(jnp.float32).astype(jnp.bfloat16)
            hot_x = lax.broadcasted_iota(jnp.int32, (CX, wide), 0) == cell_x
            first = piece * wide // 128
            value = jnp.concatenate([gathered[first + n, t] for n in range(wide // 128)], axis=1)
            high = value.astype(jnp.bfloat16).astype(jnp.float32)
            rows = [
                jnp.where(hot_x, part[c:c + 1, :], 0.0).astype(jnp.bfloat16)
                for part in (high, value - high) for c in range(6)
            ]
            out = lax.dot_general(
                jnp.concatenate(rows, axis=0), hot_z, (((1,), (1,)), ((), ())),
                preferred_element_type=jnp.float32)
            n = 6 * CX
            out = out[0:n] + out[n:2 * n]
            ref = plane if t == 0 else last_plane
            if piece == 0:
                ref[...] = out
            else:
                ref[...] = ref[...] + out

    def apply_source(ref, spans):
        @pl.when(on_fault)
        def _():
            for c in range(6):
                for x0, n in spans:
                    at = pl.ds((x0 + XP) * ROW + YP, n, stride=ROW)
                    Sf[c, at, :] = Sf[c, at, :] - ref[c * CX + x0:c * CX + x0 + n, :]

    middle = ((2, CX - 4),)

    i, j = (lax.broadcasted_iota(jnp.int32, (256, 128), n) for n in range(2))
    off = (i & 127) - j
    for n, (a, b) in enumerate(((1, 0), (0, -1))):
        weight = jnp.where(off == a, 27.0, jnp.where(off == b, -27.0, jnp.where(
            off == a + 1, -1.0, jnp.where(off == b - 1, 1.0, 0.0))))
        band[n] = weight.astype(jnp.bfloat16)

    @pl.when(jnp.logical_not(on_fault))
    def _():
        last_plane[...] = jnp.zeros_like(last_plane)

    source_first()
    loads[0].wait()
    for copy in loads[4:]:
        copy.start()
    yz_send(0, 0)
    yz_send(0, 1)
    x_start(0, 1)
    deep_part(0, 0)
    deep_part(0, 1)
    loads[2].wait()
    loads[3].wait()
    yz_recv(0, 0)
    source_second()
    interior(velocity_pair)
    yz_send(1, 0)
    source_third()
    deep_part(1, 0)
    yz_recv(0, 1)
    edges(0, velocity_pair)
    yz_send(1, 1)
    for copy in loads[4:]:
        copy.wait()
    yz_recv(1, 0)
    interior(stress_pair)
    source_gather()
    source_plane(0, 0)
    source_plane(0, 1)
    apply_source(plane, middle)
    yz_send(2, 0)
    deep_part(1, 1)
    deep_part(2, 0)
    x_wait_send(0)
    yz_recv(1, 1)
    edges(1, stress_pair, plane)
    yz_send(2, 1)
    yz_recv(2, 0)
    interior(velocity_pair)
    yz_send(3, 0)
    deep_part(2, 1)
    deep_part(3, 0)
    source_plane(1, 0)
    x_wait_send(1)
    yz_recv(2, 1)
    edges(2, velocity_pair)
    yz_send(3, 1)
    yz_recv(3, 0)
    interior(stress_pair)
    source_plane(1, 1)
    apply_source(last_plane, middle)
    deep_part(3, 1)
    yz_recv(3, 1)
    x_wait_send(2)
    for h in range(4):
        for part in range(2):
            for there, pair_of in (("k", y_copies(h, part)), ("d", z_copies(h, part))):
                each(has[there + "_up"], [pair_of[0]], lambda c: c.wait_send())
                each(has[there + "_dn"], [pair_of[1]], lambda c: c.wait_send())
    over_groups(lambda g: c_copy(group, g).wait_send())
    pair_copy(parity).wait_send()
    over_fault(lambda h: g_copy(chunk, h).wait_send())
    x_wait_recv(3, 0)
    x_wait_recv(3, 1)
    x_wait_send(3)


def solution(mesh):
    ns, nd, nh = (mesh.shape[a] for a in ("strike", "dip", "depth"))

    def body(velocity, stress, memory, lam, mu, buo, rel, ane, rate, cell, active, offset):
        cx, cy, cz = lam.shape
        subf = cell.shape[1]
        assert cz == 128 and subf == 128 * nd * nh
        planes, rows = cx + 2 * XP, cy + 2 * YP
        f32 = jnp.float32
        block = pltpu.VMEM((cx, cy, cz), f32)
        dma = pltpu.SemaphoreType.DMA
        hbm = pl.BlockSpec(memory_space=pltpu.HBM)
        vmem = pl.BlockSpec(memory_space=pltpu.VMEM)
        between = (
            pltpu.VMEM((6, planes, rows, cz), f32),
            pltpu.VMEM((3, planes, rows, cz), f32),
            pltpu.VMEM((6, cx, cy, cz), f32),
            pltpu.VMEM((3, cx, cy, cz), f32),
            block, block, block, block,
            pltpu.VMEM((6 * cx, cz), f32),
        )
        held = pl.pallas_call(
            functools.partial(kernel, (ns, nd, nh, cx, cy, subf)),
            out_shape=between,
            in_specs=[hbm] * 12,
            out_specs=(vmem,) * 9,
            scratch_shapes=[
                block,
                pltpu.VMEM((6, rate.shape[1], 128), f32),
                pltpu.VMEM(cell.shape, jnp.int32),
                pltpu.SMEM(active.shape, jnp.int32),
                pltpu.SMEM(offset.shape, jnp.int32),
                *[(pltpu.VMEM((4, 64, cz), f32), pltpu.VMEM((4, 24, cz), f32))] * 4,
                *[(pltpu.VMEM((4, 2, cy, cz), f32), pltpu.VMEM((4, 1, cy, cz), f32))] * 3,
                pltpu.VMEM((2, 2 * cz, cz), jnp.bfloat16),
                pltpu.VMEM((ns // NA, STEPS, 8, 128), f32),
                pltpu.VMEM((NA, STEPS, 8, 128), f32),
                pltpu.VMEM((STEPS, 8, 128), f32),
                pltpu.VMEM((nd * nh, STEPS, 8, 128), f32),
                pltpu.VMEM((6 * cx, cz), f32),
                dma((12,)), dma((4, 4)), dma((4, 4)), dma((4, 2, 2)), dma((4, 2, 2)), dma((4, 2, 2)), dma((4, 2, 2)),
                dma((ns // NA,)), dma((ns // NA,)), dma, dma, dma((nh,)), dma((nd * nh,)),
            ],
            compiler_params=pltpu.CompilerParams(
                collective_id=0, has_side_effects=True, vmem_limit_bytes=40 * 1024 * 1024
            ),
            cost_estimate=pl.CostEstimate(flops=30_000_000, bytes_accessed=6_000_000, transcendentals=0),
        )(*(
            pltpu.with_memory_space_constraint(a, pltpu.HBM)
            for a in (velocity, stress, memory, lam, mu, buo, rel, ane, jnp.transpose(rate, (0, 2, 1, 3)), cell, active, offset)
        ))
        return pl.pallas_call(
            functools.partial(finish, (cx, cy)),
            out_shape=tuple(jax.ShapeDtypeStruct(a.shape, f32) for a in (velocity, stress, memory)),
            in_specs=[vmem] * 9,
            out_specs=(hbm,) * 3,
            scratch_shapes=[
                pltpu.VMEM((6, 4, cy, cz), f32),
                pltpu.VMEM((6, 4, cy, cz), f32),
                dma((7,)),
            ],
            compiler_params=pltpu.CompilerParams(vmem_limit_bytes=40 * 1024 * 1024),
            cost_estimate=pl.CostEstimate(flops=2_000_000, bytes_accessed=4_000_000, transcendentals=0),
        )(*held)

    field = P(None, "strike", "dip", "depth")
    cellwise = P("strike", "dip", "depth")
    return jax.shard_map(
        body,
        mesh=mesh,
        in_specs=(field,) * 3 + (cellwise,) * 5 + (P("strike", None, None, None), P(), P(), P()),
        out_specs=(field,) * 3,
        check_vma=False,
    )
```

```python
import functools

import jax
import jax.numpy as jnp
from jax import lax
from jax.experimental import pallas as pl
from jax.experimental.pallas import tpu as pltpu
from jax.sharding import PartitionSpec as P

MESH = pl.DeviceIdType.MESH
TB = 8
STEPS = 2
R24 = 0.12 / 24.0
XP = 2
YP = 8
NA = 2

X_GROUPS = {"s": ((0, 1, 1, 2), (3, 2, 2, 1)), "v": ((0, 1, 2, 1), (1, 2, 1, 2))}
Y_FIELDS = {"s": ((3, True), (5, True), (1, False)), "v": ((1, True), (0, False), (2, False))}
Z_FIELDS = {"s": (4, 5, 2), "v": (0, 1, 2)}
Z_BACK = {"s": (True, True, False), "v": (False, False, True)}


def stress_tiles(x, m, sizes, tiles, Sf, Vf, M, deep, material, put):
    CY, ROW = sizes
    for j in tiles:
        at = (x + XP) * ROW + YP + j
        rows = pl.ds(j, 8)

        def get(c, n, at=at):
            return Vf[c, pl.ds(at + n, 8), :]

        vx = [get(0, n * ROW) for n in range(-2, 3)]
        vy = [get(1, n * ROW) for n in range(-1, 4)]
        vz = [get(2, n * ROW) for n in range(-1, 4)]
        for p in range(2):
            o = p * ROW
            lam, mu, relax, ane = material(m + p, rows)
            shear = R24 * mu
            twice = 2.0 * shear
            part = (1.0 - relax) * ane
            vx_at, vy_at, vz_at = vx[2 + p], vy[1 + p], vz[1 + p]
            xx = 27.0 * (vx_at - vx[1 + p]) - (vx[3 + p] - vx[p])
            yy = 27.0 * (vy_at - get(1, o - 1)) - (get(1, o + 1) - get(1, o - 2))
            zz = deep[2, x + p, rows, :]
            normal = R24 * lam * (xx + yy + zz)
            xy = 27.0 * ((get(0, o + 1) - vx_at) + (vy[2 + p] - vy_at)) - (
                (get(0, o + 2) - get(0, o - 1)) + (vy[3 + p] - vy[p]))
            xz = 27.0 * (vz[2 + p] - vz_at) - (vz[3 + p] - vz[p]) + deep[0, x + p, rows, :]
            yz = 27.0 * (get(2, o + 1) - vz_at) - (get(2, o + 2) - get(2, o - 1)) + deep[1, x + p, rows, :]
            grown = (
                normal + twice * xx, normal + twice * yy, normal + twice * zz,
                shear * xy, shear * xz, shear * yz,
            )
            for c in range(6):
                old = M[c, x + p, rows, :]
                new = relax * old + part * grown[c]
                stress = Sf[c, pl.ds(pl.multiple_of(at + o, 8), 8), :] + grown[c] - 0.5 * (old + new)
                put(c, x + p, at + o, rows, stress, new)


def finish(dims, S, V, M, deep, lam, mu, rel, ane, plane, vel_out, str_out, mem_out, stress, memory, sem):
    CX, CY = dims
    ROW = CY + 2 * YP
    own = pl.ds(YP, CY)
    middle = pl.ds(2, CX - 4)
    copies = [
        pltpu.make_async_copy(V.at[:, pl.ds(XP, CX), own], vel_out, sem.at[0]),
        pltpu.make_async_copy(S.at[:, pl.ds(XP + 2, CX - 4), own], str_out.at[:, middle], sem.at[1]),
        pltpu.make_async_copy(M.at[:, middle], mem_out.at[:, middle], sem.at[2]),
    ]
    for copy in copies:
        copy.start()
    Sf = S.reshape(6, (CX + 2 * XP) * ROW, 128)
    Vf = V.reshape(3, (CX + 2 * XP) * ROW, 128)

    @pl.loop(0, 2)
    def _(i):
        x = i * (CX - 2)

        def material(m, rows):
            return tuple(ref[m, rows, :] for ref in (lam, mu, rel, ane))

        def put(c, at_x, at, rows, s, m):
            place = at_x - i * (CX - 4)
            stress[c, place, rows, :] = s
            memory[c, place, rows, :] = m

        stress_tiles(x, x, (CY, ROW), range(0, CY, 8), Sf, Vf, M, deep, material, put)

    for c in range(6):
        for n, x in enumerate((0, 1, CX - 2, CX - 1)):
            stress[c, n, 0:1, :] = stress[c, n, 0:1, :] - plane[c * CX + x:c * CX + x + 1, :]
    for n in range(2):
        here, there = pl.ds(2 * n, 2), pl.ds(n * (CX - 2), 2)
        copies.append(pltpu.make_async_copy(stress.at[:, here], str_out.at[:, there], sem.at[3 + 2 * n]))
        copies.append(pltpu.make_async_copy(memory.at[:, here], mem_out.at[:, there], sem.at[4 + 2 * n]))
    for copy in copies[3:]:
        copy.start()
    for copy in copies:
        copy.wait()


def kernel(
    dims,
    vel_hbm, str_hbm, mem_hbm, lam_hbm, mu_hbm, buo_hbm, rel_hbm, ane_hbm, rate_hbm, cell_hbm,
    active_hbm, offset_hbm,
    S, V, M, deep, lam, mu, rel, ane, last_plane,
    buo, rate, cells, active, offset,
    ysend_up, ysend_dn, yrecv_up, yrecv_dn, zsend, zrecv_up, zrecv_dn, band,
    cand, pair, chosen, gathered, plane,
    ld_sem, xs_sem, xr_sem, ys_sem, yr_sem, zs_sem, zr_sem,
    c_send, c_recv, p_send, p_recv, g_send, g_recv,
):
    NS, ND, NH, CX, CY, SUBF = dims
    ROW = CY + 2 * YP
    NB = NS // NA
    s = lax.axis_index("strike")
    k = lax.axis_index("dip")
    d = lax.axis_index("depth")
    fault = ND // 2
    on_fault = k == fault
    group, parity = lax.div(s, NA), lax.rem(s, NA)
    chunk = k * NH + d

    def near(axis, pos, size, step):
        return {axis: jnp.clip(pos + step, 0, size - 1)}

    s_up, s_dn = near("strike", s, NS, 1), near("strike", s, NS, -1)
    k_up, k_dn = near("dip", k, ND, 1), near("dip", k, ND, -1)
    d_up, d_dn = near("depth", d, NH, 1), near("depth", d, NH, -1)
    has = {
        "s_up": s < NS - 1, "s_dn": s > 0,
        "k_up": k < ND - 1, "k_dn": k > 0,
        "d_up": d < NH - 1, "d_dn": d > 0,
    }

    barrier = pltpu.get_barrier_semaphore()
    count = jnp.int32(0)
    for name, to in (("s_up", s_up), ("s_dn", s_dn), ("k_up", k_up), ("k_dn", k_dn), ("d_up", d_up), ("d_dn", d_dn)):
        there = has[name]
        count = count + there.astype(jnp.int32)

        @pl.when(there)
        def _(to=to):
            pl.semaphore_signal(barrier, inc=1, device_id=to, device_id_type=MESH)

    other = {"strike": group * NA + lax.rem(parity + 1, NA)}

    @pl.loop(0, NB)
    def _(g):
        @pl.when(g != group)
        def _():
            pl.semaphore_signal(
                barrier, inc=1, device_id={"strike": g * NA + parity}, device_id_type=MESH
            )

    count = count + (NB - 1)

    count = count + NH - on_fault.astype(jnp.int32)

    @pl.when(on_fault)
    def _():
        @pl.loop(0, ND * NH)
        def _(j):
            @pl.when(j != chunk)
            def _():
                pl.semaphore_signal(
                    barrier, inc=1,
                    device_id={"dip": lax.div(j, NH), "depth": lax.rem(j, NH)},
                    device_id_type=MESH,
                )

    inner = (slice(None), pl.ds(XP, CX), pl.ds(YP, CY))
    loads = [
        pltpu.make_async_copy(str_hbm, S.at[inner], ld_sem.at[0]),
        pltpu.make_async_copy(
            rate_hbm.at[0, :, :, pl.ds(pl.multiple_of(chunk * 128, 128), 128)], rate, ld_sem.at[1]
        ),
        pltpu.make_async_copy(vel_hbm, V.at[inner], ld_sem.at[2]),
        pltpu.make_async_copy(buo_hbm, buo, ld_sem.at[3]),
        pltpu.make_async_copy(mem_hbm, M, ld_sem.at[4]),
        pltpu.make_async_copy(lam_hbm, lam, ld_sem.at[5]),
        pltpu.make_async_copy(mu_hbm, mu, ld_sem.at[6]),
        pltpu.make_async_copy(rel_hbm, rel, ld_sem.at[7]),
        pltpu.make_async_copy(ane_hbm, ane, ld_sem.at[8]),
        pltpu.make_async_copy(cell_hbm, cells, ld_sem.at[9]),
    ]
    order = (
        pltpu.make_async_copy(active_hbm, active, ld_sem.at[10]),
        pltpu.make_async_copy(offset_hbm, offset, ld_sem.at[11]),
    )
    for copy in (loads[1], *order, loads[0], loads[2], loads[3]):
        copy.start()

    pl.semaphore_wait(barrier, count)

    def x_copies(h):
        kind = "sv"[h % 2]
        ref = S if kind == "s" else V
        up, dn = [], []
        for n, (c0, nc, lu, ld) in enumerate(X_GROUPS[kind]):
            comps = pl.ds(c0, nc)
            rows = pl.ds(YP, CY)
            if h == 0:
                src_up = str_hbm.at[comps, pl.ds(CX - lu, lu)]
                src_dn = str_hbm.at[comps, pl.ds(0, ld)]
            else:
                src_up = ref.at[comps, pl.ds(XP + CX - lu, lu), rows]
                src_dn = ref.at[comps, pl.ds(XP, ld), rows]
            up.append(pltpu.make_async_remote_copy(
                src_up, ref.at[comps, pl.ds(XP - lu, lu), rows],
                xs_sem.at[h, n], xr_sem.at[h, n], device_id=s_up, device_id_type=MESH))
            dn.append(pltpu.make_async_remote_copy(
                src_dn, ref.at[comps, pl.ds(XP + CX, ld), rows],
                xs_sem.at[h, 2 + n], xr_sem.at[h, 2 + n], device_id=s_dn, device_id_type=MESH))
        return up, dn

    def each(there, copies, act):
        @pl.when(there)
        def _():
            for copy in copies:
                act(copy)

    def x_start(h, side):
        there = has["s_up"] if side == 0 else has["s_dn"]
        each(there, x_copies(h)[side], lambda c: c.start())

    def x_wait_recv(h, side):
        there = has["s_dn"] if side == 0 else has["s_up"]
        each(there, x_copies(h)[side], lambda c: c.wait_recv())

    def x_wait_send(h):
        up, dn = x_copies(h)
        each(has["s_up"], up, lambda c: c.wait_send())
        each(has["s_dn"], dn, lambda c: c.wait_send())

    x_start(0, 0)

    Sf = S.reshape(6, (CX + 2 * XP) * ROW, 128)
    Vf = V.reshape(3, (CX + 2 * XP) * ROW, 128)
    flat = {"s": Sf, "v": Vf}

    for F, nc in ((S, 6), (V, 3)):
        zero_x = jnp.zeros((nc, XP, CY, 128), jnp.float32)

        @pl.when(s == 0)
        def _(F=F, zero_x=zero_x):
            F[:, 0:XP, YP:YP + CY, :] = zero_x

        @pl.when(s == NS - 1)
        def _(F=F, zero_x=zero_x):
            F[:, XP + CX:, YP:YP + CY, :] = zero_x

    for there, refs in (
        (has["k_dn"], yrecv_up), (has["k_up"], yrecv_dn), (has["d_dn"], zrecv_up), (has["d_up"], zrecv_dn),
    ):
        @pl.when(jnp.logical_not(there))
        def _(refs=refs):
            for ref in refs:
                ref[...] = jnp.zeros(ref.shape, jnp.float32)

    for refs in (ysend_up, ysend_dn):
        for ref in refs:
            ref[:, ref.shape[1] - 8:, :] = jnp.zeros((4, 8, 128), jnp.float32)

    def y_layers(kind):
        up, dn = [], []
        for c, back in Y_FIELDS[kind]:
            up += [(c, CY - 2), (c, CY - 1)] if back else [(c, CY - 1)]
            dn += [(c, 0)] if back else [(c, 0), (c, 1)]
        return up, dn

    PLANES = (tuple(range(2, CX - 2)), (0, 1, CX - 2, CX - 1))
    SPANS = (((2, CX - 4),), ((0, 2), (CX - 2, 2)))

    def y_copies(h, part):
        size = len(PLANES[part])
        nu, nd = (-(-len(layers) * size // 8) * 8 for layers in y_layers("sv"[h % 2]))
        return (
            pltpu.make_async_remote_copy(
                ysend_up[part].at[h, pl.ds(0, nu)], yrecv_up[part].at[h, pl.ds(0, nu)],
                ys_sem.at[h, part, 0], yr_sem.at[h, part, 0], device_id=k_up, device_id_type=MESH),
            pltpu.make_async_remote_copy(
                ysend_dn[part].at[h, pl.ds(0, nd)], yrecv_dn[part].at[h, pl.ds(0, nd)],
                ys_sem.at[h, part, 1], yr_sem.at[h, part, 1], device_id=k_dn, device_id_type=MESH),
        )

    def z_copies(h, part):
        return (
            pltpu.make_async_remote_copy(
                zsend[part].at[h], zrecv_up[part].at[h],
                zs_sem.at[h, part, 0], zr_sem.at[h, part, 0], device_id=d_up, device_id_type=MESH),
            pltpu.make_async_remote_copy(
                zsend[part].at[h], zrecv_dn[part].at[h],
                zs_sem.at[h, part, 1], zr_sem.at[h, part, 1], device_id=d_dn, device_id_type=MESH),
        )

    lane = lax.broadcasted_iota(jnp.int32, (CY, 128), 1)
    slot = lane >> 2
    quarter = lane & 3

    def turn(value, n):
        return pltpu.roll(value, n % 128, 1)

    def z_slot(part, place, n):
        if part == 0:
            return place // 2, n + 16 * (place % 2)
        return 0, n + 4 * place

    def yz_send(h, part):
        kind = "sv"[h % 2]
        F = flat[kind]
        base = XP * ROW + YP
        for layers, refs in zip(y_layers(kind), (ysend_up, ysend_dn)):
            at = 0
            for c, row in layers:
                for x0, n in SPANS[part]:
                    refs[part][h, at:at + n, :] = F[c, pl.ds(base + x0 * ROW + row, n, stride=ROW), :]
                    at += n
        up, dn = y_copies(h, part)
        each(has["k_up"], [up], lambda c: c.start())
        each(has["k_dn"], [dn], lambda c: c.start())
        arrays = [jnp.zeros((CY, 128), jnp.float32)] * (2 - part)
        for place, comp in enumerate(Z_FIELDS[kind]):
            for n, x in enumerate(PLANES[part]):
                where, index = z_slot(part, place, n)
                value = F[comp, pl.ds((x + XP) * ROW + YP, CY), :]
                arrays[where] = jnp.where(slot == index, turn(value, 4 * index + 2), arrays[where])
        half = CY // 2
        last = arrays[-1]
        folded = jnp.where(lane[:half] < 64, last[:half], turn(last[half:], 64))
        if part == 0:
            zsend[0][h, 0:CY, :] = arrays[0]
            zsend[0][h, CY:CY + half, :] = folded
        else:
            zsend[1][h] = folded
        up, dn = z_copies(h, part)
        each(has["d_up"], [up], lambda c: c.start())
        each(has["d_dn"], [dn], lambda c: c.start())

    def z_got(refs, h, part, where):
        if part == 0 and where == 0:
            return refs[0][h, 0:CY, :]
        at = CY if part == 0 else 0
        value = refs[part][h, at:at + CY // 2, :]
        return jnp.concatenate([value, turn(value, -64)], axis=0)

    def yz_recv(h, part):
        kind = "sv"[h % 2]
        F = flat[kind]
        up, dn = y_copies(h, part)
        each(has["k_dn"], [up], lambda c: c.wait_recv())
        each(has["k_up"], [dn], lambda c: c.wait_recv())
        base = XP * ROW + YP
        for layers, refs, shift in zip(y_layers(kind), (yrecv_up, yrecv_dn), (-CY, CY)):
            at = 0
            for c, row in layers:
                for x0, n in SPANS[part]:
                    F[c, pl.ds(base + x0 * ROW + row + shift, n, stride=ROW), :] = refs[part][h, at:at + n, :]
                    at += n
        up, dn = z_copies(h, part)
        each(has["d_dn"], [up], lambda c: c.wait_recv())
        each(has["d_up"], [dn], lambda c: c.wait_recv())
        fixes = {}
        for place, back in enumerate(Z_BACK[kind]):
            ends = (lane == 127) | (lane < 2) if back else (lane > 125) | (lane == 0)
            for n, x in enumerate(PLANES[part]):
                where, index = z_slot(part, place, n)
                if (where, back) not in fixes:
                    mix = jnp.where(quarter < 2, z_got(zrecv_up, h, part, where), z_got(zrecv_dn, h, part, where))
                    below, two_after = turn(mix, 1), turn(mix, -2)
                    if back:
                        fix = jnp.where(quarter == 0, -two_after, jnp.where(quarter == 1, below - 27.0 * mix, below))
                    else:
                        fix = jnp.where(quarter == 1, 27.0 * turn(mix, -1) - two_after, jnp.where(quarter == 0, -two_after, below))
                    fixes[where, back] = jnp.where(quarter == 3, 0.0, fix)
                moved = turn(fixes[where, back], (127 if back else 126) - 4 * index)
                deep[place, x] = deep[place, x] + jnp.where(ends, moved, 0.0)

    def deep_part(h, part):
        kind = "sv"[h % 2]
        F = S if kind == "s" else V
        for place, (comp, back) in enumerate(zip(Z_FIELDS[kind], Z_BACK[kind])):
            f = jnp.concatenate(
                [F[comp, XP + x0:XP + x0 + n, YP:YP + CY, :].reshape(n * CY, 128) for x0, n in SPANS[part]], axis=0)
            high = f.astype(jnp.bfloat16)
            low = (f - high.astype(jnp.float32)).astype(jnp.bfloat16)
            out = lax.dot_general(
                jnp.concatenate([high, low], axis=1), band[1 if back else 0],
                (((1,), (0,)), ((), ())), preferred_element_type=jnp.float32)
            at = 0
            for x0, n in SPANS[part]:
                deep[place, x0:x0 + n] = out[at:at + n * CY].reshape(n, CY, 128)
                at += n * CY

    def velocity_pair(x, tiles):
        for j in tiles:
            at = (x + XP) * ROW + YP + j

            def get(c, n, Sf=Sf, at=at):
                return Sf[c, pl.ds(at + n, 8), :]

            xx = [get(0, n * ROW) for n in range(-1, 4)]
            xy = [get(3, n * ROW) for n in range(-2, 3)]
            xz = [get(4, n * ROW) for n in range(-2, 3)]
            for p in range(2):
                o = p * ROW
                gain = R24 * buo[x + p, pl.ds(j, 8), :]
                xy_at, yy, yz = xy[2 + p], [get(1, o + n) for n in range(-1, 3)], [get(5, o + n) for n in range(-2, 2)]
                close = (
                    (xx[2 + p] - xx[1 + p]) + (xy_at - get(3, o - 1)),
                    (xy_at - xy[1 + p]) + (yy[2] - yy[1]),
                    (xz[2 + p] - xz[1 + p]) + (yz[2] - yz[1]),
                )
                far = (
                    (xx[3 + p] - xx[p]) + (get(3, o + 1) - get(3, o - 2)),
                    (xy[3 + p] - xy[p]) + (yy[3] - yy[0]),
                    (xz[3 + p] - xz[p]) + (yz[3] - yz[0]),
                )
                for c in range(3):
                    own = pl.ds(pl.multiple_of(at + o, 8), 8)
                    Vf[c, own, :] = Vf[c, own, :] + gain * (
                        27.0 * close[c] - far[c] + deep[c, x + p, pl.ds(j, 8), :])

    def stress_pair(x, tiles):
        def material(x, rows):
            return lam[x, rows, :], mu[x, rows, :], rel[x, rows, :], ane[x, rows, :]

        def put(c, x, at, rows, stress, memory):
            Sf[c, pl.ds(pl.multiple_of(at, 8), 8), :] = stress
            M[c, x, rows, :] = memory

        stress_tiles(x, x, (CY, ROW), tiles, Sf, Vf, M, deep, material, put)

    def interior(one):
        @pl.loop(0, (CX - 4) // 2)
        def _(i):
            one(2 * i + 2, range(0, CY, 8))

    nought = jnp.minimum(s, 0)

    def edges(h, one, source=None):
        sides = ((0, 0), (1, CX - 2))
        for side, x in sides if h % 2 == 0 else sides[::-1]:
            x_wait_recv(h, side)
            one(nought + x, range(0, CY, 8))
            if source is not None:
                apply_source(source, ((x, 2),))
            x_start(h + 1, 1 - side)

    def candidates():
        row = lax.broadcasted_iota(jnp.int32, (TB, 128), 0)
        weights = jnp.where((row == 0) | (row == TB - 1), 0.5 / (TB - 1), 1.0 / (TB - 1))
        for t in range(STEPS):
            o = offset[t]
            for c in range(6):
                samples = rate[c, pl.ds(o, TB), :]
                cand[group, t, c:c + 1, :] = jnp.sum(samples * weights, axis=0, keepdims=True)
            cand[group, t, 6:8, :] = jnp.zeros((2, 128), jnp.float32)

    def c_copy(sender, receiver):
        return pltpu.make_async_remote_copy(
            cand.at[sender], cand.at[sender], c_send.at[receiver], c_recv.at[sender],
            device_id={"strike": receiver * NA + parity}, device_id_type=MESH)

    def over_groups(act):
        @pl.loop(0, NB)
        def _(g):
            @pl.when(g != group)
            def _():
                act(g)

    def pair_copy(which):
        return pltpu.make_async_remote_copy(
            pair.at[which], pair.at[which], p_send, p_recv, device_id=other, device_id_type=MESH)

    def g_copy(which, h):
        return pltpu.make_async_remote_copy(
            chosen, gathered.at[which], g_send.at[h], g_recv.at[which],
            device_id={"dip": fault, "depth": h}, device_id_type=MESH)

    def over_fault(act):
        @pl.loop(0, NH)
        def _(h):
            @pl.when(jnp.logical_not(on_fault & (h == d)))
            def _():
                act(h)

    def source_first():
        loads[1].wait()
        for copy in order:
            copy.wait()
        candidates()
        over_groups(lambda g: c_copy(group, g).start())

    def source_second():
        over_groups(lambda g: c_copy(g, group).wait_recv())
        for t in range(STEPS):
            pair[parity, t] = cand[lax.div(active[t], NA), t]
        pair_copy(parity).start()

    def source_third():
        pair_copy(lax.rem(parity + 1, NA)).wait_recv()
        for t in range(STEPS):
            value = pair[lax.rem(active[t], NA), t]
            chosen[t] = value

            @pl.when(on_fault)
            def _(t=t, value=value):
                gathered[chunk, t] = value

        over_fault(lambda h: g_copy(chunk, h).start())

    def source_gather():
        @pl.when(on_fault)
        def _():
            @pl.loop(0, ND * NH)
            def _(j):
                @pl.when(j != chunk)
                def _():
                    g_copy(j, 0).wait_recv()

    def source_plane(t, piece):
        @pl.when(on_fault)
        def _():
            seg = active[t]
            depth_total = 128 * NH
            wide = SUBF // 2
            cell = cells[pl.ds(seg, 1), piece * wide:(piece + 1) * wide]
            cell_x = lax.div(cell, depth_total)
            cell_z = cell - cell_x * depth_total - d * 128
            cell_x = cell_x - s * CX
            hot_z = (lax.broadcasted_iota(jnp.int32, (128, wide), 0) == cell_z).astype(jnp.float32).astype(jnp.bfloat16)
            hot_x = lax.broadcasted_iota(jnp.int32, (CX, wide), 0) == cell_x
            first = piece * wide // 128
            value = jnp.concatenate([gathered[first + n, t] for n in range(wide // 128)], axis=1)
            high = value.astype(jnp.bfloat16).astype(jnp.float32)
            rows = [
                jnp.where(hot_x, part[c:c + 1, :], 0.0).astype(jnp.bfloat16)
                for part in (high, value - high) for c in range(6)
            ]
            out = lax.dot_general(
                jnp.concatenate(rows, axis=0), hot_z, (((1,), (1,)), ((), ())),
                preferred_element_type=jnp.float32)
            n = 6 * CX
            out = out[0:n] + out[n:2 * n]
            ref = plane if t == 0 else last_plane
            if piece == 0:
                ref[...] = out
            else:
                ref[...] = ref[...] + out

    def apply_source(ref, spans):
        @pl.when(on_fault)
        def _():
            for c in range(6):
                for x0, n in spans:
                    at = pl.ds((x0 + XP) * ROW + YP, n, stride=ROW)
                    Sf[c, at, :] = Sf[c, at, :] - ref[c * CX + x0:c * CX + x0 + n, :]

    middle = ((2, CX - 4),)

    i, j = (lax.broadcasted_iota(jnp.int32, (256, 128), n) for n in range(2))
    off = (i & 127) - j
    for n, (a, b) in enumerate(((1, 0), (0, -1))):
        weight = jnp.where(off == a, 27.0, jnp.where(off == b, -27.0, jnp.where(
            off == a + 1, -1.0, jnp.where(off == b - 1, 1.0, 0.0))))
        band[n] = weight.astype(jnp.bfloat16)

    @pl.when(jnp.logical_not(on_fault))
    def _():
        last_plane[...] = jnp.zeros_like(last_plane)

    source_first()
    loads[0].wait()
    for copy in loads[4:]:
        copy.start()
    yz_send(0, 0)
    yz_send(0, 1)
    x_start(0, 1)
    deep_part(0, 0)
    deep_part(0, 1)
    loads[2].wait()
    loads[3].wait()
    yz_recv(0, 0)
    source_second()
    interior(velocity_pair)
    yz_send(1, 0)
    source_third()
    deep_part(1, 0)
    yz_recv(0, 1)
    edges(0, velocity_pair)
    yz_send(1, 1)
    for copy in loads[4:]:
        copy.wait()
    yz_recv(1, 0)
    interior(stress_pair)
    source_gather()
    source_plane(0, 0)
    source_plane(0, 1)
    apply_source(plane, middle)
    yz_send(2, 0)
    deep_part(1, 1)
    deep_part(2, 0)
    x_wait_send(0)
    yz_recv(1, 1)
    edges(1, stress_pair, plane)
    yz_send(2, 1)
    yz_recv(2, 0)
    interior(velocity_pair)
    yz_send(3, 0)
    deep_part(2, 1)
    deep_part(3, 0)
    source_plane(1, 0)
    x_wait_send(1)
    yz_recv(2, 1)
    edges(2, velocity_pair)
    yz_send(3, 1)
    yz_recv(3, 0)
    interior(stress_pair)
    source_plane(1, 1)
    apply_source(last_plane, middle)
    deep_part(3, 1)
    yz_recv(3, 1)
    x_wait_send(2)
    for h in range(4):
        for part in range(2):
            for there, pair_of in (("k", y_copies(h, part)), ("d", z_copies(h, part))):
                each(has[there + "_up"], [pair_of[0]], lambda c: c.wait_send())
                each(has[there + "_dn"], [pair_of[1]], lambda c: c.wait_send())
    over_groups(lambda g: c_copy(group, g).wait_send())
    pair_copy(parity).wait_send()
    over_fault(lambda h: g_copy(chunk, h).wait_send())
    x_wait_recv(3, 0)
    x_wait_recv(3, 1)
    x_wait_send(3)


def solution(mesh):
    ns, nd, nh = (mesh.shape[a] for a in ("strike", "dip", "depth"))

    def body(velocity, stress, memory, lam, mu, buo, rel, ane, rate, cell, active, offset):
        cx, cy, cz = lam.shape
        subf = cell.shape[1]
        assert cz == 128 and subf == 128 * nd * nh
        planes, rows = cx + 2 * XP, cy + 2 * YP
        f32 = jnp.float32
        block = pltpu.VMEM((cx, cy, cz), f32)
        dma = pltpu.SemaphoreType.DMA
        hbm = pl.BlockSpec(memory_space=pltpu.HBM)
        vmem = pl.BlockSpec(memory_space=pltpu.VMEM)
        between = (
            pltpu.VMEM((6, planes, rows, cz), f32),
            pltpu.VMEM((3, planes, rows, cz), f32),
            pltpu.VMEM((6, cx, cy, cz), f32),
            pltpu.VMEM((3, cx, cy, cz), f32),
            block, block, block, block,
            pltpu.VMEM((6 * cx, cz), f32),
        )
        held = pl.pallas_call(
            functools.partial(kernel, (ns, nd, nh, cx, cy, subf)),
            out_shape=between,
            in_specs=[hbm] * 12,
            out_specs=(vmem,) * 9,
            scratch_shapes=[
                block,
                pltpu.VMEM((6, rate.shape[1], 128), f32),
                pltpu.VMEM(cell.shape, jnp.int32),
                pltpu.SMEM(active.shape, jnp.int32),
                pltpu.SMEM(offset.shape, jnp.int32),
                *[(pltpu.VMEM((4, 64, cz), f32), pltpu.VMEM((4, 24, cz), f32))] * 4,
                *[(pltpu.VMEM((4, cy + cy // 2, cz), f32), pltpu.VMEM((4, cy // 2, cz), f32))] * 3,
                pltpu.VMEM((2, 2 * cz, cz), jnp.bfloat16),
                pltpu.VMEM((ns // NA, STEPS, 8, 128), f32),
                pltpu.VMEM((NA, STEPS, 8, 128), f32),
                pltpu.VMEM((STEPS, 8, 128), f32),
                pltpu.VMEM((nd * nh, STEPS, 8, 128), f32),
                pltpu.VMEM((6 * cx, cz), f32),
                dma((12,)), dma((4, 4)), dma((4, 4)), dma((4, 2, 2)), dma((4, 2, 2)), dma((4, 2, 2)), dma((4, 2, 2)),
                dma((ns // NA,)), dma((ns // NA,)), dma, dma, dma((nh,)), dma((nd * nh,)),
            ],
            compiler_params=pltpu.CompilerParams(
                collective_id=0, has_side_effects=True, vmem_limit_bytes=40 * 1024 * 1024
            ),
            cost_estimate=pl.CostEstimate(flops=30_000_000, bytes_accessed=6_000_000, transcendentals=0),
        )(*(
            pltpu.with_memory_space_constraint(a, pltpu.HBM)
            for a in (velocity, stress, memory, lam, mu, buo, rel, ane, jnp.transpose(rate, (0, 2, 1, 3)), cell, active, offset)
        ))
        return pl.pallas_call(
            functools.partial(finish, (cx, cy)),
            out_shape=tuple(jax.ShapeDtypeStruct(a.shape, f32) for a in (velocity, stress, memory)),
            in_specs=[vmem] * 9,
            out_specs=(hbm,) * 3,
            scratch_shapes=[
                pltpu.VMEM((6, 4, cy, cz), f32),
                pltpu.VMEM((6, 4, cy, cz), f32),
                dma((7,)),
            ],
            compiler_params=pltpu.CompilerParams(vmem_limit_bytes=40 * 1024 * 1024),
            cost_estimate=pl.CostEstimate(flops=2_000_000, bytes_accessed=4_000_000, transcendentals=0),
        )(*held)

    field = P(None, "strike", "dip", "depth")
    cellwise = P("strike", "dip", "depth")
    return jax.shard_map(
        body,
        mesh=mesh,
        in_specs=(field,) * 3 + (cellwise,) * 5 + (P("strike", None, None, None), P(), P(), P()),
        out_specs=(field,) * 3,
        check_vma=False,
    )
```
